32 devices in a mesh: seq: 16 (over z, x, core), batch: 2 (over y).
Axes of the slice: x: 2, y: 2, z: 4, core: 2. Of those that a mesh axis runs over, the one named last changes fastest.
Arguments:
- inputs: bfloat16 [2, 2048, 1024], P('batch', 'seq'), may hold values from -6 to 6
- lengths: int32 [2, 8], P('batch'), may hold values from 64 to 1599, as said below
- proj_query: bfloat16 [1024, 1024], replicated, may hold values from -0.1875 to 0.1875
- proj_latent: bfloat16 [1024, 512], replicated, may hold values from -0.1875 to 0.1875
- proj_expand: bfloat16 [256, 256], replicated, may hold values from -0.375 to 0.375
- proj_output: bfloat16 [1024, 1024], replicated, may hold values from -1.5 to 1.5
- ffn_gate: bfloat16 [1024, 2816], replicated, may hold values from -0.1875 to 0.1875
- ffn_up: bfloat16 [1024, 2816], replicated, may hold values from -0.1875 to 0.1875
- ffn_down: bfloat16 [2816, 1024], replicated, may hold values from -0.109375 to 0.109375
- norm_attn: bfloat16 [1024], replicated, may hold values from 0.099609375 to 1.8984375
- norm_ffn: bfloat16 [1024], replicated, may hold values from 0.099609375 to 1.8984375
- cotangent: bfloat16 [2, 2048, 1024], P('batch', 'seq'), may hold values from -6 to 6
Outputs:
- output: bfloat16 [2, 2048, 1024], P('batch', 'seq')
- input_grad: bfloat16 [2, 2048, 1024], P('batch', 'seq')
- grad_query: float32 [1024, 1024], P('seq')
- grad_latent: float32 [1024, 512], P('seq')
- grad_expand: float32 [256, 256], P(None, 'seq')
- grad_output: float32 [1024, 1024], P('seq')
- grad_gate: float32 [1024, 2816], P('seq')
- grad_up: float32 [1024, 2816], P('seq')
- grad_down: float32 [2816, 1024], P(None, 'seq')
- grad_norm_attn: float32 [1024], P('seq')
- grad_norm_ffn: float32 [1024], P('seq')
The draws below stay inside these ranges and needn't reach their ends.
Inputs may be any that keep to these rules, and one draw needn't show every extreme that they name: `lengths`: in each bucket the first document is the longest; the other 7 documents have 128 // 2 to 73 positions; 1 to 16 positions at the end of a bucket are padding.
All inputs are finite; a program needn't handle non-finite values.
Results may differ from the reference program's by a relative error of at most 0.015.
Values may be sent and summed in bfloat16 or wider, within the bound.
No kernel may reach another device: no remote copies, remote signals or barrier semaphores. Data moves between devices by JAX's collectives and lax.ppermute only.
A program may use at most 192 MiB of HBM per device.

```python
import jax
import jax.numpy as jnp
from jax import lax

D = 1024
HEADS = 16
HD = 64
GROUPS = 2
LAT = 256
FF = 2816
TOK_DEV = 128
DOCS = 8
SEQ_LEN = 2048
SHORT_MOST = 73
BUCKETS = 2


def draw_lengths(key, part):
    key = jax.random.fold_in(key, 17)
    pad_key, short_key, pick_key = jax.random.split(key, 3)
    padding = jax.random.randint(pad_key, (BUCKETS, 1), 1, TOK_DEV // 8 + 1)
    short = jax.random.randint(short_key, (BUCKETS, DOCS - 1), TOK_DEV // 2, SHORT_MOST + 1)
    chosen = jax.random.randint(pick_key, (), 0, BUCKETS)
    rows = jnp.arange(BUCKETS, dtype=jnp.int32)[:, None]
    padding = jnp.where(rows == chosen, 1, padding)
    short = jnp.where(rows == chosen, TOK_DEV // 2, short)
    longest = SEQ_LEN - padding - jnp.sum(short, axis=1, keepdims=True)
    return jnp.concatenate([longest, short], axis=1).astype(jnp.int32)


def shard_levels(key, dims, cuts, low, top_value):
    def one(position, shards_of):
        steps = jax.random.uniform(jax.random.fold_in(jax.random.fold_in(key, 6), position), (shards_of,), jnp.float32, low / len(cuts), top_value / len(cuts))
        return jnp.repeat(jnp.exp(steps), dims[position] // shards_of).reshape((-1,) + (1,) * (len(dims) - position - 1))

    level = one(*cuts[0])
    for cut in cuts[1:]:
        level = level * one(*cut)
    return level


def bell_draw(key, extent, spread, bound, pieces=(), held_as=jnp.bfloat16):
    drawn = spread * jax.random.normal(key, extent, jnp.float32)
    if pieces:
        drawn = drawn * shard_levels(key, extent, pieces, -0.22, 0.18)
    return jnp.clip(drawn, -bound, bound).astype(held_as)


def setup_inputs(seed: int = 0) -> dict:
    arg_keys = jax.random.split(jax.random.key(seed), 13)
    return {
        "inputs": bell_draw(arg_keys[0], (BUCKETS, SEQ_LEN, D), 1.0, 6.0, ((0, 2), (1, 16))),
        "lengths": draw_lengths(jax.random.fold_in(arg_keys[12], 71), 0),
        "proj_query": bell_draw(arg_keys[2], (D, HEADS * HD), D ** -0.5, 0.1875),
        "proj_latent": bell_draw(arg_keys[3], (D, GROUPS * LAT), D ** -0.5, 0.1875),
        "proj_expand": bell_draw(arg_keys[4], (LAT, GROUPS * 2 * HD), LAT ** -0.5, 0.375),
        "proj_output": bell_draw(arg_keys[5], (HEADS * HD, D), 16 ** -0.5, 1.5),
        "ffn_gate": bell_draw(arg_keys[6], (D, FF), D ** -0.5, 0.1875),
        "ffn_up": bell_draw(arg_keys[7], (D, FF), D ** -0.5, 0.1875),
        "ffn_down": bell_draw(arg_keys[8], (FF, D), FF ** -0.5, 0.109375),
        "norm_attn": jnp.clip(1.0 + 0.18 * jax.random.normal(arg_keys[9], (D,), jnp.float32), 0.099609375, 1.8984375).astype(jnp.bfloat16),
        "norm_ffn": jnp.clip(1.0 + 0.18 * jax.random.normal(arg_keys[10], (D,), jnp.float32), 0.099609375, 1.8984375).astype(jnp.bfloat16),
        "cotangent": bell_draw(arg_keys[11], (BUCKETS, SEQ_LEN, D), 1.0, 6.0, ((0, 2), (1, 16))),
    }


@jax.custom_vjp
def low(v):
    return lax.optimization_barrier(v.astype(jnp.bfloat16)).astype(jnp.float32)

@jax.custom_vjp
def low_back(v):
    return v

def low_keep(v):
    return (low(v), None)

def low_pass(kept, grad):
    return (grad,)

def back_keep(v):
    return (v, None)

def back_low(kept, grad):
    return (low(grad),)
low.defvjp(low_keep, low_pass)
low_back.defvjp(back_keep, back_low)
eps = 1e-05
highest = lax.Precision.HIGHEST

def rms_gain(hidden, gain):
    return hidden * lax.rsqrt(lax.optimization_barrier(jnp.mean(hidden * hidden, axis=-1, keepdims=True)) + eps) * gain

def matmul(left, right):
    return jnp.dot(left, right, precision=highest)

def doc_numbers(lengths_row, count):
    ends = jnp.cumsum(lengths_row)
    places = jnp.arange(count, dtype=jnp.int32)
    return lax.optimization_barrier(jnp.sum((places[:, None] >= ends[None, :]).astype(jnp.int32), axis=1))

def layer(hidden, proj_query, proj_latent, proj_expand, proj_output, ffn_gate, ffn_up, ffn_down, norm_attn, norm_ffn, docs):
    seq_len = hidden.shape[0]
    per_group = HEADS // GROUPS
    normed = low(rms_gain(hidden, norm_attn))
    query = low_back(low(matmul(normed, proj_query)))
    latent = low_back(low(matmul(normed, proj_latent)))
    key_list = []
    value_list = []
    for group in range(GROUPS):
        both = matmul(latent[:, group * LAT:(group + 1) * LAT], proj_expand[:, group * 2 * HD:(group + 1) * 2 * HD])
        key_list.append(both[:, :HD])
        value_list.append(both[:, HD:])
    keys = low_back(low(jnp.stack(key_list)))
    values = low_back(low(jnp.stack(value_list)))
    places = jnp.arange(seq_len, dtype=jnp.int32)
    block = min(512, seq_len)
    count = seq_len // block

    def attend(item):
        query_block, query_docs, query_places = item
        heads = query_block.reshape(block, GROUPS, per_group, HD)
        raw = jnp.einsum('bghd,gkd->ghbk', heads, keys, precision=highest)
        raw = low_back(raw * 0.125)
        allowed = (query_docs[:, None] == docs[None, :]) & (places[None, :] <= query_places[:, None]) & (query_docs[:, None] < DOCS) | (places[None, :] == query_places[:, None])
        held = jnp.where(allowed[None, None], raw, -1e+30)
        top = lax.optimization_barrier(jnp.max(held, axis=-1, keepdims=True))
        expo = jnp.exp(held - top)
        probs = low(expo / lax.optimization_barrier(jnp.sum(expo, axis=-1, keepdims=True)))
        mixed = jnp.einsum('ghbk,gkd->bghd', probs, values, precision=highest)
        return mixed.reshape(block, HEADS * HD)
    attended = lax.map(jax.checkpoint(attend), (query.reshape(count, block, HEADS * HD), docs.reshape(count, block), places.reshape(count, block)))
    attended = low_back(low(attended.reshape(seq_len, HEADS * HD)))
    middle = hidden + low_back(matmul(attended, proj_output))
    normed_two = low(rms_gain(middle, norm_ffn))
    gate = low_back(matmul(normed_two, ffn_gate))
    upper = low_back(matmul(normed_two, ffn_up))
    activ = low(jax.nn.silu(gate) * upper)
    return middle + low_back(matmul(activ, ffn_down))

def reference(inputs, lengths, proj_query, proj_latent, proj_expand, proj_output, ffn_gate, ffn_up, ffn_down, norm_attn, norm_ffn, cotangent):
    params = tuple((w.astype(jnp.float32) for w in (proj_query, proj_latent, proj_expand, proj_output, ffn_gate, ffn_up, ffn_down, norm_attn, norm_ffn)))
    outputs = []
    input_grads = []
    totals = tuple((jnp.zeros(w.shape, jnp.float32) for w in params))
    for bucket in range(BUCKETS):
        docs = doc_numbers(lengths[bucket], SEQ_LEN)

        def forward(hidden, wq, wl, we, wo, wg, wu, wd, ga, gf):
            return layer(hidden, wq, wl, we, wo, wg, wu, wd, ga, gf, docs)
        result, pull = jax.vjp(forward, inputs[bucket].astype(jnp.float32), *params)
        grads = pull(cotangent[bucket].astype(jnp.float32))
        outputs.append(result.astype(jnp.bfloat16))
        input_grads.append(grads[0].astype(jnp.bfloat16))
        totals = tuple((t + g for t, g in zip(totals, grads[1:])))
    return (jnp.stack(outputs), jnp.stack(input_grads), totals[0], totals[1], totals[2], totals[3], totals[4], totals[5], totals[6], totals[7], totals[8])
```

```python
import functools

import jax
import jax.numpy as jnp
from jax import lax
from jax.experimental import pallas as pl
from jax.experimental.pallas import tpu as pltpu
from jax.sharding import Mesh
from jax.sharding import PartitionSpec as P

HEADS = 16
HD = 64
GROUPS = 2
PER = HEADS // GROUPS
LAT = 256
DOCS = 8
LANE = 128
CHUNK = 256

F32 = jnp.float32
BF16 = jnp.bfloat16
eps = 1e-05
scale = 0.125
masked = -1e30

SEQ = ("z", "x", "core")
PLANE = ("x", "core", "batch")
WIDE = 3 * LANE

VM = pl.BlockSpec(memory_space=pltpu.VMEM)
SM = pl.BlockSpec(memory_space=pltpu.SMEM)
ANY = pl.BlockSpec(memory_space=pl.ANY)
LIMIT = 60 * 1024 * 1024


def nn(left, right):
    return jnp.dot(left, right, preferred_element_type=F32)


def tn(left, right):
    return lax.dot_general(left, right, (((0,), (0,)), ((), ())), preferred_element_type=F32)


def nt(left, right):
    return lax.dot_general(left, right, (((1,), (1,)), ((), ())), preferred_element_type=F32)


def shape(dims, dtype):
    return jax.ShapeDtypeStruct(dims, dtype)


def norm_forward(hidden, gain):
    inverse = lax.rsqrt(jnp.mean(hidden * hidden, axis=-1, keepdims=True) + eps)
    return (hidden * inverse * gain, inverse)


def norm_backward(hidden, gain, inverse, grad):
    scaled = grad * gain
    gain_grad = jnp.sum(grad * hidden * inverse, axis=0, keepdims=True)
    cubed = inverse * inverse * inverse
    hidden_grad = inverse * scaled - hidden * cubed * jnp.mean(
        scaled * hidden, axis=-1, keepdims=True
    )
    return (hidden_grad, gain_grad)


def doc_bounds(sc, tok):
    first = sc[0]
    query = first + lax.broadcasted_iota(jnp.int32, (1, tok), 1)
    begin = jnp.zeros((1, tok), jnp.int32)
    low = jnp.int32(0)
    end = jnp.int32(0)
    for d in range(DOCS):
        end = end + sc[8 + d]
        begin = jnp.where(query >= end, end, begin)
        low = jnp.where(first >= end, end, low)
    begin = jnp.where(query >= end, query, begin)
    low = jnp.where(first >= end, first, low)
    return query, begin, low // CHUNK, (first + tok - 1) // CHUNK + 1


def chunk_bias(chunk, query, begin):
    key = chunk * CHUNK + lax.broadcasted_iota(jnp.int32, (CHUNK, LANE), 0)
    bias = jnp.where((key >= begin) & (key <= query), 0.0, masked)
    return jnp.concatenate([bias] * PER, axis=1)


def attend_kernel(
    nz, relative, sc, k00, k01, k10, k11, qp, hidden, wo, gain,
    kvs, ot, logs, left, mid, normed, top, total, acc,
):
    tok = hidden.shape[0]
    z, x, core = sc[1], sc[2], sc[3]
    for rc, rx, ref in ((0, 0, k00), (0, 1, k01), (1, 0, k10), (1, 1, k11)):
        for k in range(nz):
            where_z = z - k if relative else k
            slot = (where_z * 2 + (rx ^ x)) * 2 + (rc ^ core)

            @pl.when(where_z >= 0)
            def _():
                kvs[pl.ds(pl.multiple_of(slot * tok, tok), tok), :] = ref[k]

    query, begin, low, high = doc_bounds(sc, tok)
    top[...] = jnp.full(top.shape, masked, F32)
    total[...] = jnp.zeros(total.shape, F32)
    acc[...] = jnp.zeros(acc.shape, F32)

    @pl.loop(low, high)
    def _(chunk):
        kv = kvs[pl.ds(pl.multiple_of(chunk * CHUNK, CHUNK), CHUNK), :]
        bias = chunk_bias(chunk, query, begin)
        for g in range(GROUPS):
            part = kv[:, g * LANE : (g + 1) * LANE]
            raw = nn(part, qp[g]) + bias
            old = top[g]
            new = jnp.maximum(old, jnp.max(raw, axis=0, keepdims=True))
            prob = jnp.exp(raw - new)
            fade = jnp.exp(old - new)
            top[g] = new
            total[g] = total[g] * fade + jnp.sum(prob, axis=0, keepdims=True)
            acc[g] = acc[g] * fade + tn(part, prob.astype(BF16))

    for g in range(GROUPS):
        mixed = acc[g, HD : 2 * HD, :] * (1.0 / total[g])
        ot[g] = mixed
        logs[g] = top[g] + jnp.log(total[g])
        for h in range(PER):
            row = (g * PER + h) * HD
            left[0, row : row + HD, :] = mixed[:, h * LANE : (h + 1) * LANE].astype(BF16)
    middle = hidden[...].astype(F32) + tn(left[0], wo[...])
    mid[...] = middle
    value, unused = norm_forward(middle, gain[...])
    normed[...] = value.astype(BF16)
    left[1] = value.T.astype(BF16)


def attend(sc, kv_parts, qp, hidden, wo, gain, nz, relative):
    tok, width = hidden.shape
    seq_len = nz * 4 * tok
    return pl.pallas_call(
        functools.partial(attend_kernel, nz, relative),
        out_shape=(
            shape((seq_len, 2 * LANE), BF16),
            shape((GROUPS, HD, PER * tok), F32),
            shape((GROUPS, 1, PER * tok), F32),
            shape((2, width, tok), BF16),
            shape((tok, width), F32),
            shape((tok, width), BF16),
        ),
        in_specs=[SM] + [VM] * 8,
        out_specs=(VM,) * 6,
        scratch_shapes=[
            pltpu.VMEM((GROUPS, 1, PER * tok), F32),
            pltpu.VMEM((GROUPS, 1, PER * tok), F32),
            pltpu.VMEM((GROUPS, 2 * HD, PER * tok), F32),
        ],
        compiler_params=pltpu.CompilerParams(vmem_limit_bytes=LIMIT),
        name="attend",
    )(sc, *kv_parts, qp, hidden, wo, gain)


def start_tile(place):
    return (place * 11) // 4


def feed_kernel(
    steps, sc, normed, grad_out, mid, gain, wo, wg, wu, wd, *rest
):
    sends = rest[:8]
    output, dmid, dop, gain_grad = rest[8:12]
    acc, back, dgate_s, dup_s, act_s = rest[12:]
    step = pl.program_id(0)

    @pl.when(step == 0)
    def _():
        acc[...] = jnp.zeros(acc.shape, F32)
        back[...] = jnp.zeros(back.shape, F32)

    n2 = normed[...]
    dy = grad_out[...]
    gate = nn(n2, wg[...])
    upper = nn(n2, wu[...])
    d_act = nt(dy, wd[...])
    sigma = jax.nn.sigmoid(gate)
    swish = gate * sigma
    act = (swish * upper).astype(BF16)
    dgate = (d_act * upper * sigma * (1.0 + gate * (1.0 - sigma))).astype(BF16)
    dup = (d_act * swish).astype(BF16)
    acc[...] += nn(act, wd[...])
    back[...] += nt(dgate, wg[...]) + nt(dup, wu[...])
    tile = wg.shape[1]
    cols = pl.ds(pl.multiple_of(step * tile, tile), tile)
    dgate_s[:, cols] = dgate
    dup_s[:, cols] = dup
    act_s[:, cols] = act

    @pl.when(step == steps - 1)
    def _():
        middle = mid[...]
        output[...] = (middle + acc[...]).astype(BF16)
        inverse = lax.rsqrt(jnp.mean(middle * middle, axis=-1, keepdims=True) + eps)
        grad, gains = norm_backward(middle, gain[...], inverse, back[...])
        grad = grad + dy.astype(F32)
        dmid[...] = grad
        gain_grad[...] = gains
        low = grad.astype(BF16)
        back[...] = low.astype(F32)
        for k in range(8):
            place = sc[4] ^ k
            cols = pl.ds(pl.multiple_of(start_tile(place) * LANE, LANE), WIDE)
            sends[k][:, 0:WIDE] = dgate_s[:, cols]
            sends[k][:, WIDE : 2 * WIDE] = dup_s[:, cols]
            sends[k][:, 2 * WIDE : 3 * WIDE] = act_s[:, cols]
            cols = pl.ds(pl.multiple_of(place * LANE, LANE), LANE)
            sends[k][:, 3 * WIDE :] = back[:, cols].astype(BF16)
        turned = nt(wo[...], low).astype(BF16)
        dop[:, 0:HD, :] = jnp.zeros((GROUPS, HD, dop.shape[2]), BF16)
        for g in range(GROUPS):
            for h in range(PER):
                row = (g * PER + h) * HD
                dop[g, HD:, h * LANE : (h + 1) * LANE] = turned[row : row + HD, :]


def feed(sc, normed, grad_out, mid, gain, wo, wg, wu, wd):
    tok, width = normed.shape
    hidden = wg.shape[1]
    tile = 2 * LANE
    steps = hidden // tile
    fixed = lambda *dims: pl.BlockSpec(dims, lambda i: (0,) * len(dims))
    send = shape((tok, 3 * WIDE + LANE), BF16)
    return pl.pallas_call(
        functools.partial(feed_kernel, steps),
        grid=(steps,),
        out_shape=(send,) * 8
        + (
            shape((tok, width), BF16),
            shape((tok, width), F32),
            shape((GROUPS, 2 * HD, PER * tok), BF16),
            shape((1, width), F32),
        ),
        in_specs=[
            SM,
            fixed(tok, width),
            fixed(tok, width),
            fixed(tok, width),
            fixed(1, width),
            fixed(width, width),
            pl.BlockSpec((width, tile), lambda i: (0, i)),
            pl.BlockSpec((width, tile), lambda i: (0, i)),
            pl.BlockSpec((tile, width), lambda i: (i, 0)),
        ],
        out_specs=(fixed(*send.shape),) * 8
        + (
            fixed(tok, width),
            fixed(tok, width),
            fixed(GROUPS, 2 * HD, PER * tok),
            fixed(1, width),
        ),
        scratch_shapes=[
            pltpu.VMEM((tok, width), F32),
            pltpu.VMEM((tok, width), F32),
            pltpu.VMEM((tok, hidden), BF16),
            pltpu.VMEM((tok, hidden), BF16),
            pltpu.VMEM((tok, hidden), BF16),
        ],
        compiler_params=pltpu.CompilerParams(vmem_limit_bytes=LIMIT),
        name="feed",
    )(sc, normed, grad_out, mid, gain, wo, wg, wu, wd)


def back_kernel(nz, sc, kvs, qp, dop, ot, logs, *rest):
    sends = rest[:8]
    dq, keep, send = rest[8:11]
    acc, rows, block = rest[11:]
    tok = dq.shape[0]
    x, core = sc[2], sc[3]

    @pl.loop(0, nz)
    def _(i):
        keep[:, i] = jnp.zeros((2,) + keep.shape[2:], BF16)
        send[:, i] = jnp.zeros((2,) + send.shape[2:], BF16)

    query, begin, low, high = doc_bounds(sc, tok)
    acc[...] = jnp.zeros(acc.shape, F32)
    for g in range(GROUPS):
        rows[g] = jnp.sum(dop[g, HD:, :].astype(F32) * ot[g], axis=0, keepdims=True)

    @pl.loop(low, high)
    def _(chunk):
        kv = kvs[pl.ds(pl.multiple_of(chunk * CHUNK, CHUNK), CHUNK), :]
        bias = chunk_bias(chunk, query, begin)
        for g in range(GROUPS):
            part = kv[:, g * LANE : (g + 1) * LANE]
            prob = jnp.exp(nn(part, qp[g]) + bias - logs[g])
            slope = (prob * (nn(part, dop[g]) - rows[g])).astype(BF16)
            block[:, g * LANE : (g + 1) * LANE] = nt(slope, qp[g]) + nt(prob.astype(BF16), dop[g])
            acc[g] += tn(part, slope)
        where_z = chunk // 2
        rel = (chunk % 2) ^ x
        keep[rel, where_z] = block[pl.ds(pl.multiple_of(core * tok, tok), tok), :].astype(BF16)
        send[rel, where_z] = block[pl.ds(pl.multiple_of((1 - core) * tok, tok), tok), :].astype(BF16)

    for g in range(GROUPS):
        for h in range(0, PER, 2):
            pair = [acc[g, 0:HD, (h + i) * LANE : (h + i + 1) * LANE] for i in range(2)]
            col = (g * PER + h) * HD
            dq[:, col : col + LANE] = (jnp.concatenate(pair, axis=0).T * scale).astype(BF16)
    for k in range(8):
        place = sc[4] ^ k
        sends[k][...] = dq[:, pl.ds(pl.multiple_of(place * LANE, LANE), LANE)]


def attend_back(sc, kvs, qp, dop, ot, logs, nz, tok):
    width = HEADS * HD
    part = shape((2, nz, tok, 2 * LANE), BF16)
    return pl.pallas_call(
        functools.partial(back_kernel, nz),
        out_shape=(shape((tok, LANE), BF16),) * 8 + (shape((tok, width), BF16), part, part),
        in_specs=[SM] + [VM] * 5,
        out_specs=(VM,) * 11,
        scratch_shapes=[
            pltpu.VMEM((GROUPS, 2 * HD, PER * tok), F32),
            pltpu.VMEM((GROUPS, 1, PER * tok), F32),
            pltpu.VMEM((CHUNK, 2 * LANE), F32),
        ],
        compiler_params=pltpu.CompilerParams(vmem_limit_bytes=LIMIT),
        name="attend_back",
    )(sc, kvs, qp, dop, ot, logs)


def weight_kernel(plan, nz, sc, *refs):
    count = max(index for index, unused, unused in plan) + 1
    lefts = refs[:count]
    rights = refs[count : count + 8]
    keep, send = refs[count + 8 : count + 10]
    wide, tall, sems = refs[count + 10 :]
    tok = rights[0].shape[0]
    copies = []
    for k in range(8):
        place = sc[4] ^ k
        copies.append(
            pltpu.make_async_copy(rights[k], tall.at[pl.ds(k * tok, tok), :], sems.at[count, k])
        )
        for i in range(count):
            copies.append(
                pltpu.make_async_copy(
                    lefts[i].at[place], wide.at[i, :, pl.ds(k * tok, tok)], sems.at[i, k]
                )
            )
    for copy in copies:
        copy.start()
    for copy in copies:
        copy.wait()
    bit = sc[1] % 2
    size = keep.shape[1]

    @pl.loop(0, nz // 2)
    def _(i):
        for ref, half in ((keep, bit), (send, 1 - bit)):
            rows = pl.ds(pl.multiple_of((2 * i + half) * size, size), size)
            for index, begin, stop in plan:
                ref[i, :, begin:stop] = nn(wide[index, rows, :], tall[:, begin:stop]).astype(BF16)


def weight_terms(sc, lefts, rights, plan, nz):
    tok, width = rights[0].shape
    rows = lefts[0].shape[1]
    half = shape((nz // 2, rows // nz, width), BF16)
    return pl.pallas_call(
        functools.partial(weight_kernel, plan, nz),
        out_shape=(half, half),
        in_specs=[SM] + [ANY] * (len(lefts) + 8),
        out_specs=(VM, VM),
        scratch_shapes=[
            pltpu.VMEM((len(lefts), rows, 8 * tok), BF16),
            pltpu.VMEM((8 * tok, width), BF16),
            pltpu.SemaphoreType.DMA((len(lefts) + 1, 8)),
        ],
        compiler_params=pltpu.CompilerParams(vmem_limit_bytes=LIMIT),
        name="weight_terms",
    )(sc, *lefts, *rights)


def swap(value, axis):
    return lax.ppermute(value, axis, [(0, 1), (1, 0)])


def plane_swap(parts):
    moved = [parts[0]]
    for k in range(1, 8):
        moved.append(lax.ppermute(parts[k], PLANE, [(d, d ^ k) for d in range(8)]))
    return moved


def z_halve(value, z, nz, step):
    bit = (z >> step) & 1
    pairs = value.reshape((value.shape[0] // 2, 2) + value.shape[1:])
    keep = lax.dynamic_index_in_dim(pairs, bit, 1, keepdims=False)
    send = lax.dynamic_index_in_dim(pairs, 1 - bit, 1, keepdims=False)
    return keep, send


def z_finish(keep, send, z, nz):
    flip = lambda step: [(i, i ^ (1 << step)) for i in range(nz)]
    total = keep.astype(F32) + lax.ppermute(send, "z", flip(0)).astype(F32)
    step = 1
    while (1 << step) < nz:
        keep, send = z_halve(total, z, nz, step)
        total = keep + lax.ppermute(send.astype(BF16), "z", flip(step)).astype(F32)
        step += 1
    return total[0]


def rows_out(block, place):
    parts = block.astype(BF16).reshape(4, block.shape[0] // 4, block.shape[1])
    rows = [lax.dynamic_index_in_dim(parts, (place ^ k) >> 1, 0, keepdims=False) for k in range(8)]
    return plane_swap(rows)


def place_kernel(rows, hidden, sc, *refs):
    parts = refs[:8]
    gate, up, down, outp = refs[8:]
    for k in range(8):
        place = sc[4] ^ k
        start = start_tile(place)
        part = parts[k][...].astype(F32)
        twice = (place > 0) & (start < start_tile(place - 1) + 3)
        for index, ref in ((0, gate), (1, up), (2, down)):
            for i in range(3):

                @pl.when(jnp.logical_not(twice) if i == 0 else start >= 0)
                def _():
                    cols = pl.ds(pl.multiple_of((start + i) * LANE, LANE), LANE)
                    col = index * WIDE + i * LANE
                    ref[:, cols] = part[:, col : col + LANE]

        outp[:, pl.ds(pl.multiple_of(place * LANE, LANE), LANE)] = part[:, 3 * WIDE :]


def place_wide(sc, parts, hidden, width):
    rows = parts[0].shape[0]
    wide = shape((rows, hidden), F32)
    return pl.pallas_call(
        functools.partial(place_kernel, rows, hidden),
        out_shape=(wide, wide, wide, shape((rows, width), F32)),
        in_specs=[SM] + [VM] * 8,
        out_specs=(VM,) * 4,
        compiler_params=pltpu.CompilerParams(vmem_limit_bytes=LIMIT),
        name="place_wide",
    )(sc, *parts)


def in_place(parts, place):
    stacked = jnp.stack(parts)
    order = place ^ jnp.arange(8, dtype=jnp.int32)
    stacked = jnp.take(stacked, order, axis=0)
    return stacked.transpose(1, 0, 2).reshape(parts[0].shape[0], -1).astype(F32)


def shards(
    inputs, lengths, proj_query, proj_latent, proj_expand, proj_output,
    ffn_gate, ffn_up, ffn_down, norm_attn, norm_ffn, cotangent,
):
    tok, width = inputs.shape[1:]
    nz = lax.axis_size("z")
    z, x, core, batch = [lax.axis_index(a) for a in ("z", "x", "core", "batch")]
    place = (x * 2 + core) * 2 + batch
    hidden_size = ffn_gate.shape[1]
    first = ((z * 2 + x) * 2 + core) * tok
    sc = jnp.stack([first, z, x, core, place, place, place, place]).astype(jnp.int32)
    sc = jnp.concatenate([sc, lengths[0]])

    hidden_low = inputs[0]
    hidden = hidden_low.astype(F32)
    dy = cotangent[0]
    gain_attn = norm_attn.astype(F32)[None]
    gain_ffn = norm_ffn.astype(F32)[None]

    normed, inverse = norm_forward(hidden, gain_attn)
    normed_low = normed.astype(BF16)
    latent = nn(normed_low, proj_latent).astype(BF16)
    kv = jnp.concatenate(
        [
            nn(latent[:, g * LAT : (g + 1) * LAT], proj_expand[:, g * LANE : (g + 1) * LANE])
            for g in range(GROUPS)
        ],
        axis=1,
    ).astype(BF16)

    relative = nz <= 4
    if relative:
        moved = [kv]
        for k in range(1, nz):
            moved.append(lax.ppermute(kv, "z", [(i, i + k) for i in range(nz - k)]))
        k00 = jnp.stack(moved)
    else:
        k00 = lax.all_gather(kv, "z", axis=0)
    k01 = swap(k00, "x")
    k10 = swap(k00, "core")
    k11 = swap(k01, "core")

    queries = nn(normed_low, proj_query).astype(BF16) * scale
    turned = queries.T.reshape(GROUPS, PER, HD, tok).transpose(0, 2, 1, 3)
    qp = jnp.pad(turned.reshape(GROUPS, HD, PER * tok), ((0, 0), (0, HD), (0, 0)))
    early = lax.all_gather(jnp.stack([dy.T, normed_low.T]), PLANE, axis=1)

    kvs, ot, logs, left, mid, normed_two = attend(
        sc, (k00, k01, k10, k11), qp, hidden_low, proj_output, gain_ffn, nz, relative
    )
    later = lax.all_gather(left, PLANE, axis=1)
    fed = feed(
        sc, normed_two, dy, mid, gain_ffn, proj_output, ffn_gate, ffn_up, ffn_down
    )
    output, dmid, dop, gain_two = fed[8:]
    wide_parts = plane_swap(fed[:8])

    backed = attend_back(sc, kvs, qp, dop, ot, logs, nz, tok)
    dq, keep, send = backed[8:]
    came = swap(send, "core")
    side = (keep[1].astype(F32) + came[1].astype(F32)).astype(BF16)
    side = swap(side, "x").astype(F32)
    term = keep[0].astype(F32) + came[0].astype(F32) + side
    if relative:
        kv_grad = lax.dynamic_index_in_dim(term, z, 0, keepdims=False)
        term_low = term.astype(BF16)
        for k in range(1, nz):
            block = lax.dynamic_index_in_dim(term_low, jnp.maximum(z - k, 0), 0, keepdims=False)
            block = lax.ppermute(block, "z", [(i, i - k) for i in range(k, nz)])
            kv_grad = kv_grad + block.astype(F32)
    else:
        kv_grad = lax.psum_scatter(term, "z", scatter_dimension=0, tiled=False)
    kv_grad = kv_grad.astype(BF16)
    query_parts = plane_swap(backed[:8])

    d_latent = jnp.concatenate(
        [
            nt(kv_grad[:, g * LANE : (g + 1) * LANE], proj_expand[:, g * LANE : (g + 1) * LANE])
            for g in range(GROUPS)
        ],
        axis=1,
    ).astype(BF16)
    lat_cols = d_latent.shape[1] // 8
    lat_split = d_latent.reshape(tok, 8, lat_cols).transpose(1, 0, 2)
    lat_parts = plane_swap(
        [lax.dynamic_index_in_dim(lat_split, place ^ k, 0, keepdims=False) for k in range(8)]
    )
    d_normed = nt(dq, proj_query) + nt(d_latent, proj_latent)
    d_hidden, gain_one = norm_backward(hidden, gain_attn, inverse, d_normed)
    input_grad = (d_hidden + dmid).astype(BF16)

    seq = nz * 4
    expand_t = jnp.concatenate(
        [
            lax.dot_general(
                kv_grad[:, g * LANE : (g + 1) * LANE],
                latent[:, g * LAT : (g + 1) * LAT],
                (((0,), (0,)), ((), ())),
                preferred_element_type=F32,
            )
            for g in range(GROUPS)
        ],
        axis=0,
    )
    small = jnp.concatenate(
        [
            expand_t.reshape(seq, -1),
            gain_one.reshape(seq, -1),
            gain_two.reshape(seq, -1),
        ],
        axis=1,
    )
    small = small.reshape(nz, 2, 2, -1)
    for axis, where, dim in (("core", core, 2), ("x", x, 1)):
        mine = lax.dynamic_index_in_dim(small, where, dim, keepdims=False)
        other = lax.dynamic_index_in_dim(small, 1 - where, dim, keepdims=False)
        small = mine + swap(other.astype(BF16), axis).astype(F32)
    step = 0
    while (1 << step) < nz:
        mine, other = z_halve(small, z, nz, step)
        flips = [(i, i ^ (1 << step)) for i in range(nz)]
        small = mine + lax.ppermute(other.astype(BF16), "z", flips).astype(F32)
        step += 1
    small_low = small[0].astype(BF16)
    small = small_low.astype(F32) + swap(small_low, "batch").astype(F32)
    cut = expand_t.size // seq
    gains = (small.shape[0] - cut) // 2
    grad_expand = small[:cut].reshape(-1, expand_t.shape[1]).T
    grad_norm_attn = small[cut : cut + gains]
    grad_norm_ffn = small[cut + gains :]

    dys, n1s = early[0], early[1]
    os, n2s = later[0], later[1]
    plan = ((0, 0, 2 * WIDE), (1, 2 * WIDE, 3 * WIDE), (2, 3 * WIDE, 3 * WIDE + LANE))
    keep, send = weight_terms(sc, (n2s, dys, os), wide_parts, plan, nz)
    wide = z_finish(keep, send, z, nz)
    grad_gate, grad_up, grad_down_t, grad_output = place_wide(
        sc, rows_out(wide, place), hidden_size, width
    )
    keep, send = weight_terms(sc, (n1s,), query_parts, ((0, 0, LANE),), nz)
    grad_query = in_place(rows_out(z_finish(keep, send, z, nz), place), place)
    keep, send = weight_terms(sc, (n1s,), lat_parts, ((0, 0, lat_cols),), nz)
    grad_latent = in_place(rows_out(z_finish(keep, send, z, nz), place), place)
    return (
        output[None],
        input_grad[None],
        grad_query,
        grad_latent,
        grad_expand,
        grad_output,
        grad_gate,
        grad_up,
        grad_down_t.T,
        grad_norm_attn,
        grad_norm_ffn,
    )


def solution(mesh):
    seq, batch = mesh.shape["seq"], mesh.shape["batch"]
    fine = Mesh(mesh.devices.reshape(seq // 4, 2, 2, batch), SEQ + ("batch",))
    return jax.shard_map(
        shards,
        mesh=fine,
        in_specs=(P("batch", SEQ, None), P("batch", None))
        + (P(),) * 9
        + (P("batch", SEQ, None),),
        out_specs=(
            P("batch", SEQ, None),
            P("batch", SEQ, None),
            P(SEQ, None),
            P(SEQ, None),
            P(None, SEQ),
            P(SEQ, None),
            P(SEQ, None),
            P(SEQ, None),
            P(None, SEQ),
            P(SEQ),
            P(SEQ),
        ),
        check_vma=False,
    )
```

```python
import functools

import jax
import jax.numpy as jnp
from jax import lax
from jax.experimental import pallas as pl
from jax.experimental.pallas import tpu as pltpu
from jax.sharding import Mesh
from jax.sharding import PartitionSpec as P

HEADS = 16
HD = 64
GROUPS = 2
PER = HEADS // GROUPS
LAT = 256
DOCS = 8
LANE = 128
CHUNK = 256

F32 = jnp.float32
BF16 = jnp.bfloat16
eps = 1e-05
scale = 0.125
masked = -1e30

SEQ = ("z", "x", "core")
PLANE = ("x", "batch")
FOUR = 4
TILES = 6
WIDE = TILES * LANE

VM = pl.BlockSpec(memory_space=pltpu.VMEM)
SM = pl.BlockSpec(memory_space=pltpu.SMEM)
ANY = pl.BlockSpec(memory_space=pl.ANY)
MIB = 1024 * 1024


def nn(left, right):
    return jnp.dot(left, right, preferred_element_type=F32)


def tn(left, right):
    return lax.dot_general(left, right, (((0,), (0,)), ((), ())), preferred_element_type=F32)


def nt(left, right):
    return lax.dot_general(left, right, (((1,), (1,)), ((), ())), preferred_element_type=F32)


def shape(dims, dtype):
    return jax.ShapeDtypeStruct(dims, dtype)


def cost(micros):
    return pl.CostEstimate(flops=0, bytes_accessed=int(micros * 3.6e6), transcendentals=0)


def call(kernel, name, ins, specs, outs, scratch=(), after=(), room=8, micros=0.01):
    count, extra = len(ins), len(after)

    def body(*refs):
        kernel(*refs[:count], *refs[count + extra :])

    return pl.pallas_call(
        body,
        out_shape=tuple(outs),
        in_specs=list(specs) + [ANY] * extra,
        out_specs=(VM,) * len(outs),
        scratch_shapes=list(scratch),
        compiler_params=pltpu.CompilerParams(vmem_limit_bytes=room * MIB),
        cost_estimate=cost(micros),
        name=name,
    )(*ins, *after)


def gain_row(gain):
    return gain[...].astype(F32)[None]


def norm_forward(hidden, gain):
    inverse = lax.rsqrt(jnp.mean(hidden * hidden, axis=-1, keepdims=True) + eps)
    return (hidden * inverse * gain, inverse)


def norm_backward(hidden, gain, inverse, grad):
    scaled = grad * gain
    gain_grad = jnp.sum(grad * hidden * inverse, axis=0, keepdims=True)
    cubed = inverse * inverse * inverse
    hidden_grad = inverse * scaled - hidden * cubed * jnp.mean(
        scaled * hidden, axis=-1, keepdims=True
    )
    return (hidden_grad, gain_grad)


def by_core(value, nz):
    size = value.shape[0] // (nz * 4)
    rows = [value[i * size : (i + 1) * size] for i in range(nz * 4)]
    return jnp.concatenate(rows[0::2] + rows[1::2], axis=0)


def doc_bounds(sc, tok):
    first = sc[0]
    query = first + lax.broadcasted_iota(jnp.int32, (1, tok), 1)
    begin = jnp.zeros((1, tok), jnp.int32)
    low = jnp.int32(0)
    end = jnp.int32(0)
    for d in range(DOCS):
        end = end + sc[8 + d]
        begin = jnp.where(query >= end, end, begin)
        low = jnp.where(first >= end, end, low)
    begin = jnp.where(query >= end, query, begin)
    low = jnp.where(first >= end, first, low)
    return query, begin, low // CHUNK, (first + tok - 1) // CHUNK + 1


def chunk_bias(chunk, query, begin):
    key = chunk * CHUNK + lax.broadcasted_iota(jnp.int32, (CHUNK, LANE), 0)
    bias = jnp.where((key >= begin) & (key <= query), 0.0, masked)
    return jnp.concatenate([bias] * PER, axis=1)


def attend_kernel(
    nz, relative, sc, k00, k01, k10, k11, qp, hidden, wo, gain,
    kvs, ot, logs, left_o, left_n, mid, normed, top, total, acc, mixed_all, wo_s, sem,
):
    load = pltpu.make_async_copy(wo, wo_s, sem)
    load.start()
    tok = hidden.shape[0]
    z, x, core = sc[1], sc[2], sc[3]
    for rc, rx, ref in ((0, 0, k00), (0, 1, k01), (1, 0, k10), (1, 1, k11)):
        for k in range(nz):
            where_z = z - k if relative else k
            slot = (where_z * 2 + (rx ^ x)) * 2 + (rc ^ core)

            @pl.when(where_z >= 0)
            def _():
                kvs[pl.ds(pl.multiple_of(slot * tok, tok), tok), :] = ref[k]

    query, begin, low, high = doc_bounds(sc, tok)
    top[...] = jnp.full(top.shape, masked, F32)
    total[...] = jnp.zeros(total.shape, F32)
    acc[...] = jnp.zeros(acc.shape, F32)

    @pl.loop(low, high)
    def _(chunk):
        kv = kvs[pl.ds(pl.multiple_of(chunk * CHUNK, CHUNK), CHUNK), :]
        bias = chunk_bias(chunk, query, begin)
        for g in range(GROUPS):
            part = kv[:, g * LANE : (g + 1) * LANE]
            raw = nn(part, qp[g]) + bias
            old = top[g]
            new = jnp.maximum(old, jnp.max(raw, axis=0, keepdims=True))
            prob = jnp.exp(raw - new)
            fade = jnp.exp(old - new)
            top[g] = new
            total[g] = total[g] * fade + jnp.sum(prob, axis=0, keepdims=True)
            acc[g] = acc[g] * fade + tn(part, prob.astype(BF16))

    for g in range(GROUPS):
        mixed = acc[g, HD : 2 * HD, :] * (1.0 / total[g])
        ot[g] = mixed
        logs[g] = top[g] + jnp.log(total[g])
        for h in range(PER):
            row = (g * PER + h) * HD
            mixed_all[row : row + HD, :] = mixed[:, h * LANE : (h + 1) * LANE]
    every = mixed_all[...]
    left_o[...] = by_core(every, nz).astype(BF16)
    load.wait()
    middle = hidden[...].astype(F32) + tn(every.astype(BF16), wo_s[...])
    mid[...] = middle
    value, unused = norm_forward(middle, gain_row(gain))
    normed[...] = value.astype(BF16)
    left_n[...] = by_core(value.T, nz).astype(BF16)


def attend(sc, kv_parts, qp, hidden, wo, gain, nz, relative, after=()):
    tok, width = hidden.shape
    left = shape((width, tok), BF16)
    return call(
        functools.partial(attend_kernel, nz, relative),
        "attend",
        (sc, *kv_parts, qp, hidden, wo, gain),
        [SM] + [VM] * 6 + [ANY, VM],
        (
            shape((nz * 4 * tok, 2 * LANE), BF16),
            shape((GROUPS, HD, PER * tok), F32),
            shape((GROUPS, 1, PER * tok), F32),
            left,
            left,
            shape((tok, width), F32),
            shape((tok, width), BF16),
        ),
        [
            pltpu.VMEM((GROUPS, 1, PER * tok), F32),
            pltpu.VMEM((GROUPS, 1, PER * tok), F32),
            pltpu.VMEM((GROUPS, 2 * HD, PER * tok), F32),
            pltpu.VMEM((HEADS * HD, tok), F32),
            pltpu.VMEM(wo.shape, BF16),
            pltpu.SemaphoreType.DMA,
        ],
        after,
        60,
    )


def start_tile(place):
    return (place * 11) // 2


def feed_kernel(tile, sc, normed, grad_out, mid, gain, wo, wg, wu, wd, *rest):
    sends = rest[:FOUR]
    output, dmid, dop, gain_grad = rest[FOUR : FOUR + 4]
    vg, vu, vd, vo, dgate_s, dup_s, act_s, sems = rest[FOUR + 4 :]
    steps = wd.shape[0] // tile
    copies = []
    for t in range(steps):
        span = pl.ds(t * tile, tile)
        copies.append(
            (
                pltpu.make_async_copy(wg.at[:, span], vg.at[:, span], sems.at[0, t]),
                pltpu.make_async_copy(wu.at[:, span], vu.at[:, span], sems.at[1, t]),
                pltpu.make_async_copy(wd.at[span, :], vd.at[span, :], sems.at[2, t]),
            )
        )
    copies.append((pltpu.make_async_copy(wo, vo, sems.at[3, 0]),))
    for group in copies:
        for copy in group:
            copy.start()
    n2 = normed[...]
    dy = grad_out[...]
    for t in range(steps):
        span = slice(t * tile, (t + 1) * tile)
        for copy in copies[t]:
            copy.wait()
        gate = nn(n2, vg[:, span])
        upper = nn(n2, vu[:, span])
        d_act = nt(dy, vd[span, :])
        sigma = jax.nn.sigmoid(gate)
        swish = gate * sigma
        act_s[:, span] = (swish * upper).astype(BF16)
        dgate_s[:, span] = (d_act * upper * sigma * (1.0 + gate * (1.0 - sigma))).astype(BF16)
        dup_s[:, span] = (d_act * swish).astype(BF16)
    copies[steps][0].wait()
    middle = mid[...]
    output[...] = (middle + nn(act_s[...], vd[...])).astype(BF16)
    back = nt(dgate_s[...], vg[...]) + nt(dup_s[...], vu[...])
    inverse = lax.rsqrt(jnp.mean(middle * middle, axis=-1, keepdims=True) + eps)
    grad, gains = norm_backward(middle, gain_row(gain), inverse, back)
    grad = grad + dy.astype(F32)
    dmid[...] = grad
    gain_grad[...] = gains
    for k in range(FOUR):
        cols = pl.ds(pl.multiple_of(start_tile(sc[4] ^ k) * LANE, LANE), WIDE)
        for i, ref in enumerate((dgate_s, dup_s, act_s)):
            sends[k][:, i * WIDE : (i + 1) * WIDE] = ref[:, cols]
    turned = nt(vo[...], grad.astype(BF16)).astype(BF16)
    dop[:, 0:HD, :] = jnp.zeros((GROUPS, HD, dop.shape[2]), BF16)
    for g in range(GROUPS):
        for h in range(PER):
            row = (g * PER + h) * HD
            dop[g, HD:, h * LANE : (h + 1) * LANE] = turned[row : row + HD, :]


def feed(sc, normed, grad_out, mid, gain, wo, wg, wu, wd, after=()):
    tok, width = normed.shape
    hidden = wg.shape[1]
    tile = 2 * LANE
    return call(
        functools.partial(feed_kernel, tile),
        "feed",
        (sc, normed, grad_out, mid, gain, wo, wg, wu, wd),
        [SM] + [VM] * 4 + [ANY] * 4,
        (shape((tok, 3 * WIDE), BF16),) * FOUR
        + (
            shape((tok, width), BF16),
            shape((tok, width), F32),
            shape((GROUPS, 2 * HD, PER * tok), BF16),
            shape((1, width), F32),
        ),
        [
            pltpu.VMEM((width, hidden), BF16),
            pltpu.VMEM((width, hidden), BF16),
            pltpu.VMEM((hidden, width), BF16),
            pltpu.VMEM((width, width), BF16),
            pltpu.VMEM((tok, hidden), BF16),
            pltpu.VMEM((tok, hidden), BF16),
            pltpu.VMEM((tok, hidden), BF16),
            pltpu.SemaphoreType.DMA((4, hidden // tile)),
        ],
        after,
        60,
    )


def back_kernel(
    nz, sc, kvs, qp, dop, ot, logs, dq, keep_own, keep_far, send_own, send_far, acc, rows, block
):
    tok = dq.shape[0]
    x, core = sc[2], sc[3]

    @pl.loop(0, nz)
    def _(i):
        for ref in (keep_own, keep_far, send_own, send_far):
            ref[i] = jnp.zeros(ref.shape[1:], BF16)

    query, begin, low, high = doc_bounds(sc, tok)
    acc[...] = jnp.zeros(acc.shape, F32)
    for g in range(GROUPS):
        rows[g] = jnp.sum(dop[g, HD:, :].astype(F32) * ot[g], axis=0, keepdims=True)

    @pl.loop(low, high)
    def _(chunk):
        kv = kvs[pl.ds(pl.multiple_of(chunk * CHUNK, CHUNK), CHUNK), :]
        bias = chunk_bias(chunk, query, begin)
        for g in range(GROUPS):
            part = kv[:, g * LANE : (g + 1) * LANE]
            prob = jnp.exp(nn(part, qp[g]) + bias - logs[g])
            slope = (prob * (nn(part, dop[g]) - rows[g])).astype(BF16)
            block[:, g * LANE : (g + 1) * LANE] = nt(slope, qp[g]) + nt(prob.astype(BF16), dop[g])
            acc[g] += tn(part, slope)
        where_z = chunk // 2
        near = (chunk % 2) == x
        mine = block[pl.ds(pl.multiple_of(core * tok, tok), tok), :].astype(BF16)
        other = block[pl.ds(pl.multiple_of((1 - core) * tok, tok), tok), :].astype(BF16)

        @pl.when(near)
        def _():
            keep_own[where_z] = mine
            send_own[where_z] = other

        @pl.when(jnp.logical_not(near))
        def _():
            keep_far[where_z] = mine
            send_far[where_z] = other

    for g in range(GROUPS):
        for h in range(0, PER, 2):
            pair = [acc[g, 0:HD, (h + i) * LANE : (h + i + 1) * LANE] for i in range(2)]
            col = (g * PER + h) * HD
            dq[:, col : col + LANE] = (jnp.concatenate(pair, axis=0).T * scale).astype(BF16)


def attend_back(sc, kvs, qp, dop, ot, logs, nz, tok, after=()):
    part = shape((nz, tok, 2 * LANE), BF16)
    return call(
        functools.partial(back_kernel, nz),
        "attend_back",
        (sc, kvs, qp, dop, ot, logs),
        [SM] + [VM] * 5,
        (shape((tok, HEADS * HD), BF16), part, part, part, part),
        [
            pltpu.VMEM((GROUPS, 2 * HD, PER * tok), F32),
            pltpu.VMEM((GROUPS, 1, PER * tok), F32),
            pltpu.VMEM((CHUNK, 2 * LANE), F32),
        ],
        after,
        60,
        9,
    )


def stack_kernel(*refs):
    for k, ref in enumerate(refs[:-1]):
        refs[-1][k] = ref[...]


def stack(arrays, after=()):
    dims = (len(arrays),) + arrays[0].shape
    return call(
        stack_kernel, "stack", arrays, [VM] * len(arrays), (shape(dims, BF16),), after=after
    )[0]


def kv_add_kernel(keep_own, keep_far, came_own, came_far, rest, side):
    rest[...] = keep_own[...].astype(F32) + came_own[...].astype(F32)
    side[...] = (keep_far[...].astype(F32) + came_far[...].astype(F32)).astype(BF16)


def kv_add(terms, after=()):
    dims = terms[0].shape
    return call(
        kv_add_kernel, "kv_add", terms, [VM] * 4, (shape(dims, F32), shape(dims, BF16)),
        after=after, room=60,
    )


def kv_split_kernel(sc, rest, came, own, *sends):
    z = sc[1]
    own[...] = rest[z] + came[z].astype(F32)
    for k, ref in enumerate(sends):
        at = jnp.maximum(z - k - 1, 0)
        ref[...] = (rest[at] + came[at].astype(F32)).astype(BF16)


def kv_split(sc, rest, came, after=()):
    nz, tok, width = rest.shape
    block = (tok, width)
    return call(
        kv_split_kernel,
        "kv_split",
        (sc, rest, came),
        [SM, VM, VM],
        (shape(block, F32),) + (shape(block, BF16),) * (nz - 1),
        after=after,
    )


def weight_kernel(counts, groups, extra, sc, *refs):
    lefts = []
    for count, unused in counts:
        lefts.append(refs[:count])
        refs = refs[count:]
    rights, refs = refs[:FOUR], refs[FOUR:]
    added, refs = refs[:extra], refs[extra:]
    outs, (wide, tall, sems) = refs[: 2 * len(groups)], refs[2 * len(groups) :]
    tok = rights[0].shape[0]
    copies = []
    for k in range(FOUR):
        span = pl.ds(k * tok, tok)
        copies.append(
            pltpu.make_async_copy(rights[k], tall.at[span, :], sems.at[len(counts), k])
        )
        for i, (count, kind) in enumerate(counts):
            if count == FOUR:
                source = lefts[i][k]
            elif kind is None:
                source = lefts[i][0].at[sc[4] ^ k]
            else:
                source = lefts[i][0].at[sc[4] ^ k, kind]
            copies.append(pltpu.make_async_copy(source, wide.at[i, :, span], sems.at[i, k]))
    for copy in copies:
        copy.start()
    for copy in copies:
        copy.wait()
    core = sc[3]
    half = wide.shape[1] // 2
    for i, group in enumerate(groups):
        first = group[0][1]
        for ref, where in ((outs[2 * i + 1], 1 - core), (outs[2 * i], core)):
            rows = pl.ds(pl.multiple_of(where * half, half), half)
            for index, begin, stop in group:
                for at in range(begin, stop, CHUNK):
                    upto = min(at + CHUNK, stop)
                    block = nn(wide[index, rows, :], tall[:, at:upto])
                    ref[:, at - first : upto - first] = block.astype(BF16)
            for other in added:
                ref[:, group[-1][2] - first :] = other[rows, :]


def weight_terms(sc, lefts, rights, groups, extra=(), after=()):
    tok, width = rights[0].shape
    rows = lefts[0][1][0].shape[-2]
    more = sum(array.shape[1] for array in extra)
    counts = tuple((len(arrays), kind) for kind, arrays in lefts)
    flat = [array for unused, arrays in lefts for array in arrays] + rights
    outs = ()
    for group in groups:
        outs += (shape((rows // 2, group[-1][2] - group[0][1] + more), BF16),) * 2
    return call(
        functools.partial(weight_kernel, counts, groups, len(extra)),
        "weight_terms",
        (sc, *flat, *extra),
        [SM] + [ANY] * len(flat) + [VM] * len(extra),
        outs,
        [
            pltpu.VMEM((len(lefts), rows, FOUR * tok), BF16),
            pltpu.VMEM((FOUR * tok, width), BF16),
            pltpu.SemaphoreType.DMA((len(lefts) + 1, FOUR)),
        ],
        after,
        16,
    )


def halve_kernel(step, sc, kept, came, keep, send):
    bit = (sc[1] >> step) & 1

    @pl.loop(0, keep.shape[0])
    def _(i):
        for ref, half in ((send, 1 - bit), (keep, bit)):
            total = kept[2 * i + half].astype(F32) + came[2 * i + half].astype(F32)
            ref[i] = total.astype(BF16)


def halve(sc, kept, came, step, after=()):
    half = shape((kept.shape[0] // 2,) + kept.shape[1:], BF16)
    return call(
        functools.partial(halve_kernel, step),
        "halve", (sc, kept, came), [SM, VM, VM], (half, half), after=after,
    )


def split_kernel(sc, *refs):
    ins, (mine, other, total) = refs[:-3], refs[-3:]
    rows = mine.shape[0]
    value = ins[0][...].astype(F32)
    for ref in ins[1:]:
        value = value + ref[...].astype(F32)
    total[...] = value
    x = sc[2]
    for ref, at in ((mine, x), (other, 1 - x)):
        ref[...] = total[pl.ds(pl.multiple_of(at * rows, rows), rows), :].astype(BF16)


def split_rows(sc, terms, after=()):
    rows, width = terms[0].shape
    mine, other = call(
        split_kernel, "split_rows", (sc, *terms), [SM] + [VM] * len(terms),
        (shape((rows // 2, width), BF16),) * 2,
        [pltpu.VMEM((rows, width), F32)], after=after,
    )
    return plane_swap([mine, mine, other, other])


def swap(value, axis):
    return lax.ppermute(value, axis, [(0, 1), (1, 0)])


def plane_swap(parts):
    moved = [parts[0]]
    for k in range(1, FOUR):
        moved.append(lax.ppermute(parts[k], PLANE, [(d, d ^ k) for d in range(FOUR)]))
    return moved


def put_tiles(place, part, ref):
    start = start_tile(place)
    twice = (place > 0) & (start < start_tile(place - 1) + TILES)
    for i in range(TILES):

        @pl.when(jnp.logical_not(twice) if i == 0 else start >= 0)
        def _():
            cols = pl.ds(pl.multiple_of((start + i) * LANE, LANE), LANE)
            ref[:, cols] = part[:, i * LANE : (i + 1) * LANE]


def place_kernel(plan, sc, *refs):
    parts = refs[:FOUR]
    outs = refs[FOUR:]
    for k in range(FOUR):
        place = sc[4] ^ k
        part = parts[k][...].astype(F32)
        for (begin, stop, tiled), ref in zip(plan, outs):
            size = stop - begin
            if tiled:
                put_tiles(place, part[:, begin:stop], ref)
            else:
                ref[:, pl.ds(pl.multiple_of(place * size, size), size)] = part[:, begin:stop]
    if len(outs) > len(plan):
        expand, gains = outs[len(plan) :]
        begin = plan[-1][1]
        total = [None] * FOUR
        for k in range(FOUR):
            total[k] = parts[k][:, begin:].astype(F32)
        even = [jnp.where(sc[4] % 2 == 0, total[i], total[i + 1]) for i in (0, 2)]
        odd = [jnp.where(sc[4] % 2 == 0, total[i + 1], total[i]) for i in (0, 2)]
        value = (even[0] + odd[0]) + (even[1] + odd[1])
        size = expand.shape[0]
        for j in range(FOUR):
            expand[:, j * HD : (j + 1) * HD] = value[j * size : (j + 1) * size, :HD]
        gains[...] = value.T[HD : HD + 8, :]


def put(sc, parts, plan, widths, small=0, after=()):
    rows = parts[0].shape[0]
    outs = tuple(shape((rows, width), F32) for width in widths)
    if small:
        outs += (shape((rows // FOUR, small), F32), shape((8, rows), F32))
    return call(
        functools.partial(place_kernel, plan), "put", (sc, *parts), [SM] + [VM] * FOUR,
        outs, after=after,
    )


def enter_kernel(hidden, gain, wl, we, normed, latent, kv):
    value, unused = norm_forward(hidden[...].astype(F32), gain_row(gain))
    low = value.astype(BF16)
    normed[...] = low
    rows = nn(low, wl[...]).astype(BF16)
    latent[...] = rows
    for g in range(GROUPS):
        span = slice(g * LANE, (g + 1) * LANE)
        kv[:, span] = nn(rows[:, g * LAT : (g + 1) * LAT], we[:, span]).astype(BF16)


def enter(hidden, gain, wl, we):
    tok, width = hidden.shape
    return call(
        enter_kernel,
        "enter",
        (hidden, gain, wl, we),
        [VM] * 4,
        (
            shape((tok, width), BF16),
            shape((tok, wl.shape[1]), BF16),
            shape((tok, we.shape[1]), BF16),
        ),
        room=60,
    )


def query_kernel(nz, normed, dy, wq, qp, left):
    low = normed[...]
    left[0] = by_core(dy[...].astype(F32).T, nz).astype(BF16)
    left[1] = by_core(low.astype(F32).T, nz).astype(BF16)
    turned = (nn(low, wq[...]).astype(BF16) * scale).T
    qp[:, HD:, :] = jnp.zeros((GROUPS, HD, qp.shape[2]), BF16)
    for g in range(GROUPS):
        for h in range(PER):
            row = (g * PER + h) * HD
            qp[g, 0:HD, h * LANE : (h + 1) * LANE] = turned[row : row + HD, :]


def query(normed, dy, wq, nz, after=()):
    tok, width = normed.shape
    return call(
        functools.partial(query_kernel, nz),
        "query",
        (normed, dy, wq),
        [VM] * 3,
        (
            shape((GROUPS, 2 * HD, PER * tok), BF16),
            shape((2, width, tok), BF16),
        ),
        after=after,
    )


def leave_kernel(nz, count, sc, hidden, dmid, gain, dq, base, latent, gain_two, we, wl, *refs):
    moved = refs[:count]
    input_grad, small = refs[count : count + 2]
    sends = refs[count + 2 : count + 2 + FOUR]
    lat, terms = refs[count + 2 + FOUR :]
    total = moved[0][...].astype(F32)
    for ref in moved[1:]:
        total = total + ref[...].astype(F32)
    kv_grad = total.astype(BF16)
    rows = latent[...]
    expand = []
    for g in range(GROUPS):
        span = slice(g * LANE, (g + 1) * LANE)
        wide = slice(g * LAT, (g + 1) * LAT)
        lat[:, wide] = nt(kv_grad[:, span], we[:, span])
        expand.append(tn(kv_grad[:, span], rows[:, wide]))
    expand = jnp.concatenate(expand, axis=0)
    grad = base[...] + nt(lat[...].astype(BF16), wl[...])
    value = hidden[...].astype(F32)
    inverse = lax.rsqrt(jnp.mean(value * value, axis=-1, keepdims=True) + eps)
    hidden_grad, gains = norm_backward(value, gain_row(gain), inverse, grad)
    input_grad[...] = (hidden_grad + dmid[...]).astype(BF16)
    width = gains.shape[1]
    blank = jnp.zeros((HD, width), F32)
    tail = jnp.zeros((LANE - HD - 2, width), F32)
    terms[...] = jnp.concatenate([blank, gains, gain_two[...], tail], axis=0).T
    count = nz * 4
    size, tall = width // count, expand.shape[0] // count
    for i in range(count):
        for j in range(FOUR):
            at = i * size + j * tall
            terms[at : at + tall, :HD] = expand[i * tall : (i + 1) * tall, j * HD : (j + 1) * HD]
    small[...] = by_core(terms[...], nz).astype(BF16)
    part, half = dq.shape[1] // FOUR, lat.shape[1] // FOUR
    for k in range(FOUR):
        place = sc[4] ^ k
        cols = pl.ds(pl.multiple_of(place * part, part), part)
        sends[k][:, :part] = dmid[:, cols].astype(BF16)
        sends[k][:, part : 2 * part] = dq[:, cols]
        cols = pl.ds(pl.multiple_of(place * half, half), half)
        sends[k][:, 2 * part :] = lat[:, cols].astype(BF16)


def leave(sc, hidden, dmid, gain, dq, base, latent, gain_two, we, wl, moved, nz, after=()):
    tok, width = hidden.shape
    lat = latent.shape[1]
    return call(
        functools.partial(leave_kernel, nz, len(moved)),
        "leave",
        (sc, hidden, dmid, gain, dq, base, latent, gain_two, we, wl, *moved),
        [SM] + [VM] * (9 + len(moved)),
        (shape((tok, width), BF16), shape((width, LANE), BF16))
        + (shape((tok, (2 * width + lat) // FOUR), BF16),) * FOUR,
        [pltpu.VMEM((tok, lat), F32), pltpu.VMEM((width, LANE), F32)],
        after,
        60,
    )


def shards(
    inputs, lengths, proj_query, proj_latent, proj_expand, proj_output,
    ffn_gate, ffn_up, ffn_down, norm_attn, norm_ffn, cotangent,
):
    tok, width = inputs.shape[1:]
    nz = lax.axis_size("z")
    z, x, core, batch = [lax.axis_index(a) for a in ("z", "x", "core", "batch")]
    place = x * 2 + batch
    hidden_size = ffn_gate.shape[1]
    first = ((z * 2 + x) * 2 + core) * tok
    sc = jnp.stack([first, z, x, core, place, place, place, place]).astype(jnp.int32)
    sc = jnp.concatenate([sc, lengths[0]])

    hidden = inputs[0]
    dy = cotangent[0]

    def across(value, step):
        return lax.ppermute(value, "z", [(i, i ^ (1 << step)) for i in range(nz)])

    normed, latent, kv = enter(hidden, norm_attn, proj_latent, proj_expand)
    relative = nz <= 4
    if relative:
        moved = [kv]
        for k in range(1, nz):
            moved.append(lax.ppermute(kv, "z", [(i, i + k) for i in range(nz - k)]))
        k00 = stack(moved, after=(sc,))
    else:
        k00 = lax.all_gather(kv, "z", axis=0)
    qp, left = query(normed, dy, proj_query, nz, after=(k00,))
    early = lax.all_gather(left, PLANE, axis=0)
    k01 = swap(k00, "x")
    k10 = swap(k00, "core")
    k11 = swap(k01, "core")

    kvs, ot, logs, left_o, left_n2, mid, normed_two = attend(
        sc, (k00, k01, k10, k11), qp, hidden, proj_output, norm_ffn, nz, relative
    )
    n2s = plane_swap([left_n2] * FOUR)
    os = lax.all_gather(left_o, PLANE, axis=0)
    fed = feed(sc, normed_two, dy, mid, norm_ffn, proj_output, ffn_gate, ffn_up, ffn_down)
    output, dmid, dop, gain_two = fed[FOUR:]
    parts_a = plane_swap(fed[:FOUR])

    def blocks(value):
        return value.reshape((nz, -1) + value.shape[1:])

    chunks = {}
    last = []

    def begin(name, keep, send):
        chunks[name] = (blocks(keep), blocks(swap(send, "core")), 0)

    def advance(name):
        keep, came, step = chunks[name]
        while True:
            keep, send = halve(sc, keep, came, step, after=last[-1:])
            last.append(keep)
            came = across(send, step)
            step += 1
            if step == 1 or (1 << step) >= nz:
                break
        chunks[name] = (keep, came, step)

    def finish(name):
        keep, came, unused = chunks[name]
        chunks[name] = split_rows(sc, (keep[0], came[0]), after=last[-1:])
        last.append(chunks[name][0])

    def place_out(name, plan, widths, small=0):
        outs = put(sc, chunks[name], plan, widths, small, after=last[-1:])
        last.append(outs[0])
        return outs

    dq, keep_own, keep_far, send_own, send_far = attend_back(
        sc, kvs, qp, dop, ot, logs, nz, tok, after=n2s[1:]
    )
    rest, side = kv_add(
        (keep_own, keep_far, swap(send_own, "core"), swap(send_far, "core")), after=(early,)
    )
    side = swap(side, "x")
    if relative:
        moved = list(kv_split(sc, rest, side, after=parts_a[1:]))
        last.append(moved[0])
        for k in range(1, nz):
            moved[k] = lax.ppermute(moved[k], "z", [(i, i - k) for i in range(k, nz)])
    else:
        term = rest + side.astype(F32)
        moved = [lax.psum_scatter(term, "z", scatter_dimension=0, tiled=False)]
    terms = weight_terms(
        sc,
        ((None, tuple(n2s)), (0, (early,))),
        parts_a,
        (((0, 0, WIDE),), ((0, WIDE, 2 * WIDE),), ((1, 2 * WIDE, 3 * WIDE),)),
        after=last[-1:],
    )
    last.append(terms[0])
    for i, name in enumerate(("gate", "up", "down")):
        begin(name, *terms[2 * i : 2 * i + 2])
    for name in ("gate", "up", "down"):
        advance(name)
    base = nt(dq, proj_query)
    left_out = leave(
        sc, hidden, dmid, norm_attn, dq, base, latent, gain_two, proj_expand, proj_latent,
        moved, nz, after=(last[-1], os),
    )
    input_grad, small = left_out[:2]
    last.append(input_grad)
    parts_c = plane_swap(left_out[2:])
    advance("gate")
    advance("up")
    finish("gate")
    part, lat_part = width // FOUR, latent.shape[1] // FOUR
    end = 2 * part + lat_part
    terms = weight_terms(
        sc,
        ((None, (os,)), (1, (early,))),
        parts_c,
        (((0, 0, part), (1, part, end)),),
        (small,),
        after=last[-1:],
    )
    last.append(terms[0])
    begin("rest", *terms)
    advance("down")
    advance("rest")
    finish("up")
    advance("rest")
    finish("down")
    (grad_gate,) = place_out("gate", ((0, WIDE, True),), (hidden_size,))
    (grad_up,) = place_out("up", ((0, WIDE, True),), (hidden_size,))
    finish("rest")
    (grad_down_t,) = place_out("down", ((0, WIDE, True),), (hidden_size,))
    grad_output, grad_query, grad_latent, expand_t, gains = place_out(
        "rest",
        ((0, part, False), (part, 2 * part, False), (2 * part, end, False)),
        (width, width, latent.shape[1]),
        LAT,
    )
    grad_expand = expand_t.T
    grad_norm_attn, grad_norm_ffn = gains[0], gains[1]
    return (
        output[None],
        input_grad[None],
        grad_query,
        grad_latent,
        grad_expand,
        grad_output,
        grad_gate,
        grad_up,
        grad_down_t.T,
        grad_norm_attn,
        grad_norm_ffn,
    )


def solution(mesh):
    seq, batch = mesh.shape["seq"], mesh.shape["batch"]
    fine = Mesh(mesh.devices.reshape(seq // 4, 2, 2, batch), SEQ + ("batch",))
    return jax.shard_map(
        shards,
        mesh=fine,
        in_specs=(P("batch", SEQ, None), P("batch", None))
        + (P(),) * 9
        + (P("batch", SEQ, None),),
        out_specs=(
            P("batch", SEQ, None),
            P("batch", SEQ, None),
            P(SEQ, None),
            P(SEQ, None),
            P(None, SEQ),
            P(SEQ, None),
            P(SEQ, None),
            P(SEQ, None),
            P(None, SEQ),
            P(SEQ),
            P(SEQ),
        ),
        check_vma=False,
    )
```

```python
import functools

import jax
import jax.numpy as jnp
from jax import lax
from jax.experimental import pallas as pl
from jax.experimental.pallas import tpu as pltpu
from jax.sharding import Mesh
from jax.sharding import PartitionSpec as P

HEADS = 16
HD = 64
GROUPS = 2
PER = HEADS // GROUPS
LAT = 256
DOCS = 8
LANE = 128
CHUNK = 256

F32 = jnp.float32
BF16 = jnp.bfloat16
eps = 1e-05
scale = 0.125
masked = -1e30

SEQ = ("z", "x", "core")
PLANE = ("x", "batch")
FOUR = 4
TILES = 6
WIDE = TILES * LANE

VM = pl.BlockSpec(memory_space=pltpu.VMEM)
SM = pl.BlockSpec(memory_space=pltpu.SMEM)
ANY = pl.BlockSpec(memory_space=pl.ANY)
HB = pl.BlockSpec(memory_space=pltpu.HBM)
MIB = 1024 * 1024


def nn(left, right):
    return jnp.dot(left, right, preferred_element_type=F32)


def tn(left, right):
    return lax.dot_general(left, right, (((0,), (0,)), ((), ())), preferred_element_type=F32)


def nt(left, right):
    return lax.dot_general(left, right, (((1,), (1,)), ((), ())), preferred_element_type=F32)


def shape(dims, dtype):
    return jax.ShapeDtypeStruct(dims, dtype)


def cost(micros):
    return pl.CostEstimate(flops=0, bytes_accessed=int(micros * 3.6e6), transcendentals=0)


def call(kernel, name, ins, specs, outs, scratch=(), after=(), room=8, micros=0.01):
    count, extra = len(ins), len(after)

    def body(*refs):
        kernel(*refs[:count], *refs[count + extra :])

    return pl.pallas_call(
        body,
        out_shape=tuple(outs),
        in_specs=list(specs) + [ANY] * extra,
        out_specs=(VM,) * len(outs),
        scratch_shapes=list(scratch),
        compiler_params=pltpu.CompilerParams(vmem_limit_bytes=room * MIB),
        cost_estimate=cost(micros),
        name=name,
    )(*ins, *after)


def gain_row(gain):
    return gain[...].astype(F32)[None]


def norm_forward(hidden, gain):
    inverse = lax.rsqrt(jnp.mean(hidden * hidden, axis=-1, keepdims=True) + eps)
    return (hidden * inverse * gain, inverse)


def norm_backward(hidden, gain, inverse, grad):
    scaled = grad * gain
    gain_grad = jnp.sum(grad * hidden * inverse, axis=0, keepdims=True)
    cubed = inverse * inverse * inverse
    hidden_grad = inverse * scaled - hidden * cubed * jnp.mean(
        scaled * hidden, axis=-1, keepdims=True
    )
    return (hidden_grad, gain_grad)


def by_core(value, nz):
    size = value.shape[0] // (nz * 4)
    rows = [value[i * size : (i + 1) * size] for i in range(nz * 4)]
    order = [i + j for i in range(0, nz * 4, 4) for j in (0, 2, 1, 3)]
    return jnp.concatenate([rows[i] for i in order], axis=0)


def doc_bounds(sc, tok):
    first = sc[0]
    query = first + lax.broadcasted_iota(jnp.int32, (1, tok), 1)
    begin = jnp.zeros((1, tok), jnp.int32)
    low = jnp.int32(0)
    end = jnp.int32(0)
    for d in range(DOCS):
        end = end + sc[8 + d]
        begin = jnp.where(query >= end, end, begin)
        low = jnp.where(first >= end, end, low)
    begin = jnp.where(query >= end, query, begin)
    low = jnp.where(first >= end, first, low)
    return query, begin, low // CHUNK, (first + tok - 1) // CHUNK + 1


def chunk_bias(chunk, query, begin):
    key = chunk * CHUNK + lax.broadcasted_iota(jnp.int32, (CHUNK, LANE), 0)
    bias = jnp.where((key >= begin) & (key <= query), 0.0, masked)
    return jnp.concatenate([bias] * PER, axis=1)


def attend_kernel(
    nz, relative, sc, k00, k01, k10, k11, qp, hidden, wo, gain,
    kvs, ot, logs, left_o, left_n, mid, normed, top, total, acc, mixed_all, wo_s, sem,
):
    load = pltpu.make_async_copy(wo, wo_s, sem)
    load.start()
    tok = hidden.shape[0]
    z, x, core = sc[1], sc[2], sc[3]
    for rc, rx, ref in ((0, 0, k00), (0, 1, k01), (1, 0, k10), (1, 1, k11)):
        for k in range(nz):
            where_z = z - k if relative else k
            slot = (where_z * 2 + (rx ^ x)) * 2 + (rc ^ core)

            @pl.when(where_z >= 0)
            def _():
                kvs[pl.ds(pl.multiple_of(slot * tok, tok), tok), :] = ref[k]

    query, begin, low, high = doc_bounds(sc, tok)
    top[...] = jnp.full(top.shape, masked, F32)
    total[...] = jnp.zeros(total.shape, F32)
    acc[...] = jnp.zeros(acc.shape, F32)

    @pl.loop(low, high)
    def _(chunk):
        kv = kvs[pl.ds(pl.multiple_of(chunk * CHUNK, CHUNK), CHUNK), :]
        bias = chunk_bias(chunk, query, begin)
        for g in range(GROUPS):
            part = kv[:, g * LANE : (g + 1) * LANE]
            raw = nn(part, qp[g]) + bias
            old = top[g]
            new = jnp.maximum(old, jnp.max(raw, axis=0, keepdims=True))
            prob = jnp.exp(raw - new)
            fade = jnp.exp(old - new)
            top[g] = new
            total[g] = total[g] * fade + jnp.sum(prob, axis=0, keepdims=True)
            acc[g] = acc[g] * fade + tn(part[:, HD:], prob.astype(BF16))

    for g in range(GROUPS):
        mixed = acc[g] * (1.0 / total[g])
        ot[g] = mixed
        logs[g] = top[g] + jnp.log(total[g])
        for h in range(PER):
            row = (g * PER + h) * HD
            mixed_all[row : row + HD, :] = mixed[:, h * LANE : (h + 1) * LANE]
    every = mixed_all[...]
    left_o[...] = by_core(every, nz).astype(BF16)
    load.wait()
    middle = hidden[...].astype(F32) + tn(every.astype(BF16), wo_s[...])
    mid[...] = middle
    value, unused = norm_forward(middle, gain_row(gain))
    normed[...] = value.astype(BF16)
    left_n[...] = by_core(value.T, nz).astype(BF16)


def attend(sc, kv_parts, qp, hidden, wo, gain, nz, relative, after=()):
    tok, width = hidden.shape
    left = shape((width, tok), BF16)
    return call(
        functools.partial(attend_kernel, nz, relative),
        "attend",
        (sc, *kv_parts, qp, hidden, wo, gain),
        [SM] + [VM] * 6 + [ANY, VM],
        (
            shape((nz * 4 * tok, 2 * LANE), BF16),
            shape((GROUPS, HD, PER * tok), F32),
            shape((GROUPS, 1, PER * tok), F32),
            left,
            left,
            shape((tok, width), F32),
            shape((tok, width), BF16),
        ),
        [
            pltpu.VMEM((GROUPS, 1, PER * tok), F32),
            pltpu.VMEM((GROUPS, 1, PER * tok), F32),
            pltpu.VMEM((GROUPS, HD, PER * tok), F32),
            pltpu.VMEM((HEADS * HD, tok), F32),
            pltpu.VMEM(wo.shape, BF16),
            pltpu.SemaphoreType.DMA,
        ],
        after,
        60,
    )


def start_tile(place):
    return (place * 11) // 2


def feed_kernel(tile, sc, normed, grad_out, mid, gain, wo, wg, wu, wd, *rest):
    sends = rest[:FOUR]
    output, dmid, dop, gain_grad = rest[FOUR : FOUR + 4]
    vg, vu, vd, vo, dgate_s, dup_s, act_s, sems = rest[FOUR + 4 :]
    steps = wd.shape[0] // tile
    copies = []
    for t in range(steps):
        span = pl.ds(t * tile, tile)
        copies.append(
            (
                pltpu.make_async_copy(wg.at[:, span], vg.at[:, span], sems.at[0, t]),
                pltpu.make_async_copy(wu.at[:, span], vu.at[:, span], sems.at[1, t]),
                pltpu.make_async_copy(wd.at[span, :], vd.at[span, :], sems.at[2, t]),
            )
        )
    copies.append((pltpu.make_async_copy(wo, vo, sems.at[3, 0]),))
    for group in copies:
        for copy in group:
            copy.start()
    n2 = normed[...]
    dy = grad_out[...]
    for t in range(steps):
        span = slice(t * tile, (t + 1) * tile)
        for copy in copies[t]:
            copy.wait()
        gate = nn(n2, vg[:, span])
        upper = nn(n2, vu[:, span])
        d_act = nt(dy, vd[span, :])
        sigma = jax.nn.sigmoid(gate)
        swish = gate * sigma
        act_s[:, span] = (swish * upper).astype(BF16)
        dgate_s[:, span] = (d_act * upper * sigma * (1.0 + gate * (1.0 - sigma))).astype(BF16)
        dup_s[:, span] = (d_act * swish).astype(BF16)
    copies[steps][0].wait()
    middle = mid[...]
    output[...] = (middle + nn(act_s[...], vd[...])).astype(BF16)
    back = nt(dgate_s[...], vg[...]) + nt(dup_s[...], vu[...])
    inverse = lax.rsqrt(jnp.mean(middle * middle, axis=-1, keepdims=True) + eps)
    grad, gains = norm_backward(middle, gain_row(gain), inverse, back)
    grad = grad + dy.astype(F32)
    dmid[...] = grad
    gain_grad[...] = gains
    for k in range(FOUR):
        cols = pl.ds(pl.multiple_of(start_tile(sc[4] ^ k) * LANE, LANE), WIDE)
        for i, ref in enumerate((dgate_s, dup_s, act_s)):
            sends[k][:, i * WIDE : (i + 1) * WIDE] = ref[:, cols]
    turned = nt(vo[...], grad.astype(BF16)).astype(BF16)
    dop[:, 0:HD, :] = jnp.zeros((GROUPS, HD, dop.shape[2]), BF16)
    for g in range(GROUPS):
        for h in range(PER):
            row = (g * PER + h) * HD
            dop[g, HD:, h * LANE : (h + 1) * LANE] = turned[row : row + HD, :]


def feed(sc, normed, grad_out, mid, gain, wo, wg, wu, wd, after=()):
    tok, width = normed.shape
    hidden = wg.shape[1]
    tile = 2 * LANE
    return call(
        functools.partial(feed_kernel, tile),
        "feed",
        (sc, normed, grad_out, mid, gain, wo, wg, wu, wd),
        [SM] + [VM] * 4 + [ANY] * 4,
        (shape((tok, 3 * WIDE), BF16),) * FOUR
        + (
            shape((tok, width), BF16),
            shape((tok, width), F32),
            shape((GROUPS, 2 * HD, PER * tok), BF16),
            shape((1, width), F32),
        ),
        [
            pltpu.VMEM((width, hidden), BF16),
            pltpu.VMEM((width, hidden), BF16),
            pltpu.VMEM((hidden, width), BF16),
            pltpu.VMEM((width, width), BF16),
            pltpu.VMEM((tok, hidden), BF16),
            pltpu.VMEM((tok, hidden), BF16),
            pltpu.VMEM((tok, hidden), BF16),
            pltpu.SemaphoreType.DMA((4, hidden // tile)),
        ],
        after,
        60,
    )


def back_kernel(
    nz, sc, kvs, qp, dop, ot, logs, dq, keep_own, keep_far, send_own, send_far, acc, rows, block
):
    tok = dq.shape[0]
    x, core = sc[2], sc[3]

    @pl.loop(0, nz)
    def _(i):
        for ref in (keep_own, keep_far, send_own, send_far):
            ref[i] = jnp.zeros(ref.shape[1:], BF16)

    query, begin, low, high = doc_bounds(sc, tok)
    acc[...] = jnp.zeros(acc.shape, F32)
    for g in range(GROUPS):
        rows[g] = jnp.sum(dop[g, HD:, :].astype(F32) * ot[g], axis=0, keepdims=True)

    @pl.loop(low, high)
    def _(chunk):
        kv = kvs[pl.ds(pl.multiple_of(chunk * CHUNK, CHUNK), CHUNK), :]
        bias = chunk_bias(chunk, query, begin)
        for g in range(GROUPS):
            part = kv[:, g * LANE : (g + 1) * LANE]
            prob = jnp.exp(nn(part, qp[g]) + bias - logs[g])
            slope = (prob * (nn(part, dop[g]) - rows[g])).astype(BF16)
            block[:, g * LANE : (g + 1) * LANE] = nt(slope, qp[g]) + nt(prob.astype(BF16), dop[g])
            acc[g] += tn(part, slope)
        where_z = chunk // 2
        near = (chunk % 2) == x
        mine = block[pl.ds(pl.multiple_of(core * tok, tok), tok), :].astype(BF16)
        other = block[pl.ds(pl.multiple_of((1 - core) * tok, tok), tok), :].astype(BF16)

        @pl.when(near)
        def _():
            keep_own[where_z] = mine
            send_own[where_z] = other

        @pl.when(jnp.logical_not(near))
        def _():
            keep_far[where_z] = mine
            send_far[where_z] = other

    for g in range(GROUPS):
        for h in range(0, PER, 2):
            pair = [acc[g, 0:HD, (h + i) * LANE : (h + i + 1) * LANE] for i in range(2)]
            col = (g * PER + h) * HD
            dq[:, col : col + LANE] = (jnp.concatenate(pair, axis=0).T * scale).astype(BF16)


def attend_back(sc, kvs, qp, dop, ot, logs, nz, tok, after=()):
    part = shape((nz, tok, 2 * LANE), BF16)
    return call(
        functools.partial(back_kernel, nz),
        "attend_back",
        (sc, kvs, qp, dop, ot, logs),
        [SM] + [VM] * 5,
        (shape((tok, HEADS * HD), BF16), part, part, part, part),
        [
            pltpu.VMEM((GROUPS, 2 * HD, PER * tok), F32),
            pltpu.VMEM((GROUPS, 1, PER * tok), F32),
            pltpu.VMEM((CHUNK, 2 * LANE), F32),
        ],
        after,
        60,
        9,
    )


def stack_kernel(*refs):
    for k, ref in enumerate(refs[:-1]):
        refs[-1][k] = ref[...]


def stack(arrays, after=()):
    dims = (len(arrays),) + arrays[0].shape
    return call(
        stack_kernel, "stack", arrays, [VM] * len(arrays), (shape(dims, BF16),), after=after
    )[0]


def kv_cut_kernel(sc, *refs):
    given, rest = refs[:4], refs[4:]
    own, sends, held, sems = rest[0], rest[1:-2], rest[-2], rest[-1]
    copies = [pltpu.make_async_copy(given[i], held.at[i], sems.at[i]) for i in range(4)]
    for copy in copies:
        copy.start()
    for copy in copies:
        copy.wait()
    z = sc[1]
    for i in range(2):
        own[i] = held[i, z].astype(F32) + held[i + 2, z].astype(F32)
        for k, ref in enumerate(sends):
            at = jnp.maximum(z - k - 1, 0)
            ref[i] = (held[i, at].astype(F32) + held[i + 2, at].astype(F32)).astype(BF16)


def kv_cut(sc, terms, count, after=()):
    dims = (2,) + terms[0].shape[1:]
    return call(
        kv_cut_kernel, "kv_cut", (sc, *terms), [SM] + [HB] * 4,
        (shape(dims, F32),) + (shape(dims, BF16),) * count,
        [pltpu.VMEM((4,) + terms[0].shape, BF16), pltpu.SemaphoreType.DMA((4,))],
        after=after, room=12,
    )


def base_kernel(dq, wq, base):
    base[...] = nt(dq[...], wq[...])


def base_terms(dq, wq, after=()):
    return call(
        base_kernel, "base", (dq, wq), [VM] * 2, (shape((dq.shape[0], wq.shape[0]), F32),),
        after=after, room=12,
    )[0]


def kv_sum_kernel(*refs):
    moved, (rest, side) = refs[:-2], refs[-2:]
    total = moved[0][...].astype(F32)
    for ref in moved[1:]:
        total = total + ref[...].astype(F32)
    rest[...] = total[0]
    side[...] = total[1].astype(BF16)


def kv_sum(moved, after=()):
    dims = moved[0].shape[1:]
    return call(
        kv_sum_kernel, "kv_sum", moved, [VM] * len(moved), (shape(dims, F32), shape(dims, BF16)),
        after=after,
    )


def weight_kernel(counts, plan, extra, split, sc, *refs):
    lefts = []
    for count in counts:
        lefts.append(refs[:count])
        refs = refs[count:]
    rights, refs = refs[:FOUR], refs[FOUR:]
    added, refs = refs[:extra], refs[extra:]
    outs, (wide, tall, made, sems) = refs[:-4], refs[-4:]
    tok = rights[0].shape[-2]
    copies = []
    for k in range(FOUR):
        span = pl.ds(k * tok, tok)
        count = tall.shape[1]
        pairs = [(rights[k].at[:, 0:count], tall.at[span, :])]
        for at in range(count, rights[k].shape[1], LANE):
            which, row = divmod(at - count, wide.shape[1])
            pairs.append((rights[k].at[:, at : at + LANE], wide.at[which, row : row + LANE, span]))
        for t, (source, target) in enumerate(pairs):
            copies.append(pltpu.make_async_copy(source, target, sems.at[len(counts) + t, k]))
        for i, count in enumerate(counts):
            if count == 0:
                continue
            source = lefts[i][0].at[sc[4] ^ k]
            copies.append(pltpu.make_async_copy(source, wide.at[i, :, span], sems.at[i, k]))
    for copy in copies:
        copy.start()
    for copy in copies:
        copy.wait()
    ref = outs[0] if not split else made
    for index, begin, stop in plan:
        for at in range(begin, stop, CHUNK):
            cols = slice(at, min(at + CHUNK, stop))
            ref[:, cols] = nn(wide[index], tall[:, cols]).astype(BF16)
    for other in added:
        ref[:, plan[-1][2] :] = other[...]
    if split:
        keep, send = outs
        nz, size, unused = keep.shape

        @pl.loop(0, nz)
        def _(i):
            for out, where in ((send, 1 - sc[3]), (keep, sc[3])):
                rows = pl.ds(pl.multiple_of((2 * i + where) * size, size), size)
                out[i] = made[rows, :]


def weight_terms(sc, lefts, rights, plan, extra=(), nz=None, after=()):
    tok = rights[0].shape[-2]
    width = plan[-1][2]
    rows = lefts[0][0]
    moves = 1 + (rights[0].shape[1] - width) // LANE
    wide = width + sum(array.shape[1] for array in extra)
    counts = tuple(len(arrays) for unused, arrays in lefts)
    flat = [array for unused, arrays in lefts for array in arrays] + rights
    if nz:
        outs = (shape((nz, rows // (2 * nz), wide), BF16),) * 2
    else:
        outs = (shape((rows, wide), BF16),)
    return call(
        functools.partial(weight_kernel, counts, plan, len(extra), bool(nz)),
        "weight_terms",
        (sc, *flat, *extra),
        [SM] + [ANY] * len(flat) + [VM] * len(extra),
        outs,
        [
            pltpu.VMEM((len(lefts), rows, FOUR * tok), BF16),
            pltpu.VMEM((FOUR * tok, width), BF16),
            pltpu.VMEM((rows, wide) if nz else (16, LANE), BF16),
            pltpu.SemaphoreType.DMA((len(lefts) + moves, FOUR)),
        ],
        after,
        20,
    )


def halve_kernel(step, sc, kept, came, keep, send):
    bit = (sc[1] >> step) & 1

    @pl.loop(0, keep.shape[0])
    def _(i):
        for ref, half in ((send, 1 - bit), (keep, bit)):
            total = kept[2 * i + half].astype(F32) + came[2 * i + half].astype(F32)
            ref[i] = total.astype(BF16)


def halve(sc, kept, came, step, after=()):
    half = shape((kept.shape[0] // 2,) + kept.shape[1:], BF16)
    return call(
        functools.partial(halve_kernel, step),
        "halve", (sc, kept, came), [SM, VM, VM], (half, half), after=after,
    )


def split_kernel(sc, *refs):
    ins, (mine, other, total) = refs[:-3], refs[-3:]
    rows = mine.shape[0]
    value = (ins[0][sc[1]] if len(ins[0].shape) == 3 else ins[0][...]).astype(F32)
    for ref in ins[1:]:
        value = value + ref[...].astype(F32)
    total[...] = value
    x = sc[2]
    for ref, at in ((mine, x), (other, 1 - x)):
        ref[...] = total[pl.ds(pl.multiple_of(at * rows, rows), rows), :].astype(BF16)


def split_rows(sc, terms, after=()):
    rows, width = terms[0].shape[-2:]
    mine, other = call(
        split_kernel, "split_rows", (sc, *terms), [SM] + [VM] * len(terms),
        (shape((rows // 2, width), BF16),) * 2,
        [pltpu.VMEM((rows, width), F32)], after=after, room=16,
    )
    return plane_swap([mine, mine, other, other])


def swap(value, axis):
    return lax.ppermute(value, axis, [(0, 1), (1, 0)])


def plane_swap(parts):
    moved = [parts[0]]
    for k in range(1, FOUR):
        moved.append(lax.ppermute(parts[k], PLANE, [(d, d ^ k) for d in range(FOUR)]))
    return moved


def place_kernel(plan, count, sc, *refs):
    results = refs[count : count + max(entry[3] for entry in plan) + 1]
    small = refs[count + len(results) :]
    for k in range(FOUR):
        place = sc[4] ^ k
        start = start_tile(place)
        twice = (place > 0) & (start < start_tile(place - 1) + TILES)
        for chunk, begin, stop, to, first in plan:
            part = refs[chunk * FOUR + k][:, begin:stop].astype(F32)
            size = stop - begin
            if first is None:
                cols = pl.ds(pl.multiple_of(place * size, size), size)
                results[to][:, cols] = part
                continue
            for i in range(size // LANE):

                @pl.when(jnp.logical_not(twice) if first + i == 0 else start >= 0)
                def _():
                    cols = pl.ds(pl.multiple_of((start + first + i) * LANE, LANE), LANE)
                    results[to][:, cols] = part[:, i * LANE : (i + 1) * LANE]

    if small:
        expand, gains = small
        begin = plan[-1][2]
        total = [refs[k][:, begin:].astype(F32) for k in range(FOUR)]
        even = [jnp.where(sc[4] % 2 == 0, total[i], total[i + 1]) for i in (0, 2)]
        odd = [jnp.where(sc[4] % 2 == 0, total[i + 1], total[i]) for i in (0, 2)]
        value = (even[0] + odd[0]) + (even[1] + odd[1])
        size = expand.shape[0]
        for j in range(FOUR):
            expand[:, j * HD : (j + 1) * HD] = value[j * size : (j + 1) * size, :HD]
        gains[...] = value.T[HD : HD + 8, :]


def put(sc, parts, plan, widths, small=0, after=()):
    rows = parts[0].shape[0]
    outs = tuple(shape((rows, width), F32) for width in widths)
    if small:
        outs += (shape((rows // FOUR, small), F32), shape((8, rows), F32))
    return call(
        functools.partial(place_kernel, plan, len(parts)), "put", (sc, *parts),
        [SM] + [VM] * len(parts), outs, after=after,
    )


def enter_kernel(nz, hidden, gain, wl, we, dy, wq, latent, kv, left_dy, left_one, qp, wq_s, sem):
    load = pltpu.make_async_copy(wq, wq_s, sem)
    load.start()
    value, unused = norm_forward(hidden[...].astype(F32), gain_row(gain))
    low = value.astype(BF16)
    rows = nn(low, wl[...]).astype(BF16)
    latent[...] = rows
    for g in range(GROUPS):
        span = slice(g * LANE, (g + 1) * LANE)
        kv[:, span] = nn(rows[:, g * LAT : (g + 1) * LAT], we[:, span]).astype(BF16)
    left_dy[...] = by_core(dy[...].astype(F32).T, nz).astype(BF16)
    left_one[...] = by_core(value.T, nz).astype(BF16)
    load.wait()
    turned = (nn(low, wq_s[...]).astype(BF16) * scale).T
    qp[:, HD:, :] = jnp.zeros((GROUPS, HD, qp.shape[2]), BF16)
    for g in range(GROUPS):
        for h in range(PER):
            at = (g * PER + h) * HD
            qp[g, 0:HD, h * LANE : (h + 1) * LANE] = turned[at : at + HD, :]


def enter(hidden, gain, wl, we, dy, wq, nz):
    tok, width = hidden.shape
    left = shape((width, tok), BF16)
    return call(
        functools.partial(enter_kernel, nz),
        "enter",
        (hidden, gain, wl, we, dy, wq),
        [VM] * 5 + [HB],
        (
            shape((tok, wl.shape[1]), BF16),
            shape((tok, we.shape[1]), BF16),
            left,
            left,
            shape((GROUPS, 2 * HD, PER * tok), BF16),
        ),
        [pltpu.VMEM(wq.shape, BF16), pltpu.SemaphoreType.DMA],
        room=60,
    )


def leave_kernel(
    nz, count, sc, hidden, dmid, gain, dq, base, latent, gain_two, we, wl, left_o, left_one, *refs
):
    moved = refs[:count]
    input_grad, small = refs[count : count + 2]
    sends = refs[count + 2 : count + 2 + FOUR]
    lat, terms = refs[count + 2 + FOUR :]
    total = moved[0][...].astype(F32)
    for ref in moved[1:]:
        total = total + ref[...].astype(F32)
    kv_grad = total.astype(BF16)
    rows = latent[...]
    expand = []
    for g in range(GROUPS):
        span = slice(g * LANE, (g + 1) * LANE)
        wide = slice(g * LAT, (g + 1) * LAT)
        lat[:, wide] = nt(kv_grad[:, span], we[:, span])
        expand.append(tn(kv_grad[:, span], rows[:, wide]))
    expand = jnp.concatenate(expand, axis=0)
    grad = base[...] + nt(lat[...].astype(BF16), wl[...])
    value = hidden[...].astype(F32)
    inverse = lax.rsqrt(jnp.mean(value * value, axis=-1, keepdims=True) + eps)
    hidden_grad, gains = norm_backward(value, gain_row(gain), inverse, grad)
    input_grad[...] = (hidden_grad + dmid[...]).astype(BF16)
    width = gains.shape[1]
    blank = jnp.zeros((HD, width), F32)
    tail = jnp.zeros((LANE - HD - 2, width), F32)
    terms[...] = jnp.concatenate([blank, gains, gain_two[...], tail], axis=0).T
    count = nz * 4
    size, tall = width // count, expand.shape[0] // count
    for i in range(count):
        for j in range(FOUR):
            at = i * size + j * tall
            terms[at : at + tall, :HD] = expand[i * tall : (i + 1) * tall, j * HD : (j + 1) * HD]
    small[...] = by_core(terms[...], nz).astype(BF16)
    part, half = dq.shape[1] // FOUR, lat.shape[1] // FOUR
    for k in range(FOUR):
        place = sc[4] ^ k
        cols = pl.ds(pl.multiple_of(place * part, part), part)
        sends[k][:, :part] = dmid[:, cols].astype(BF16)
        sends[k][:, part : 2 * part] = dq[:, cols]
        cols = pl.ds(pl.multiple_of(place * half, half), half)
        end = 2 * part + half
        sends[k][:, 2 * part : end] = lat[:, cols].astype(BF16)
        for left in (left_o, left_one):
            for at in range(0, left.shape[0], LANE):
                sends[k][:, end : end + LANE] = left[at : at + LANE, :]
                end += LANE


def leave(sc, hidden, dmid, gain, dq, base, latent, gain_two, we, wl, lefts, moved, nz, after=()):
    tok, width = hidden.shape
    lat = latent.shape[1]
    return call(
        functools.partial(leave_kernel, nz, len(moved)),
        "leave",
        (sc, hidden, dmid, gain, dq, base, latent, gain_two, we, wl, *lefts, *moved),
        [SM] + [VM] * (11 + len(moved)),
        (shape((tok, width), BF16), shape((width, LANE), BF16))
        + (shape((tok, (2 * width + lat) // FOUR + 2 * width), BF16),) * FOUR,
        [pltpu.VMEM((tok, lat), F32), pltpu.VMEM((width, LANE), F32)],
        after,
        60,
    )


def shards(
    inputs, lengths, proj_query, proj_latent, proj_expand, proj_output,
    ffn_gate, ffn_up, ffn_down, norm_attn, norm_ffn, cotangent,
):
    tok, width = inputs.shape[1:]
    nz = lax.axis_size("z")
    z, x, core, batch = [lax.axis_index(a) for a in ("z", "x", "core", "batch")]
    place = x * 2 + batch
    hidden_size = ffn_gate.shape[1]
    first = ((z * 2 + x) * 2 + core) * tok
    sc = jnp.stack([first, z, x, core, place, place, place, place]).astype(jnp.int32)
    sc = jnp.concatenate([sc, lengths[0]])

    hidden = inputs[0]
    dy = cotangent[0]

    latent, kv, left_dy, left_one, qp = enter(
        hidden, norm_attn, proj_latent, proj_expand, dy, proj_query, nz
    )
    dys = lax.all_gather(left_dy, PLANE, axis=0)
    relative = nz == 4
    if relative:
        moved = [kv]
        for k in range(1, nz):
            moved.append(lax.ppermute(kv, "z", [(i, i + k) for i in range(nz - k)]))
        k00 = stack(moved, after=(sc,))
    else:
        k00 = lax.all_gather(kv, "z", axis=0)
    k01 = swap(k00, "x")
    k10 = swap(k00, "core")
    k11 = swap(k01, "core")

    kvs, ot, logs, left_o, left_n2, mid, normed_two = attend(
        sc, (k00, k01, k10, k11), qp, hidden, proj_output, norm_ffn, nz, relative
    )
    n2s = lax.all_gather(left_n2, PLANE, axis=0)
    fed = feed(
        sc, normed_two, dy, mid, norm_ffn, proj_output, ffn_gate, ffn_up, ffn_down,
        after=(dys,),
    )
    output, dmid, dop, gain_two = fed[FOUR:]
    parts_a = plane_swap(fed[:FOUR])

    last = []

    dq, keep_own, keep_far, send_own, send_far = attend_back(
        sc, kvs, qp, dop, ot, logs, nz, tok
    )
    pieces = (keep_own, keep_far, swap(send_own, "core"), swap(send_far, "core"))
    if relative:
        moved = list(kv_cut(sc, pieces, nz - 1, after=(n2s, *parts_a[1:3])))
        for k in range(1, nz):
            moved[k] = lax.ppermute(moved[k], "z", [(i, i - k) for i in range(k, nz)])
        last.append(moved[0])
    else:
        both = [pieces[i].astype(F32) + pieces[i + 2].astype(F32) for i in range(2)]
        both = jnp.stack(both, axis=1)
        moved = [lax.psum_scatter(both, "z", scatter_dimension=0, tiled=False)]
    base = base_terms(dq, proj_query, after=last[-1:])
    rest, side = kv_sum(moved, after=(base,))
    last.append(rest)
    moved = [rest, swap(side, "x")]
    (main,) = weight_terms(
        sc,
        ((width, (n2s,)), (width, (dys,))),
        parts_a,
        ((0, 0, 2 * WIDE), (1, 2 * WIDE, 3 * WIDE)),
        after=last[-1:],
    )
    last.append(main)
    main = lax.psum_scatter(main, ("z", "core"), scatter_dimension=0, tiled=True)
    left_out = leave(
        sc, hidden, dmid, norm_attn, dq, base, latent, gain_two, proj_expand, proj_latent,
        (left_o, left_one), moved, nz, after=last[-1:],
    )
    input_grad, small = left_out[:2]
    last.append(input_grad)
    parts_c = plane_swap(left_out[2:])
    part, lat_part = width // FOUR, latent.shape[1] // FOUR
    end = 2 * part + lat_part
    keep, send = weight_terms(
        sc,
        ((width, ()), (width, ())),
        parts_c,
        ((0, 0, part), (1, part, end)),
        (small,),
        nz,
        after=last[-1:],
    )
    last.append(keep)
    came = swap(send, "core")
    step = 0
    while (1 << step) < nz:
        keep, send = halve(sc, keep, came, step, after=last[-1:])
        last.append(keep)
        came = lax.ppermute(send, "z", [(i, i ^ (1 << step)) for i in range(nz)])
        step += 1
        if step == 1:
            main = split_rows(sc, (main,), after=last[-1:])
            last.append(main[0])
    rest = split_rows(sc, (keep[0], came[0]), after=last[-1:])
    last.append(rest[0])
    grad_gate, grad_up, grad_down_t = put(
        sc,
        main,
        tuple((0, i * WIDE, (i + 1) * WIDE, i, 0) for i in range(3)),
        (hidden_size,) * 3,
        after=last[-1:],
    )
    grad_output, grad_query, grad_latent, expand_t, gains = put(
        sc,
        rest,
        ((0, 0, part, 0, None), (0, part, 2 * part, 1, None), (0, 2 * part, end, 2, None)),
        (width, width, latent.shape[1]),
        LAT,
        after=(grad_gate,),
    )
    grad_expand = expand_t.T
    grad_norm_attn, grad_norm_ffn = gains[0], gains[1]
    return (
        output[None],
        input_grad[None],
        grad_query,
        grad_latent,
        grad_expand,
        grad_output,
        grad_gate,
        grad_up,
        grad_down_t.T,
        grad_norm_attn,
        grad_norm_ffn,
    )


def solution(mesh):
    seq, batch = mesh.shape["seq"], mesh.shape["batch"]
    fine = Mesh(mesh.devices.reshape(seq // 4, 2, 2, batch), SEQ + ("batch",))
    return jax.shard_map(
        shards,
        mesh=fine,
        in_specs=(P("batch", SEQ, None), P("batch", None))
        + (P(),) * 9
        + (P("batch", SEQ, None),),
        out_specs=(
            P("batch", SEQ, None),
            P("batch", SEQ, None),
            P(SEQ, None),
            P(SEQ, None),
            P(None, SEQ),
            P(SEQ, None),
            P(SEQ, None),
            P(SEQ, None),
            P(None, SEQ),
            P(SEQ),
            P(SEQ),
        ),
        check_vma=False,
    )
```

```python
import functools

import jax
import jax.numpy as jnp
from jax import lax
from jax.experimental import pallas as pl
from jax.experimental.pallas import tpu as pltpu
from jax.sharding import Mesh
from jax.sharding import PartitionSpec as P

HEADS = 16
HD = 64
GROUPS = 2
PER = HEADS // GROUPS
LAT = 256
DOCS = 8
LANE = 128
CHUNK = 256

F32 = jnp.float32
BF16 = jnp.bfloat16
eps = 1e-05
scale = 0.125
masked = -1e30

SEQ = ("z", "x", "core")
PLANE = ("x", "batch")
FOUR = 4

VM = pl.BlockSpec(memory_space=pltpu.VMEM)
SM = pl.BlockSpec(memory_space=pltpu.SMEM)
ANY = pl.BlockSpec(memory_space=pl.ANY)
HB = pl.BlockSpec(memory_space=pltpu.HBM)
MIB = 1024 * 1024


def nn(left, right):
    return jnp.dot(left, right, preferred_element_type=F32)


def tn(left, right):
    return lax.dot_general(left, right, (((0,), (0,)), ((), ())), preferred_element_type=F32)


def nt(left, right):
    return lax.dot_general(left, right, (((1,), (1,)), ((), ())), preferred_element_type=F32)


def shape(dims, dtype):
    return jax.ShapeDtypeStruct(dims, dtype)


def cost(micros):
    return pl.CostEstimate(flops=0, bytes_accessed=int(micros * 3.6e6), transcendentals=0)


def call(kernel, name, ins, specs, outs, scratch=(), after=(), room=8, micros=0.01, token=False):
    count, extra = len(ins), len(after)

    if token:
        outs = (*outs, shape((8, LANE), F32))

    def body(*refs):
        refs = refs[:count] + refs[count + extra :]
        if token:
            at = count + len(outs) - 1
            refs[at][...] = jnp.zeros((8, LANE), F32)
            refs = refs[:at] + refs[at + 1 :]
        kernel(*refs)

    return pl.pallas_call(
        body,
        out_shape=tuple(outs),
        in_specs=list(specs) + [ANY] * extra,
        out_specs=(VM,) * len(outs),
        scratch_shapes=list(scratch),
        compiler_params=pltpu.CompilerParams(vmem_limit_bytes=room * MIB),
        cost_estimate=cost(micros),
        name=name,
    )(*ins, *after)


def gain_row(gain):
    return gain[...].astype(F32)[None]


def norm_forward(hidden, gain):
    inverse = lax.rsqrt(jnp.mean(hidden * hidden, axis=-1, keepdims=True) + eps)
    return (hidden * inverse * gain, inverse)


def norm_backward(hidden, gain, inverse, grad):
    scaled = grad * gain
    gain_grad = jnp.sum(grad * hidden * inverse, axis=0, keepdims=True)
    cubed = inverse * inverse * inverse
    hidden_grad = inverse * scaled - hidden * cubed * jnp.mean(
        scaled * hidden, axis=-1, keepdims=True
    )
    return (hidden_grad, gain_grad)


def by_core(value, nz):
    size = value.shape[0] // (nz * 4)
    rows = [value[i * size : (i + 1) * size] for i in range(nz * 4)]
    order = [i + j for i in range(0, nz * 4, 4) for j in (0, 2, 1, 3)]
    return jnp.concatenate([rows[i] for i in order], axis=0)


def doc_bounds(sc, tok):
    first = sc[0]
    query = first + lax.broadcasted_iota(jnp.int32, (1, tok), 1)
    begin = jnp.zeros((1, tok), jnp.int32)
    low = jnp.int32(0)
    end = jnp.int32(0)
    for d in range(DOCS):
        end = end + sc[8 + d]
        begin = jnp.where(query >= end, end, begin)
        low = jnp.where(first >= end, end, low)
    begin = jnp.where(query >= end, query, begin)
    low = jnp.where(first >= end, first, low)
    return query, begin, low // CHUNK, (first + tok - 1) // CHUNK + 1


def chunk_bias(chunk, query, begin):
    key = chunk * CHUNK + lax.broadcasted_iota(jnp.int32, (CHUNK, LANE), 0)
    bias = jnp.where((key >= begin) & (key <= query), 0.0, masked)
    return jnp.concatenate([bias] * PER, axis=1)


def attend_kernel(
    nz, relative, sc, k00, k01, k10, k11, qp, hidden, wo, gain,
    kvs, ot, logs, left_o, left_n, mid, normed, top, total, acc, mixed_all, wo_s, sem,
):
    load = pltpu.make_async_copy(wo, wo_s, sem)
    load.start()
    tok = hidden.shape[0]
    z, x, core = sc[1], sc[2], sc[3]
    for rc, rx, ref in ((0, 0, k00), (0, 1, k01), (1, 0, k10), (1, 1, k11)):
        for k in range(nz):
            where_z = z - k if relative else k
            slot = (where_z * 2 + (rx ^ x)) * 2 + (rc ^ core)

            @pl.when(where_z >= 0)
            def _():
                kvs[pl.ds(pl.multiple_of(slot * tok, tok), tok), :] = ref[k]

    query, begin, low, high = doc_bounds(sc, tok)
    top[...] = jnp.full(top.shape, masked, F32)
    total[...] = jnp.zeros(total.shape, F32)
    acc[...] = jnp.zeros(acc.shape, F32)

    @pl.loop(low, high)
    def _(chunk):
        kv = kvs[pl.ds(pl.multiple_of(chunk * CHUNK, CHUNK), CHUNK), :]
        bias = chunk_bias(chunk, query, begin)
        for g in range(GROUPS):
            part = kv[:, g * LANE : (g + 1) * LANE]
            raw = nn(part, qp[g]) + bias
            old = top[g]
            new = jnp.maximum(old, jnp.max(raw, axis=0, keepdims=True))
            prob = jnp.exp(raw - new)
            fade = jnp.exp(old - new)
            top[g] = new
            total[g] = total[g] * fade + jnp.sum(prob, axis=0, keepdims=True)
            acc[g] = acc[g] * fade + tn(part[:, HD:], prob.astype(BF16))

    for g in range(GROUPS):
        mixed = acc[g] * (1.0 / total[g])
        ot[g] = mixed
        logs[g] = top[g] + jnp.log(total[g])
        for h in range(PER):
            row = (g * PER + h) * HD
            mixed_all[row : row + HD, :] = mixed[:, h * LANE : (h + 1) * LANE]
    every = mixed_all[...]
    left_o[...] = by_core(every, nz).astype(BF16)
    load.wait()
    middle = hidden[...].astype(F32) + tn(every.astype(BF16), wo_s[...])
    mid[...] = middle
    value, unused = norm_forward(middle, gain_row(gain))
    normed[...] = value.astype(BF16)
    left_n[...] = by_core(value.T, nz).astype(BF16)


def attend(sc, kv_parts, qp, hidden, wo, gain, nz, relative, after=()):
    tok, width = hidden.shape
    left = shape((width, tok), BF16)
    return call(
        functools.partial(attend_kernel, nz, relative),
        "attend",
        (sc, *kv_parts, qp, hidden, wo, gain),
        [SM] + [VM] * 6 + [ANY, VM],
        (
            shape((nz * 4 * tok, 2 * LANE), BF16),
            shape((GROUPS, HD, PER * tok), F32),
            shape((GROUPS, 1, PER * tok), F32),
            left,
            left,
            shape((tok, width), F32),
            shape((tok, width), BF16),
        ),
        [
            pltpu.VMEM((GROUPS, 1, PER * tok), F32),
            pltpu.VMEM((GROUPS, 1, PER * tok), F32),
            pltpu.VMEM((GROUPS, HD, PER * tok), F32),
            pltpu.VMEM((HEADS * HD, tok), F32),
            pltpu.VMEM(wo.shape, BF16),
            pltpu.SemaphoreType.DMA,
        ],
        after,
        60,
    )


def packed(hidden):
    return -(-(3 * hidden // FOUR) // LANE) * LANE


def feed_kernel(tile, sc, normed, grad_out, mid, gain, wo, wg, wu, wd, *rest):
    sends = rest[:FOUR]
    output, dmid, dop, gain_grad = rest[FOUR : FOUR + 4]
    vg, vu, vd, vo, dgate_s, dup_s, act_s, sems = rest[FOUR + 4 :]
    steps = wd.shape[0] // tile
    copies = []
    for t in range(steps):
        span = pl.ds(t * tile, tile)
        copies.append(
            (
                pltpu.make_async_copy(wg.at[:, span], vg.at[:, span], sems.at[0, t]),
                pltpu.make_async_copy(wu.at[:, span], vu.at[:, span], sems.at[1, t]),
                pltpu.make_async_copy(wd.at[span, :], vd.at[span, :], sems.at[2, t]),
            )
        )
    copies.append((pltpu.make_async_copy(wo, vo, sems.at[3, 0]),))
    for group in copies:
        for copy in group:
            copy.start()
    n2 = normed[...]
    dy = grad_out[...]
    for t in range(steps):
        span = slice(t * tile, (t + 1) * tile)
        for copy in copies[t]:
            copy.wait()
        gate = nn(n2, vg[:, span])
        upper = nn(n2, vu[:, span])
        d_act = nt(dy, vd[span, :])
        sigma = jax.nn.sigmoid(gate)
        swish = gate * sigma
        act_s[:, span] = (swish * upper).astype(BF16)
        dgate_s[:, span] = (d_act * upper * sigma * (1.0 + gate * (1.0 - sigma))).astype(BF16)
        dup_s[:, span] = (d_act * swish).astype(BF16)
    copies[steps][0].wait()
    middle = mid[...]
    output[...] = (middle + nn(act_s[...], vd[...])).astype(BF16)
    back = nt(dgate_s[...], vg[...]) + nt(dup_s[...], vu[...])
    inverse = lax.rsqrt(jnp.mean(middle * middle, axis=-1, keepdims=True) + eps)
    grad, gains = norm_backward(middle, gain_row(gain), inverse, back)
    grad = grad + dy.astype(F32)
    dmid[...] = grad
    gain_grad[...] = gains
    part = wg.shape[1] // FOUR
    for k in range(FOUR):
        place = sc[4] ^ k
        cols = pl.ds(pl.multiple_of((place // 2) * 2 * part, LANE), 2 * part)
        pieces = []
        for ref in (dgate_s, dup_s, act_s):
            both = ref[:, cols].astype(F32)
            pieces.append(jnp.where(place % 2 == 0, both[:, :part], both[:, part:]))
        pieces.append(jnp.zeros((both.shape[0], sends[k].shape[1] - 3 * part), F32))
        sends[k][...] = jnp.concatenate(pieces, axis=1).astype(BF16)
    turned = nt(vo[...], grad.astype(BF16)).astype(BF16)
    dop[:, 0:HD, :] = jnp.zeros((GROUPS, HD, dop.shape[2]), BF16)
    for g in range(GROUPS):
        for h in range(PER):
            row = (g * PER + h) * HD
            dop[g, HD:, h * LANE : (h + 1) * LANE] = turned[row : row + HD, :]


def feed(sc, normed, grad_out, mid, gain, wo, wg, wu, wd, after=()):
    tok, width = normed.shape
    hidden = wg.shape[1]
    tile = 2 * LANE
    wide = packed(hidden)
    return call(
        functools.partial(feed_kernel, tile),
        "feed",
        (sc, normed, grad_out, mid, gain, wo, wg, wu, wd),
        [SM] + [VM] * 4 + [ANY] * 4,
        (shape((tok, wide), BF16),) * FOUR
        + (
            shape((tok, width), BF16),
            shape((tok, width), F32),
            shape((GROUPS, 2 * HD, PER * tok), BF16),
            shape((1, width), F32),
        ),
        [
            pltpu.VMEM((width, hidden), BF16),
            pltpu.VMEM((width, hidden), BF16),
            pltpu.VMEM((hidden, width), BF16),
            pltpu.VMEM((width, width), BF16),
            pltpu.VMEM((tok, hidden), BF16),
            pltpu.VMEM((tok, hidden), BF16),
            pltpu.VMEM((tok, hidden), BF16),
            pltpu.SemaphoreType.DMA((4, hidden // tile)),
        ],
        after,
        60,
    )


def back_kernel(
    nz, sc, kvs, qp, dop, ot, logs, dq, keep_own, keep_far, send_own, send_far, acc, rows, block
):
    tok = dq.shape[0]
    x, core = sc[2], sc[3]

    @pl.loop(0, nz)
    def _(i):
        for ref in (keep_own, keep_far, send_own, send_far):
            ref[i] = jnp.zeros(ref.shape[1:], BF16)

    query, begin, low, high = doc_bounds(sc, tok)
    acc[...] = jnp.zeros(acc.shape, F32)
    for g in range(GROUPS):
        rows[g] = jnp.sum(dop[g, HD:, :].astype(F32) * ot[g], axis=0, keepdims=True)

    @pl.loop(low, high)
    def _(chunk):
        kv = kvs[pl.ds(pl.multiple_of(chunk * CHUNK, CHUNK), CHUNK), :]
        bias = chunk_bias(chunk, query, begin)
        for g in range(GROUPS):
            part = kv[:, g * LANE : (g + 1) * LANE]
            prob = jnp.exp(nn(part, qp[g]) + bias - logs[g])
            slope = (prob * (nn(part, dop[g]) - rows[g])).astype(BF16)
            block[:, g * LANE : (g + 1) * LANE] = nt(slope, qp[g]) + nt(prob.astype(BF16), dop[g])
            acc[g] += tn(part, slope)
        where_z = chunk // 2
        near = (chunk % 2) == x
        mine = block[pl.ds(pl.multiple_of(core * tok, tok), tok), :].astype(BF16)
        other = block[pl.ds(pl.multiple_of((1 - core) * tok, tok), tok), :].astype(BF16)

        @pl.when(near)
        def _():
            keep_own[where_z] = mine
            send_own[where_z] = other

        @pl.when(jnp.logical_not(near))
        def _():
            keep_far[where_z] = mine
            send_far[where_z] = other

    for g in range(GROUPS):
        for h in range(0, PER, 2):
            pair = [acc[g, 0:HD, (h + i) * LANE : (h + i + 1) * LANE] for i in range(2)]
            col = (g * PER + h) * HD
            dq[:, col : col + LANE] = (jnp.concatenate(pair, axis=0).T * scale).astype(BF16)


def attend_back(sc, kvs, qp, dop, ot, logs, nz, tok, after=()):
    part = shape((nz, tok, 2 * LANE), BF16)
    return call(
        functools.partial(back_kernel, nz),
        "attend_back",
        (sc, kvs, qp, dop, ot, logs),
        [SM] + [VM] * 5,
        (shape((tok, HEADS * HD), BF16), part, part, part, part),
        [
            pltpu.VMEM((GROUPS, 2 * HD, PER * tok), F32),
            pltpu.VMEM((GROUPS, 1, PER * tok), F32),
            pltpu.VMEM((CHUNK, 2 * LANE), F32),
        ],
        after,
        60,
        9,
    )


def stack_kernel(*refs):
    for k, ref in enumerate(refs[:-1]):
        refs[-1][k] = ref[...]


def stack(arrays, after=()):
    dims = (len(arrays),) + arrays[0].shape
    return call(
        stack_kernel, "stack", arrays, [VM] * len(arrays), (shape(dims, BF16),), after=after
    )[0]


def kv_cut_kernel(sc, *refs):
    given, rest = refs[:4], refs[4:]
    own, sends, held, sems = rest[0], rest[1:-2], rest[-2], rest[-1]
    copies = [pltpu.make_async_copy(given[i], held.at[i], sems.at[i]) for i in range(4)]
    for copy in copies:
        copy.start()
    for copy in copies:
        copy.wait()
    z = sc[1]
    for i in range(2):
        own[i] = held[i, z].astype(F32) + held[i + 2, z].astype(F32)
        for k, ref in enumerate(sends):
            at = jnp.maximum(z - k - 1, 0)
            ref[i] = (held[i, at].astype(F32) + held[i + 2, at].astype(F32)).astype(BF16)


def kv_cut(sc, terms, count, after=()):
    dims = (2,) + terms[0].shape[1:]
    return call(
        kv_cut_kernel, "kv_cut", (sc, *terms), [SM] + [HB] * 4,
        (shape(dims, F32),) + (shape(dims, BF16),) * count,
        [pltpu.VMEM((4,) + terms[0].shape, BF16), pltpu.SemaphoreType.DMA((4,))],
        after=after, room=6,
    )


def base_kernel(dq, wq, base):
    base[...] = nt(dq[...], wq[...])


def base_terms(dq, wq, after=()):
    return call(
        base_kernel, "base", (dq, wq), [VM] * 2, (shape((dq.shape[0], wq.shape[0]), F32),),
        after=after, room=6,
    )[0]


def kv_sum_kernel(*refs):
    moved, (rest, side) = refs[:-2], refs[-2:]
    total = moved[0][...].astype(F32)
    for ref in moved[1:]:
        total = total + ref[...].astype(F32)
    rest[...] = total[0]
    side[...] = total[1].astype(BF16)


def kv_sum(moved, after=()):
    dims = moved[0].shape[1:]
    return call(
        kv_sum_kernel, "kv_sum", moved, [VM] * len(moved), (shape(dims, F32), shape(dims, BF16)),
        after=after,
    )


def weight_kernel(counts, plan, extra, split, sc, *refs):
    lefts = []
    for count, unused in counts:
        lefts.append(refs[:count])
        refs = refs[count:]
    rights, refs = refs[:FOUR], refs[FOUR:]
    added, refs = refs[:extra], refs[extra:]
    outs, (wide, tall, made, sems) = refs[:-4], refs[-4:]
    tok = rights[0].shape[-2]
    copies = []
    for k in range(FOUR):
        span = pl.ds(k * tok, tok)
        count = tall.shape[1]
        pairs = [(rights[k].at[:, 0:count], tall.at[span, :])]
        for at in range(count, rights[k].shape[1], LANE):
            which, row = divmod(at - count, wide.shape[1])
            pairs.append((rights[k].at[:, at : at + LANE], wide.at[which, row : row + LANE, span]))
        for t, (source, target) in enumerate(pairs):
            copies.append(pltpu.make_async_copy(source, target, sems.at[len(counts) + t, k]))
        for i, (count, kind) in enumerate(counts):
            if count == 0:
                continue
            source = lefts[i][0].at[sc[4] ^ k]
            if kind is not None:
                source = lefts[i][0].at[sc[4] ^ k, kind]
            copies.append(pltpu.make_async_copy(source, wide.at[i, :, span], sems.at[i, k]))
    for copy in copies:
        copy.start()
    for copy in copies:
        copy.wait()
    ref = outs[0] if not split else made
    for index, begin, stop in plan:
        for at in range(begin, stop, CHUNK):
            cols = slice(at, min(at + CHUNK, stop))
            ref[:, cols] = nn(wide[index], tall[:, cols]).astype(BF16)
    for other in added:
        ref[:, plan[-1][2] :] = other[...]
    if split:
        keep, send = outs
        nz, size, unused = keep.shape

        @pl.loop(0, nz)
        def _(i):
            for out, where in ((send, 1 - sc[3]), (keep, sc[3])):
                rows = pl.ds(pl.multiple_of((2 * i + where) * size, size), size)
                out[i] = made[rows, :]


def weight_terms(sc, lefts, rights, plan, extra=(), nz=None, after=()):
    tok = rights[0].shape[-2]
    width = plan[-1][2]
    rows = lefts[0][0]
    moves = 1 + (rights[0].shape[1] - width) // LANE
    wide = width + sum(array.shape[1] for array in extra)
    counts = tuple((len(arrays), kind) for unused, arrays, kind in lefts)
    flat = [array for unused, arrays, kind in lefts for array in arrays] + rights
    if nz:
        outs = (shape((nz, rows // (2 * nz), wide), BF16),) * 2
    else:
        outs = (shape((rows, wide), BF16),)
    return call(
        functools.partial(weight_kernel, counts, plan, len(extra), bool(nz)),
        "weight_terms",
        (sc, *flat, *extra),
        [SM] + [ANY] * len(flat) + [VM] * len(extra),
        outs,
        [
            pltpu.VMEM((len(lefts), rows, FOUR * tok), BF16),
            pltpu.VMEM((FOUR * tok, width), BF16),
            pltpu.VMEM((rows, wide) if nz else (16, LANE), BF16),
            pltpu.SemaphoreType.DMA((len(lefts) + moves, FOUR)),
        ],
        after,
        14,
    )


def halve_kernel(step, sc, kept, came, keep, send):
    bit = (sc[1] >> step) & 1

    @pl.loop(0, keep.shape[0])
    def _(i):
        for ref, half in ((send, 1 - bit), (keep, bit)):
            total = kept[2 * i + half].astype(F32) + came[2 * i + half].astype(F32)
            ref[i] = total.astype(BF16)


def halve(sc, kept, came, step, after=()):
    half = shape((kept.shape[0] // 2,) + kept.shape[1:], BF16)
    return call(
        functools.partial(halve_kernel, step),
        "halve", (sc, kept, came), [SM, VM, VM], (half, half), after=after,
    )


def split_kernel(sc, *refs):
    ins, (mine, other, total) = refs[:-3], refs[-3:]
    rows = mine.shape[0]
    value = (ins[0][sc[1]] if len(ins[0].shape) == 3 else ins[0][...]).astype(F32)
    for ref in ins[1:]:
        value = value + ref[...].astype(F32)
    total[...] = value
    x = sc[2]
    for ref, at in ((mine, x), (other, 1 - x)):
        ref[...] = total[pl.ds(pl.multiple_of(at * rows, rows), rows), :].astype(BF16)


def split_rows(sc, terms, after=()):
    rows, width = terms[0].shape[-2:]
    mine, other = call(
        split_kernel, "split_rows", (sc, *terms), [SM] + [VM] * len(terms),
        (shape((rows // 2, width), BF16),) * 2,
        [pltpu.VMEM((rows, width), F32)], after=after, room=16,
    )
    return plane_swap([mine, mine, other, other])


def swap(value, axis):
    return lax.ppermute(value, axis, [(0, 1), (1, 0)])


def plane_swap(parts):
    moved = [parts[0]]
    for k in range(1, FOUR):
        moved.append(lax.ppermute(parts[k], PLANE, [(d, d ^ k) for d in range(FOUR)]))
    return moved


def place_kernel(plan, count, sc, *refs):
    results = refs[count : count + len(plan)]
    small = refs[count + len(plan) :]
    for k in range(0, FOUR, 2):
        place = sc[4] ^ k
        even = place % 2 == 0
        for (begin, stop), result in zip(plan, results):
            size = stop - begin
            near = refs[k][:, begin:stop].astype(F32)
            next_one = refs[k + 1][:, begin:stop].astype(F32)
            pair = [jnp.where(even, near, next_one), jnp.where(even, next_one, near)]
            cols = pl.ds(pl.multiple_of((place // 2) * 2 * size, LANE), 2 * size)
            result[:, cols] = jnp.concatenate(pair, axis=1)
    if small:
        expand, gains = small
        begin = plan[-1][1]
        total = [refs[k][:, begin:].astype(F32) for k in range(FOUR)]
        even = [jnp.where(sc[4] % 2 == 0, total[i], total[i + 1]) for i in (0, 2)]
        odd = [jnp.where(sc[4] % 2 == 0, total[i + 1], total[i]) for i in (0, 2)]
        value = (even[0] + odd[0]) + (even[1] + odd[1])
        size = expand.shape[0]
        for j in range(FOUR):
            expand[:, j * HD : (j + 1) * HD] = value[j * size : (j + 1) * size, :HD]
        gains[...] = value.T[HD : HD + 8, :]


def put(sc, parts, plan, widths, small=0, after=(), token=False):
    rows = parts[0].shape[0]
    outs = tuple(shape((rows, width), F32) for width in widths)
    if small:
        outs += (shape((rows // FOUR, small), F32), shape((8, rows), F32))
    return call(
        functools.partial(place_kernel, plan, len(parts)), "put", (sc, *parts),
        [SM] + [VM] * len(parts), outs, after=after, token=token,
    )


def enter_kernel(nz, hidden, gain, wl, we, dy, wq, latent, kv, left, qp, wq_s, sem):
    load = pltpu.make_async_copy(wq, wq_s, sem)
    load.start()
    value, unused = norm_forward(hidden[...].astype(F32), gain_row(gain))
    low = value.astype(BF16)
    rows = nn(low, wl[...]).astype(BF16)
    latent[...] = rows
    for g in range(GROUPS):
        span = slice(g * LANE, (g + 1) * LANE)
        kv[:, span] = nn(rows[:, g * LAT : (g + 1) * LAT], we[:, span]).astype(BF16)
    left[0] = by_core(dy[...].astype(F32).T, nz).astype(BF16)
    left[1] = by_core(value.T, nz).astype(BF16)
    load.wait()
    turned = (nn(low, wq_s[...]).astype(BF16) * scale).T
    qp[:, HD:, :] = jnp.zeros((GROUPS, HD, qp.shape[2]), BF16)
    for g in range(GROUPS):
        for h in range(PER):
            at = (g * PER + h) * HD
            qp[g, 0:HD, h * LANE : (h + 1) * LANE] = turned[at : at + HD, :]


def enter(hidden, gain, wl, we, dy, wq, nz):
    tok, width = hidden.shape
    return call(
        functools.partial(enter_kernel, nz),
        "enter",
        (hidden, gain, wl, we, dy, wq),
        [VM] * 5 + [HB],
        (
            shape((tok, wl.shape[1]), BF16),
            shape((tok, we.shape[1]), BF16),
            shape((2, width, tok), BF16),
            shape((GROUPS, 2 * HD, PER * tok), BF16),
        ),
        [pltpu.VMEM(wq.shape, BF16), pltpu.SemaphoreType.DMA],
        room=60,
    )


def leave_kernel(
    nz, count, sc, hidden, dmid, gain, dq, base, latent, gain_two, we, wl, left, *refs
):
    moved = refs[:count]
    input_grad, small = refs[count : count + 2]
    sends = refs[count + 2 : count + 2 + FOUR]
    lat, terms = refs[count + 2 + FOUR :]
    total = moved[0][...].astype(F32)
    for ref in moved[1:]:
        total = total + ref[...].astype(F32)
    kv_grad = total.astype(BF16)
    rows = latent[...]
    expand = []
    for g in range(GROUPS):
        span = slice(g * LANE, (g + 1) * LANE)
        wide = slice(g * LAT, (g + 1) * LAT)
        lat[:, wide] = nt(kv_grad[:, span], we[:, span])
        expand.append(tn(kv_grad[:, span], rows[:, wide]))
    expand = jnp.concatenate(expand, axis=0)
    grad = base[...] + nt(lat[...].astype(BF16), wl[...])
    value = hidden[...].astype(F32)
    inverse = lax.rsqrt(jnp.mean(value * value, axis=-1, keepdims=True) + eps)
    hidden_grad, gains = norm_backward(value, gain_row(gain), inverse, grad)
    input_grad[...] = (hidden_grad + dmid[...]).astype(BF16)
    width = gains.shape[1]
    blank = jnp.zeros((HD, width), F32)
    tail = jnp.zeros((LANE - HD - 2, width), F32)
    terms[...] = jnp.concatenate([blank, gains, gain_two[...], tail], axis=0).T
    count = nz * 4
    size, tall = width // count, expand.shape[0] // count
    for i in range(count):
        for j in range(FOUR):
            at = i * size + j * tall
            terms[at : at + tall, :HD] = expand[i * tall : (i + 1) * tall, j * HD : (j + 1) * HD]
    small[...] = by_core(terms[...], nz).astype(BF16)
    part, half = dq.shape[1] // FOUR, lat.shape[1] // FOUR
    for k in range(FOUR):
        place = sc[4] ^ k
        cols = pl.ds(pl.multiple_of(place * part, part), part)
        sends[k][:, :part] = dmid[:, cols].astype(BF16)
        sends[k][:, part : 2 * part] = dq[:, cols]
        cols = pl.ds(pl.multiple_of(place * half, half), half)
        end = 2 * part + half
        sends[k][:, 2 * part : end] = lat[:, cols].astype(BF16)
        for at in range(0, left.shape[0], LANE):
            sends[k][:, end + at : end + at + LANE] = left[at : at + LANE, :]


def leave(sc, hidden, dmid, gain, dq, base, latent, gain_two, we, wl, left, moved, nz, after=()):
    tok, width = hidden.shape
    lat = latent.shape[1]
    return call(
        functools.partial(leave_kernel, nz, len(moved)),
        "leave",
        (sc, hidden, dmid, gain, dq, base, latent, gain_two, we, wl, left, *moved),
        [SM] + [VM] * (10 + len(moved)),
        (shape((tok, width), BF16), shape((width, LANE), BF16))
        + (shape((tok, (2 * width + lat) // FOUR + width), BF16),) * FOUR,
        [pltpu.VMEM((tok, lat), F32), pltpu.VMEM((width, LANE), F32)],
        after,
        60,
    )


def shards(
    inputs, lengths, proj_query, proj_latent, proj_expand, proj_output,
    ffn_gate, ffn_up, ffn_down, norm_attn, norm_ffn, cotangent,
):
    tok, width = inputs.shape[1:]
    nz = lax.axis_size("z")
    z, x, core, batch = [lax.axis_index(a) for a in ("z", "x", "core", "batch")]
    place = x * 2 + batch
    hidden_size = ffn_gate.shape[1]
    first = ((z * 2 + x) * 2 + core) * tok
    sc = jnp.stack([first, z, x, core, place, place, place, place]).astype(jnp.int32)
    sc = jnp.concatenate([sc, lengths[0]])

    hidden = inputs[0]
    dy = cotangent[0]

    latent, kv, left, qp = enter(
        hidden, norm_attn, proj_latent, proj_expand, dy, proj_query, nz
    )
    early = lax.all_gather(left, PLANE, axis=0)
    relative = nz == 4
    if relative:
        moved = [kv]
        for k in range(1, nz):
            moved.append(lax.ppermute(kv, "z", [(i, i + k) for i in range(nz - k)]))
        k00 = stack(moved, after=(sc,))
    else:
        k00 = lax.all_gather(kv, "z", axis=0)
    k01 = swap(k00, "x")
    k10 = swap(k00, "core")
    k11 = swap(k01, "core")

    kvs, ot, logs, left_o, left_n2, mid, normed_two = attend(
        sc, (k00, k01, k10, k11), qp, hidden, proj_output, norm_ffn, nz, relative
    )
    n2s = lax.all_gather(left_n2, PLANE, axis=0)
    fed = feed(
        sc, normed_two, dy, mid, norm_ffn, proj_output, ffn_gate, ffn_up, ffn_down,
    )
    output, dmid, dop, gain_two = fed[FOUR:]
    parts_a = plane_swap(fed[:FOUR])

    quarter = hidden_size // FOUR
    last = []

    dq, keep_own, keep_far, send_own, send_far = attend_back(
        sc, kvs, qp, dop, ot, logs, nz, tok, after=(early,)
    )
    pieces = (keep_own, keep_far, swap(send_own, "core"), swap(send_far, "core"))
    if relative:
        moved = list(kv_cut(sc, pieces, nz - 1, after=parts_a[1:3]))
        for k in range(1, nz):
            moved[k] = lax.ppermute(moved[k], "z", [(i, i - k) for i in range(k, nz)])
        last.append(moved[0])
    else:
        both = [pieces[i].astype(F32) + pieces[i + 2].astype(F32) for i in range(2)]
        both = jnp.stack(both, axis=1)
        moved = [lax.psum_scatter(both, "z", scatter_dimension=0, tiled=False)]
    base = base_terms(dq, proj_query, after=last[-1:])
    rest, side = kv_sum(moved, after=(base,))
    last.append(rest)
    moved = [rest, swap(side, "x")]
    (main,) = weight_terms(
        sc,
        ((width, (n2s,), None), (width, (early,), 0)),
        parts_a,
        ((0, 0, 2 * quarter), (1, 2 * quarter, packed(hidden_size))),
        after=last[-1:],
    )
    last.append(main)
    main = lax.psum_scatter(main, ("z", "core"), scatter_dimension=0, tiled=True)
    left_out = leave(
        sc, hidden, dmid, norm_attn, dq, base, latent, gain_two, proj_expand, proj_latent,
        left_o, moved, nz, after=last[-1:],
    )
    input_grad, small = left_out[:2]
    last.append(input_grad)
    parts_c = plane_swap(left_out[2:])
    part, lat_part = width // FOUR, latent.shape[1] // FOUR
    end = 2 * part + lat_part
    keep, send = weight_terms(
        sc,
        ((width, (), None), (width, (early,), 1)),
        parts_c,
        ((0, 0, part), (1, part, end)),
        (small,),
        nz,
    )
    last.append(keep)
    came = swap(send, "core")
    step = 0
    while (1 << step) < nz:
        keep, send = halve(sc, keep, came, step, after=last[-1:])
        last.append(keep)
        came = lax.ppermute(send, "z", [(i, i ^ (1 << step)) for i in range(nz)])
        step += 1
    main = split_rows(sc, (main,), after=last[-1:])
    last.append(main[0])
    rest = split_rows(sc, (keep[0], came[0]), after=last[-1:])
    last.append(rest[0])
    grad_gate, grad_up, grad_down_t, token = put(
        sc,
        main,
        tuple((i * quarter, (i + 1) * quarter) for i in range(3)),
        (hidden_size,) * 3,
        after=last[-1:],
        token=True,
    )
    grad_output, grad_query, grad_latent, expand_t, gains = put(
        sc,
        rest,
        ((0, part), (part, 2 * part), (2 * part, end)),
        (width, width, latent.shape[1]),
        LAT,
        after=(token,),
    )
    grad_expand = expand_t.T
    grad_norm_attn, grad_norm_ffn = gains[0], gains[1]
    return (
        output[None],
        input_grad[None],
        grad_query,
        grad_latent,
        grad_expand,
        grad_output,
        grad_gate,
        grad_up,
        grad_down_t.T,
        grad_norm_attn,
        grad_norm_ffn,
    )


def solution(mesh):
    seq, batch = mesh.shape["seq"], mesh.shape["batch"]
    fine = Mesh(mesh.devices.reshape(seq // 4, 2, 2, batch), SEQ + ("batch",))
    return jax.shard_map(
        shards,
        mesh=fine,
        in_specs=(P("batch", SEQ, None), P("batch", None))
        + (P(),) * 9
        + (P("batch", SEQ, None),),
        out_specs=(
            P("batch", SEQ, None),
            P("batch", SEQ, None),
            P(SEQ, None),
            P(SEQ, None),
            P(None, SEQ),
            P(SEQ, None),
            P(SEQ, None),
            P(SEQ, None),
            P(None, SEQ),
            P(SEQ),
            P(SEQ),
        ),
        check_vma=False,
    )
```

```python
import functools

import jax
import jax.numpy as jnp
from jax import lax
from jax.experimental import pallas as pl
from jax.experimental.pallas import tpu as pltpu
from jax.sharding import Mesh
from jax.sharding import PartitionSpec as P

HEADS = 16
HD = 64
GROUPS = 2
PER = HEADS // GROUPS
LAT = 256
DOCS = 8
LANE = 128
CHUNK = 256

F32 = jnp.float32
BF16 = jnp.bfloat16
eps = 1e-05
scale = 0.125
masked = -1e30

SEQ = ("z", "x", "core")
PLANE = ("x", "batch")
FOUR = 4

VM = pl.BlockSpec(memory_space=pltpu.VMEM)
SM = pl.BlockSpec(memory_space=pltpu.SMEM)
ANY = pl.BlockSpec(memory_space=pl.ANY)
HB = pl.BlockSpec(memory_space=pltpu.HBM)
MIB = 1024 * 1024


def nn(left, right):
    return jnp.dot(left, right, preferred_element_type=F32)


def tn(left, right):
    return lax.dot_general(left, right, (((0,), (0,)), ((), ())), preferred_element_type=F32)


def nt(left, right):
    return lax.dot_general(left, right, (((1,), (1,)), ((), ())), preferred_element_type=F32)


def shape(dims, dtype):
    return jax.ShapeDtypeStruct(dims, dtype)


def cost(micros):
    return pl.CostEstimate(flops=0, bytes_accessed=int(micros * 3.6e6), transcendentals=0)


def call(kernel, name, ins, specs, outs, scratch=(), after=(), room=8, micros=0.01, token=False):
    count, extra = len(ins), len(after)

    if token:
        outs = (*outs, shape((8, LANE), F32))

    def body(*refs):
        refs = refs[:count] + refs[count + extra :]
        if token:
            at = count + len(outs) - 1
            refs[at][...] = jnp.zeros((8, LANE), F32)
            refs = refs[:at] + refs[at + 1 :]
        kernel(*refs)

    return pl.pallas_call(
        body,
        out_shape=tuple(outs),
        in_specs=list(specs) + [ANY] * extra,
        out_specs=(VM,) * len(outs),
        scratch_shapes=list(scratch),
        compiler_params=pltpu.CompilerParams(vmem_limit_bytes=room * MIB),
        cost_estimate=cost(micros),
        name=name,
    )(*ins, *after)


def gain_row(gain):
    return gain[...].astype(F32)[None]


def norm_forward(hidden, gain):
    inverse = lax.rsqrt(jnp.mean(hidden * hidden, axis=-1, keepdims=True) + eps)
    return (hidden * inverse * gain, inverse)


def norm_backward(hidden, gain, inverse, grad):
    scaled = grad * gain
    gain_grad = jnp.sum(grad * hidden * inverse, axis=0, keepdims=True)
    cubed = inverse * inverse * inverse
    hidden_grad = inverse * scaled - hidden * cubed * jnp.mean(
        scaled * hidden, axis=-1, keepdims=True
    )
    return (hidden_grad, gain_grad)


def by_core(value, nz):
    size = value.shape[0] // (nz * 4)
    rows = [value[i * size : (i + 1) * size] for i in range(nz * 4)]
    order = [i + j for i in range(0, nz * 4, 4) for j in (0, 2, 1, 3)]
    return jnp.concatenate([rows[i] for i in order], axis=0)


def doc_bounds(sc, tok):
    first = sc[0]
    query = first + lax.broadcasted_iota(jnp.int32, (1, tok), 1)
    begin = jnp.zeros((1, tok), jnp.int32)
    low = jnp.int32(0)
    end = jnp.int32(0)
    for d in range(DOCS):
        end = end + sc[8 + d]
        begin = jnp.where(query >= end, end, begin)
        low = jnp.where(first >= end, end, low)
    begin = jnp.where(query >= end, query, begin)
    low = jnp.where(first >= end, first, low)
    return query, begin, low // CHUNK, (first + tok - 1) // CHUNK + 1


def chunk_bias(chunk, query, begin):
    key = chunk * CHUNK + lax.broadcasted_iota(jnp.int32, (CHUNK, LANE), 0)
    bias = jnp.where((key >= begin) & (key <= query), 0.0, masked)
    return jnp.concatenate([bias] * PER, axis=1)


def attend_kernel(
    nz, relative, sc, k00, k01, k10, k11, qp, hidden, wo, gain,
    kvs, ot, logs, left_o, left_n, mid, normed, top, total, acc, mixed_all, wo_s, sem,
):
    load = pltpu.make_async_copy(wo, wo_s, sem)
    load.start()
    tok = hidden.shape[0]
    z, x, core = sc[1], sc[2], sc[3]
    for rc, rx, ref in ((0, 0, k00), (0, 1, k01), (1, 0, k10), (1, 1, k11)):
        for k in range(nz):
            where_z = z - k if relative else k
            slot = (where_z * 2 + (rx ^ x)) * 2 + (rc ^ core)

            @pl.when(where_z >= 0)
            def _():
                kvs[pl.ds(pl.multiple_of(slot * tok, tok), tok), :] = ref[k]

    query, begin, low, high = doc_bounds(sc, tok)
    top[...] = jnp.full(top.shape, masked, F32)
    total[...] = jnp.zeros(total.shape, F32)
    acc[...] = jnp.zeros(acc.shape, F32)

    @pl.loop(low, high)
    def _(chunk):
        kv = kvs[pl.ds(pl.multiple_of(chunk * CHUNK, CHUNK), CHUNK), :]
        bias = chunk_bias(chunk, query, begin)
        for g in range(GROUPS):
            part = kv[:, g * LANE : (g + 1) * LANE]
            raw = nn(part, qp[g]) + bias
            old = top[g]
            new = jnp.maximum(old, jnp.max(raw, axis=0, keepdims=True))
            prob = jnp.exp(raw - new)
            fade = jnp.exp(old - new)
            top[g] = new
            total[g] = total[g] * fade + jnp.sum(prob, axis=0, keepdims=True)
            acc[g] = acc[g] * fade + tn(part[:, HD:], prob.astype(BF16))

    for g in range(GROUPS):
        mixed = acc[g] * (1.0 / total[g])
        ot[g] = mixed
        logs[g] = top[g] + jnp.log(total[g])
        for h in range(PER):
            row = (g * PER + h) * HD
            mixed_all[row : row + HD, :] = mixed[:, h * LANE : (h + 1) * LANE]
    every = mixed_all[...]
    left_o[...] = by_core(every, nz).astype(BF16)
    load.wait()
    middle = hidden[...].astype(F32) + tn(every.astype(BF16), wo_s[...])
    mid[...] = middle
    value, unused = norm_forward(middle, gain_row(gain))
    normed[...] = value.astype(BF16)
    left_n[...] = by_core(value.T, nz).astype(BF16)


def attend(sc, kv_parts, qp, hidden, wo, gain, nz, relative, after=()):
    tok, width = hidden.shape
    left = shape((width, tok), BF16)
    return call(
        functools.partial(attend_kernel, nz, relative),
        "attend",
        (sc, *kv_parts, qp, hidden, wo, gain),
        [SM] + [VM] * 6 + [ANY, VM],
        (
            shape((nz * 4 * tok, 2 * LANE), BF16),
            shape((GROUPS, HD, PER * tok), F32),
            shape((GROUPS, 1, PER * tok), F32),
            left,
            left,
            shape((tok, width), F32),
            shape((tok, width), BF16),
        ),
        [
            pltpu.VMEM((GROUPS, 1, PER * tok), F32),
            pltpu.VMEM((GROUPS, 1, PER * tok), F32),
            pltpu.VMEM((GROUPS, HD, PER * tok), F32),
            pltpu.VMEM((HEADS * HD, tok), F32),
            pltpu.VMEM(wo.shape, BF16),
            pltpu.SemaphoreType.DMA,
        ],
        after,
        60,
    )


def packed(hidden):
    return -(-(3 * hidden // FOUR) // LANE) * LANE


def feed_kernel(tile, sc, normed, grad_out, mid, gain, wo, wg, wu, wd, *rest):
    sends = rest[:FOUR]
    output, dmid, dop, gain_grad = rest[FOUR : FOUR + 4]
    vg, vu, vd, vo, dgate_s, dup_s, act_s, sems = rest[FOUR + 4 :]
    steps = wd.shape[0] // tile
    copies = []
    for t in range(steps):
        span = pl.ds(t * tile, tile)
        copies.append(
            (
                pltpu.make_async_copy(wg.at[:, span], vg.at[:, span], sems.at[0, t]),
                pltpu.make_async_copy(wu.at[:, span], vu.at[:, span], sems.at[1, t]),
                pltpu.make_async_copy(wd.at[span, :], vd.at[span, :], sems.at[2, t]),
            )
        )
    copies.append((pltpu.make_async_copy(wo, vo, sems.at[3, 0]),))
    for group in copies:
        for copy in group:
            copy.start()
    n2 = normed[...]
    dy = grad_out[...]
    for t in range(steps):
        span = slice(t * tile, (t + 1) * tile)
        for copy in copies[t]:
            copy.wait()
        gate = nn(n2, vg[:, span])
        upper = nn(n2, vu[:, span])
        d_act = nt(dy, vd[span, :])
        sigma = jax.nn.sigmoid(gate)
        swish = gate * sigma
        act_s[:, span] = (swish * upper).astype(BF16)
        dgate_s[:, span] = (d_act * upper * sigma * (1.0 + gate * (1.0 - sigma))).astype(BF16)
        dup_s[:, span] = (d_act * swish).astype(BF16)
    copies[steps][0].wait()
    middle = mid[...]
    output[...] = (middle + nn(act_s[...], vd[...])).astype(BF16)
    back = nt(dgate_s[...], vg[...]) + nt(dup_s[...], vu[...])
    inverse = lax.rsqrt(jnp.mean(middle * middle, axis=-1, keepdims=True) + eps)
    grad, gains = norm_backward(middle, gain_row(gain), inverse, back)
    grad = grad + dy.astype(F32)
    dmid[...] = grad
    gain_grad[...] = gains
    part = wg.shape[1] // FOUR
    for k in range(FOUR):
        place = sc[4] ^ k
        cols = pl.ds(pl.multiple_of((place // 2) * 2 * part, LANE), 2 * part)
        pieces = []
        for ref in (dgate_s, dup_s, act_s):
            both = ref[:, cols].astype(F32)
            pieces.append(jnp.where(place % 2 == 0, both[:, :part], both[:, part:]))
        pieces.append(jnp.zeros((both.shape[0], sends[k].shape[1] - 3 * part), F32))
        sends[k][...] = jnp.concatenate(pieces, axis=1).astype(BF16)
    turned = nt(vo[...], grad.astype(BF16)).astype(BF16)
    dop[:, 0:HD, :] = jnp.zeros((GROUPS, HD, dop.shape[2]), BF16)
    for g in range(GROUPS):
        for h in range(PER):
            row = (g * PER + h) * HD
            dop[g, HD:, h * LANE : (h + 1) * LANE] = turned[row : row + HD, :]


def feed(sc, normed, grad_out, mid, gain, wo, wg, wu, wd, after=()):
    tok, width = normed.shape
    hidden = wg.shape[1]
    tile = 2 * LANE
    wide = packed(hidden)
    return call(
        functools.partial(feed_kernel, tile),
        "feed",
        (sc, normed, grad_out, mid, gain, wo, wg, wu, wd),
        [SM] + [VM] * 4 + [ANY] * 4,
        (shape((tok, wide), BF16),) * FOUR
        + (
            shape((tok, width), BF16),
            shape((tok, width), F32),
            shape((GROUPS, 2 * HD, PER * tok), BF16),
            shape((1, width), F32),
        ),
        [
            pltpu.VMEM((width, hidden), BF16),
            pltpu.VMEM((width, hidden), BF16),
            pltpu.VMEM((hidden, width), BF16),
            pltpu.VMEM((width, width), BF16),
            pltpu.VMEM((tok, hidden), BF16),
            pltpu.VMEM((tok, hidden), BF16),
            pltpu.VMEM((tok, hidden), BF16),
            pltpu.SemaphoreType.DMA((4, hidden // tile)),
        ],
        after,
        60,
    )


def back_kernel(
    nz, sc, kvs, qp, dop, ot, logs, dq, keep_own, keep_far, send_own, send_far, acc, rows, block
):
    tok = dq.shape[0]
    x, core = sc[2], sc[3]

    @pl.loop(0, nz)
    def _(i):
        for ref in (keep_own, keep_far, send_own, send_far):
            ref[i] = jnp.zeros(ref.shape[1:], BF16)

    query, begin, low, high = doc_bounds(sc, tok)
    acc[...] = jnp.zeros(acc.shape, F32)
    for g in range(GROUPS):
        rows[g] = jnp.sum(dop[g, HD:, :].astype(F32) * ot[g], axis=0, keepdims=True)

    @pl.loop(low, high)
    def _(chunk):
        kv = kvs[pl.ds(pl.multiple_of(chunk * CHUNK, CHUNK), CHUNK), :]
        bias = chunk_bias(chunk, query, begin)
        for g in range(GROUPS):
            part = kv[:, g * LANE : (g + 1) * LANE]
            prob = jnp.exp(nn(part, qp[g]) + bias - logs[g])
            slope = (prob * (nn(part, dop[g]) - rows[g])).astype(BF16)
            block[:, g * LANE : (g + 1) * LANE] = nt(slope, qp[g]) + nt(prob.astype(BF16), dop[g])
            acc[g] += tn(part, slope)
        where_z = chunk // 2
        near = (chunk % 2) == x
        mine = block[pl.ds(pl.multiple_of(core * tok, tok), tok), :].astype(BF16)
        other = block[pl.ds(pl.multiple_of((1 - core) * tok, tok), tok), :].astype(BF16)

        @pl.when(near)
        def _():
            keep_own[where_z] = mine
            send_own[where_z] = other

        @pl.when(jnp.logical_not(near))
        def _():
            keep_far[where_z] = mine
            send_far[where_z] = other

    for g in range(GROUPS):
        for h in range(0, PER, 2):
            pair = [acc[g, 0:HD, (h + i) * LANE : (h + i + 1) * LANE] for i in range(2)]
            col = (g * PER + h) * HD
            dq[:, col : col + LANE] = (jnp.concatenate(pair, axis=0).T * scale).astype(BF16)


def attend_back(sc, kvs, qp, dop, ot, logs, nz, tok, after=()):
    part = shape((nz, tok, 2 * LANE), BF16)
    return call(
        functools.partial(back_kernel, nz),
        "attend_back",
        (sc, kvs, qp, dop, ot, logs),
        [SM] + [VM] * 5,
        (shape((tok, HEADS * HD), BF16), part, part, part, part),
        [
            pltpu.VMEM((GROUPS, 2 * HD, PER * tok), F32),
            pltpu.VMEM((GROUPS, 1, PER * tok), F32),
            pltpu.VMEM((CHUNK, 2 * LANE), F32),
        ],
        after,
        60,
        9,
    )


def stack_kernel(*refs):
    for k, ref in enumerate(refs[:-1]):
        refs[-1][k] = ref[...]


def stack(arrays, after=()):
    dims = (len(arrays),) + arrays[0].shape
    return call(
        stack_kernel, "stack", arrays, [VM] * len(arrays), (shape(dims, BF16),), after=after
    )[0]


def kv_cut_kernel(sc, *refs):
    given, rest = refs[:4], refs[4:]
    own, sends, held, sems = rest[0], rest[1:-2], rest[-2], rest[-1]
    copies = [pltpu.make_async_copy(given[i], held.at[i], sems.at[i]) for i in range(4)]
    for copy in copies:
        copy.start()
    for copy in copies:
        copy.wait()
    z = sc[1]
    for i in range(2):
        own[i] = held[i, z].astype(F32) + held[i + 2, z].astype(F32)
        for k, ref in enumerate(sends):
            at = jnp.maximum(z - k - 1, 0)
            ref[i] = (held[i, at].astype(F32) + held[i + 2, at].astype(F32)).astype(BF16)


def kv_cut(sc, terms, count, after=()):
    dims = (2,) + terms[0].shape[1:]
    return call(
        kv_cut_kernel, "kv_cut", (sc, *terms), [SM] + [HB] * 4,
        (shape(dims, F32),) + (shape(dims, BF16),) * count,
        [pltpu.VMEM((4,) + terms[0].shape, BF16), pltpu.SemaphoreType.DMA((4,))],
        after=after, room=6,
    )


def base_kernel(dq, wq, base):
    base[...] = nt(dq[...], wq[...])


def base_terms(dq, wq, after=()):
    return call(
        base_kernel, "base", (dq, wq), [VM] * 2, (shape((dq.shape[0], wq.shape[0]), F32),),
        after=after, room=6,
    )[0]


def kv_sum_kernel(*refs):
    moved, (rest, side) = refs[:-2], refs[-2:]
    total = moved[0][...].astype(F32)
    for ref in moved[1:]:
        total = total + ref[...].astype(F32)
    rest[...] = total[0]
    side[...] = total[1].astype(BF16)


def kv_sum(moved, after=()):
    dims = moved[0].shape[1:]
    return call(
        kv_sum_kernel, "kv_sum", moved, [VM] * len(moved), (shape(dims, F32), shape(dims, BF16)),
        after=after,
    )


def weight_kernel(counts, plan, extra, split, sc, *refs):
    lefts = []
    for count, unused in counts:
        lefts.append(refs[:count])
        refs = refs[count:]
    rights, refs = refs[:FOUR], refs[FOUR:]
    added, refs = refs[:extra], refs[extra:]
    outs, (wide, tall, made, sems) = refs[:-4], refs[-4:]
    tok = rights[0].shape[-2]
    copies = []
    for k in range(FOUR):
        span = pl.ds(k * tok, tok)
        count = tall.shape[1]
        pairs = [(rights[k].at[:, 0:count], tall.at[span, :])]
        for at in range(count, rights[k].shape[1], LANE):
            which, row = divmod(at - count, wide.shape[1])
            pairs.append((rights[k].at[:, at : at + LANE], wide.at[which, row : row + LANE, span]))
        for t, (source, target) in enumerate(pairs):
            copies.append(pltpu.make_async_copy(source, target, sems.at[len(counts) + t, k]))
        for i, (count, kind) in enumerate(counts):
            if count == 0:
                continue
            source = lefts[i][0].at[sc[4] ^ k]
            if kind is not None:
                source = lefts[i][0].at[sc[4] ^ k, kind]
            copies.append(pltpu.make_async_copy(source, wide.at[i, :, span], sems.at[i, k]))
    for copy in copies:
        copy.start()
    for copy in copies:
        copy.wait()
    ref = outs[0] if not split else made
    for index, begin, stop in plan:
        for at in range(begin, stop, CHUNK):
            cols = slice(at, min(at + CHUNK, stop))
            ref[:, cols] = nn(wide[index], tall[:, cols]).astype(BF16)
    for other in added:
        ref[:, plan[-1][2] :] = other[...]
    if split:
        keep, send = outs
        nz, size, unused = keep.shape

        @pl.loop(0, nz)
        def _(i):
            for out, where in ((send, 1 - sc[3]), (keep, sc[3])):
                rows = pl.ds(pl.multiple_of((2 * i + where) * size, size), size)
                out[i] = made[rows, :]


def weight_terms(sc, lefts, rights, plan, extra=(), nz=None, after=()):
    tok = rights[0].shape[-2]
    width = plan[-1][2]
    rows = lefts[0][0]
    moves = 1 + (rights[0].shape[1] - width) // LANE
    wide = width + sum(array.shape[1] for array in extra)
    counts = tuple((len(arrays), kind) for unused, arrays, kind in lefts)
    flat = [array for unused, arrays, kind in lefts for array in arrays] + rights
    if nz:
        outs = (shape((nz, rows // (2 * nz), wide), BF16),) * 2
    else:
        outs = (shape((rows, wide), BF16),)
    return call(
        functools.partial(weight_kernel, counts, plan, len(extra), bool(nz)),
        "weight_terms",
        (sc, *flat, *extra),
        [SM] + [ANY] * len(flat) + [VM] * len(extra),
        outs,
        [
            pltpu.VMEM((len(lefts), rows, FOUR * tok), BF16),
            pltpu.VMEM((FOUR * tok, width), BF16),
            pltpu.VMEM((rows, wide) if nz else (16, LANE), BF16),
            pltpu.SemaphoreType.DMA((len(lefts) + moves, FOUR)),
        ],
        after,
        14 if nz else 60,
    )


def halve_kernel(step, sc, kept, came, keep, send):
    bit = (sc[1] >> step) & 1

    @pl.loop(0, keep.shape[0])
    def _(i):
        for ref, half in ((send, 1 - bit), (keep, bit)):
            total = kept[2 * i + half].astype(F32) + came[2 * i + half].astype(F32)
            ref[i] = total.astype(BF16)


def halve(sc, kept, came, step, after=()):
    half = shape((kept.shape[0] // 2,) + kept.shape[1:], BF16)
    return call(
        functools.partial(halve_kernel, step),
        "halve", (sc, kept, came), [SM, VM, VM], (half, half), after=after,
    )


def split_kernel(sc, *refs):
    ins, (mine, other, total) = refs[:-3], refs[-3:]
    rows = mine.shape[0]
    value = (ins[0][sc[1]] if len(ins[0].shape) == 3 else ins[0][...]).astype(F32)
    for ref in ins[1:]:
        value = value + ref[...].astype(F32)
    total[...] = value
    x = sc[2]
    for ref, at in ((mine, x), (other, 1 - x)):
        ref[...] = total[pl.ds(pl.multiple_of(at * rows, rows), rows), :].astype(BF16)


def split_rows(sc, terms, after=()):
    rows, width = terms[0].shape[-2:]
    mine, other = call(
        split_kernel, "split_rows", (sc, *terms), [SM] + [VM] * len(terms),
        (shape((rows // 2, width), BF16),) * 2,
        [pltpu.VMEM((rows, width), F32)], after=after, room=16,
    )
    return plane_swap([mine, mine, other, other])


def swap(value, axis):
    return lax.ppermute(value, axis, [(0, 1), (1, 0)])


def plane_swap(parts):
    moved = [parts[0]]
    for k in range(1, FOUR):
        moved.append(lax.ppermute(parts[k], PLANE, [(d, d ^ k) for d in range(FOUR)]))
    return moved


def place_kernel(plan, count, sc, *refs):
    results = refs[count : count + len(plan)]
    small = refs[count + len(plan) :]
    for k in range(0, FOUR, 2):
        place = sc[4] ^ k
        even = place % 2 == 0
        for (begin, stop), result in zip(plan, results):
            size = stop - begin
            near = refs[k][:, begin:stop].astype(F32)
            next_one = refs[k + 1][:, begin:stop].astype(F32)
            pair = [jnp.where(even, near, next_one), jnp.where(even, next_one, near)]
            cols = pl.ds(pl.multiple_of((place // 2) * 2 * size, LANE), 2 * size)
            result[:, cols] = jnp.concatenate(pair, axis=1)
    if small:
        expand, gains = small
        begin = plan[-1][1]
        total = [refs[k][:, begin:].astype(F32) for k in range(FOUR)]
        even = [jnp.where(sc[4] % 2 == 0, total[i], total[i + 1]) for i in (0, 2)]
        odd = [jnp.where(sc[4] % 2 == 0, total[i + 1], total[i]) for i in (0, 2)]
        value = (even[0] + odd[0]) + (even[1] + odd[1])
        size = expand.shape[0]
        for j in range(FOUR):
            expand[:, j * HD : (j + 1) * HD] = value[j * size : (j + 1) * size, :HD]
        gains[...] = value.T[HD : HD + 8, :]


def put(sc, parts, plan, widths, small=0, after=(), token=False):
    rows = parts[0].shape[0]
    outs = tuple(shape((rows, width), F32) for width in widths)
    if small:
        outs += (shape((rows // FOUR, small), F32), shape((8, rows), F32))
    return call(
        functools.partial(place_kernel, plan, len(parts)), "put", (sc, *parts),
        [SM] + [VM] * len(parts), outs, after=after, token=token,
    )


def enter_kernel(nz, hidden, gain, wl, we, dy, wq, latent, kv, left, qp, wq_s, sem):
    load = pltpu.make_async_copy(wq, wq_s, sem)
    load.start()
    value, unused = norm_forward(hidden[...].astype(F32), gain_row(gain))
    low = value.astype(BF16)
    rows = nn(low, wl[...]).astype(BF16)
    latent[...] = rows
    for g in range(GROUPS):
        span = slice(g * LANE, (g + 1) * LANE)
        kv[:, span] = nn(rows[:, g * LAT : (g + 1) * LAT], we[:, span]).astype(BF16)
    left[0] = by_core(dy[...].astype(F32).T, nz).astype(BF16)
    left[1] = by_core(value.T, nz).astype(BF16)
    load.wait()
    turned = (nn(low, wq_s[...]).astype(BF16) * scale).T
    qp[:, HD:, :] = jnp.zeros((GROUPS, HD, qp.shape[2]), BF16)
    for g in range(GROUPS):
        for h in range(PER):
            at = (g * PER + h) * HD
            qp[g, 0:HD, h * LANE : (h + 1) * LANE] = turned[at : at + HD, :]


def enter(hidden, gain, wl, we, dy, wq, nz):
    tok, width = hidden.shape
    return call(
        functools.partial(enter_kernel, nz),
        "enter",
        (hidden, gain, wl, we, dy, wq),
        [VM] * 5 + [HB],
        (
            shape((tok, wl.shape[1]), BF16),
            shape((tok, we.shape[1]), BF16),
            shape((2, width, tok), BF16),
            shape((GROUPS, 2 * HD, PER * tok), BF16),
        ),
        [pltpu.VMEM(wq.shape, BF16), pltpu.SemaphoreType.DMA],
        room=60,
    )


def leave_kernel(
    nz, count, sc, hidden, dmid, gain, dq, base, latent, gain_two, we, wl, left, *refs
):
    moved = refs[:count]
    input_grad, small = refs[count : count + 2]
    sends = refs[count + 2 : count + 2 + FOUR]
    lat, terms = refs[count + 2 + FOUR :]
    total = moved[0][...].astype(F32)
    for ref in moved[1:]:
        total = total + ref[...].astype(F32)
    kv_grad = total.astype(BF16)
    rows = latent[...]
    expand = []
    for g in range(GROUPS):
        span = slice(g * LANE, (g + 1) * LANE)
        wide = slice(g * LAT, (g + 1) * LAT)
        lat[:, wide] = nt(kv_grad[:, span], we[:, span])
        expand.append(tn(kv_grad[:, span], rows[:, wide]))
    expand = jnp.concatenate(expand, axis=0)
    grad = base[...] + nt(lat[...].astype(BF16), wl[...])
    value = hidden[...].astype(F32)
    inverse = lax.rsqrt(jnp.mean(value * value, axis=-1, keepdims=True) + eps)
    hidden_grad, gains = norm_backward(value, gain_row(gain), inverse, grad)
    input_grad[...] = (hidden_grad + dmid[...]).astype(BF16)
    width = gains.shape[1]
    blank = jnp.zeros((HD, width), F32)
    tail = jnp.zeros((LANE - HD - 2, width), F32)
    terms[...] = jnp.concatenate([blank, gains, gain_two[...], tail], axis=0).T
    count = nz * 4
    size, tall = width // count, expand.shape[0] // count
    for i in range(count):
        for j in range(FOUR):
            at = i * size + j * tall
            terms[at : at + tall, :HD] = expand[i * tall : (i + 1) * tall, j * HD : (j + 1) * HD]
    small[...] = by_core(terms[...], nz).astype(BF16)
    part, half = dq.shape[1] // FOUR, lat.shape[1] // FOUR
    for k in range(FOUR):
        place = sc[4] ^ k
        cols = pl.ds(pl.multiple_of(place * part, part), part)
        sends[k][:, :part] = dmid[:, cols].astype(BF16)
        sends[k][:, part : 2 * part] = dq[:, cols]
        cols = pl.ds(pl.multiple_of(place * half, half), half)
        end = 2 * part + half
        sends[k][:, 2 * part : end] = lat[:, cols].astype(BF16)
        for at in range(0, left.shape[0], LANE):
            sends[k][:, end + at : end + at + LANE] = left[at : at + LANE, :]


def leave(sc, hidden, dmid, gain, dq, base, latent, gain_two, we, wl, left, moved, nz, after=()):
    tok, width = hidden.shape
    lat = latent.shape[1]
    return call(
        functools.partial(leave_kernel, nz, len(moved)),
        "leave",
        (sc, hidden, dmid, gain, dq, base, latent, gain_two, we, wl, left, *moved),
        [SM] + [VM] * (10 + len(moved)),
        (shape((tok, width), BF16), shape((width, LANE), BF16))
        + (shape((tok, (2 * width + lat) // FOUR + width), BF16),) * FOUR,
        [pltpu.VMEM((tok, lat), F32), pltpu.VMEM((width, LANE), F32)],
        after,
        60,
    )


def shards(
    inputs, lengths, proj_query, proj_latent, proj_expand, proj_output,
    ffn_gate, ffn_up, ffn_down, norm_attn, norm_ffn, cotangent,
):
    tok, width = inputs.shape[1:]
    nz = lax.axis_size("z")
    z, x, core, batch = [lax.axis_index(a) for a in ("z", "x", "core", "batch")]
    place = x * 2 + batch
    hidden_size = ffn_gate.shape[1]
    first = ((z * 2 + x) * 2 + core) * tok
    sc = jnp.stack([first, z, x, core, place, place, place, place]).astype(jnp.int32)
    sc = jnp.concatenate([sc, lengths[0]])

    hidden = inputs[0]
    dy = cotangent[0]

    latent, kv, left, qp = enter(
        hidden, norm_attn, proj_latent, proj_expand, dy, proj_query, nz
    )
    early = lax.all_gather(left, PLANE, axis=0)
    relative = nz == 4
    if relative:
        moved = [kv]
        for k in range(1, nz):
            moved.append(lax.ppermute(kv, "z", [(i, i + k) for i in range(nz - k)]))
        k00 = stack(moved, after=(sc,))
    else:
        k00 = lax.all_gather(kv, "z", axis=0)
    k01 = swap(k00, "x")
    k10 = swap(k00, "core")
    k11 = swap(k01, "core")

    kvs, ot, logs, left_o, left_n2, mid, normed_two = attend(
        sc, (k00, k01, k10, k11), qp, hidden, proj_output, norm_ffn, nz, relative
    )
    n2s = lax.all_gather(left_n2, PLANE, axis=0)
    fed = feed(
        sc, normed_two, dy, mid, norm_ffn, proj_output, ffn_gate, ffn_up, ffn_down,
    )
    output, dmid, dop, gain_two = fed[FOUR:]
    parts_a = plane_swap(fed[:FOUR])

    quarter = hidden_size // FOUR
    last = []

    dq, keep_own, keep_far, send_own, send_far = attend_back(
        sc, kvs, qp, dop, ot, logs, nz, tok, after=(early,)
    )
    pieces = (keep_own, keep_far, swap(send_own, "core"), swap(send_far, "core"))
    if relative:
        moved = list(kv_cut(sc, pieces, nz - 1, after=parts_a[1:3]))
        for k in range(1, nz):
            moved[k] = lax.ppermute(moved[k], "z", [(i, i - k) for i in range(k, nz)])
        last.append(moved[0])
    else:
        both = [pieces[i].astype(F32) + pieces[i + 2].astype(F32) for i in range(2)]
        both = jnp.stack(both, axis=1)
        moved = [lax.psum_scatter(both, "z", scatter_dimension=0, tiled=False)]
    base = base_terms(dq, proj_query, after=last[-1:])
    rest, side = kv_sum(moved, after=(base,))
    last.append(rest)
    moved = [rest, swap(side, "x")]
    (main,) = weight_terms(
        sc,
        ((width, (n2s,), None), (width, (early,), 0)),
        parts_a,
        ((0, 0, 2 * quarter), (1, 2 * quarter, packed(hidden_size))),
        after=last[-1:],
    )
    last.append(main)
    main = lax.psum_scatter(main, ("z", "core"), scatter_dimension=0, tiled=True)
    left_out = leave(
        sc, hidden, dmid, norm_attn, dq, base, latent, gain_two, proj_expand, proj_latent,
        left_o, moved, nz, after=last[-1:],
    )
    input_grad, small = left_out[:2]
    last.append(input_grad)
    parts_c = plane_swap(left_out[2:])
    part, lat_part = width // FOUR, latent.shape[1] // FOUR
    end = 2 * part + lat_part
    keep, send = weight_terms(
        sc,
        ((width, (), None), (width, (early,), 1)),
        parts_c,
        ((0, 0, part), (1, part, end)),
        (small,),
        nz,
    )
    last.append(keep)
    came = swap(send, "core")
    step = 0
    while (1 << step) < nz:
        keep, send = halve(sc, keep, came, step, after=last[-1:])
        last.append(keep)
        came = lax.ppermute(send, "z", [(i, i ^ (1 << step)) for i in range(nz)])
        step += 1
    main = split_rows(sc, (main,), after=last[-1:])
    last.append(main[0])
    rest = split_rows(sc, (keep[0], came[0]), after=last[-1:])
    last.append(rest[0])
    grad_gate, grad_up, grad_down_t, token = put(
        sc,
        main,
        tuple((i * quarter, (i + 1) * quarter) for i in range(3)),
        (hidden_size,) * 3,
        after=last[-1:],
        token=True,
    )
    grad_output, grad_query, grad_latent, expand_t, gains = put(
        sc,
        rest,
        ((0, part), (part, 2 * part), (2 * part, end)),
        (width, width, latent.shape[1]),
        LAT,
        after=(token,),
    )
    grad_expand = expand_t.T
    grad_norm_attn, grad_norm_ffn = gains[0], gains[1]
    return (
        output[None],
        input_grad[None],
        grad_query,
        grad_latent,
        grad_expand,
        grad_output,
        grad_gate,
        grad_up,
        grad_down_t.T,
        grad_norm_attn,
        grad_norm_ffn,
    )


def solution(mesh):
    seq, batch = mesh.shape["seq"], mesh.shape["batch"]
    fine = Mesh(mesh.devices.reshape(seq // 4, 2, 2, batch), SEQ + ("batch",))
    return jax.shard_map(
        shards,
        mesh=fine,
        in_specs=(P("batch", SEQ, None), P("batch", None))
        + (P(),) * 9
        + (P("batch", SEQ, None),),
        out_specs=(
            P("batch", SEQ, None),
            P("batch", SEQ, None),
            P(SEQ, None),
            P(SEQ, None),
            P(None, SEQ),
            P(SEQ, None),
            P(SEQ, None),
            P(SEQ, None),
            P(None, SEQ),
            P(SEQ),
            P(SEQ),
        ),
        check_vma=False,
    )
```

```python
import functools

import jax
import jax.numpy as jnp
from jax import lax
from jax.experimental import pallas as pl
from jax.experimental.pallas import tpu as pltpu
from jax.sharding import Mesh
from jax.sharding import PartitionSpec as P

HEADS = 16
HD = 64
GROUPS = 2
PER = HEADS // GROUPS
LAT = 256
DOCS = 8
LANE = 128
CHUNK = 256

F32 = jnp.float32
BF16 = jnp.bfloat16
eps = 1e-05
scale = 0.125
masked = -1e30

SEQ = ("z", "x", "core")
PLANE = ("x", "batch")
FOUR = 4

VM = pl.BlockSpec(memory_space=pltpu.VMEM)
SM = pl.BlockSpec(memory_space=pltpu.SMEM)
ANY = pl.BlockSpec(memory_space=pl.ANY)
HB = pl.BlockSpec(memory_space=pltpu.HBM)
MIB = 1024 * 1024


def nn(left, right):
    return jnp.dot(left, right, preferred_element_type=F32)


def tn(left, right):
    return lax.dot_general(left, right, (((0,), (0,)), ((), ())), preferred_element_type=F32)


def nt(left, right):
    return lax.dot_general(left, right, (((1,), (1,)), ((), ())), preferred_element_type=F32)


def shape(dims, dtype):
    return jax.ShapeDtypeStruct(dims, dtype)


def cost(micros):
    return pl.CostEstimate(flops=0, bytes_accessed=int(micros * 3.6e6), transcendentals=0)


def call(kernel, name, ins, specs, outs, scratch=(), after=(), room=8, micros=0.01, token=False):
    count, extra = len(ins), len(after)

    if token:
        outs = (*outs, shape((8, LANE), F32))

    def body(*refs):
        refs = refs[:count] + refs[count + extra :]
        if token:
            at = count + len(outs) - 1
            refs[at][...] = jnp.zeros((8, LANE), F32)
            refs = refs[:at] + refs[at + 1 :]
        kernel(*refs)

    return pl.pallas_call(
        body,
        out_shape=tuple(outs),
        in_specs=list(specs) + [ANY] * extra,
        out_specs=(VM,) * len(outs),
        scratch_shapes=list(scratch),
        compiler_params=pltpu.CompilerParams(vmem_limit_bytes=room * MIB),
        cost_estimate=cost(micros),
        name=name,
    )(*ins, *after)


def gain_row(gain):
    return gain[...].astype(F32)[None]


def norm_forward(hidden, gain):
    inverse = lax.rsqrt(jnp.mean(hidden * hidden, axis=-1, keepdims=True) + eps)
    return (hidden * inverse * gain, inverse)


def norm_backward(hidden, gain, inverse, grad):
    scaled = grad * gain
    gain_grad = jnp.sum(grad * hidden * inverse, axis=0, keepdims=True)
    cubed = inverse * inverse * inverse
    hidden_grad = inverse * scaled - hidden * cubed * jnp.mean(
        scaled * hidden, axis=-1, keepdims=True
    )
    return (hidden_grad, gain_grad)


def by_core(value, nz):
    size = value.shape[0] // (nz * 4)
    rows = [value[i * size : (i + 1) * size] for i in range(nz * 4)]
    order = [i + j for i in range(0, nz * 4, 4) for j in (0, 2, 1, 3)]
    return jnp.concatenate([rows[i] for i in order], axis=0)


def doc_bounds(sc, tok):
    first = sc[0]
    query = first + lax.broadcasted_iota(jnp.int32, (1, tok), 1)
    begin = jnp.zeros((1, tok), jnp.int32)
    low = jnp.int32(0)
    end = jnp.int32(0)
    for d in range(DOCS):
        end = end + sc[8 + d]
        begin = jnp.where(query >= end, end, begin)
        low = jnp.where(first >= end, end, low)
    begin = jnp.where(query >= end, query, begin)
    low = jnp.where(first >= end, first, low)
    return query, begin, low // CHUNK, (first + tok - 1) // CHUNK + 1


def chunk_bias(chunk, query, begin):
    key = chunk * CHUNK + lax.broadcasted_iota(jnp.int32, (CHUNK, LANE), 0)
    bias = jnp.where((key >= begin) & (key <= query), 0.0, masked)
    return jnp.concatenate([bias] * PER, axis=1)


def attend_kernel(
    nz, relative, sc, k00, k01, k10, k11, qp, hidden, wo, gain,
    kvs, ot, logs, left_o, left_n, mid, normed, top, total, acc, mixed_all, wo_s, sem,
):
    load = pltpu.make_async_copy(wo, wo_s, sem)
    load.start()
    tok = hidden.shape[0]
    z, x, core = sc[1], sc[2], sc[3]
    for rc, rx, ref in ((0, 0, k00), (0, 1, k01), (1, 0, k10), (1, 1, k11)):
        for k in range(nz):
            where_z = z - k if relative else k
            slot = (where_z * 2 + (rx ^ x)) * 2 + (rc ^ core)

            @pl.when(where_z >= 0)
            def _():
                kvs[pl.ds(pl.multiple_of(slot * tok, tok), tok), :] = ref[k]

    query, begin, low, high = doc_bounds(sc, tok)
    top[...] = jnp.full(top.shape, masked, F32)
    total[...] = jnp.zeros(total.shape, F32)
    acc[...] = jnp.zeros(acc.shape, F32)

    @pl.loop(low, high)
    def _(chunk):
        kv = kvs[pl.ds(pl.multiple_of(chunk * CHUNK, CHUNK), CHUNK), :]
        bias = chunk_bias(chunk, query, begin)
        for g in range(GROUPS):
            part = kv[:, g * LANE : (g + 1) * LANE]
            raw = nn(part, qp[g]) + bias
            old = top[g]
            new = jnp.maximum(old, jnp.max(raw, axis=0, keepdims=True))
            prob = jnp.exp(raw - new)
            fade = jnp.exp(old - new)
            top[g] = new
            total[g] = total[g] * fade + jnp.sum(prob, axis=0, keepdims=True)
            acc[g] = acc[g] * fade + tn(part[:, HD:], prob.astype(BF16))

    for g in range(GROUPS):
        mixed = acc[g] * (1.0 / total[g])
        ot[g] = mixed
        logs[g] = top[g] + jnp.log(total[g])
        for h in range(PER):
            row = (g * PER + h) * HD
            mixed_all[row : row + HD, :] = mixed[:, h * LANE : (h + 1) * LANE]
    every = mixed_all[...]
    left_o[...] = by_core(every, nz).astype(BF16)
    load.wait()
    middle = hidden[...].astype(F32) + tn(every.astype(BF16), wo_s[...])
    mid[...] = middle
    value, unused = norm_forward(middle, gain_row(gain))
    normed[...] = value.astype(BF16)
    left_n[...] = by_core(value.T, nz).astype(BF16)


def attend(sc, kv_parts, qp, hidden, wo, gain, nz, relative, after=()):
    tok, width = hidden.shape
    left = shape((width, tok), BF16)
    return call(
        functools.partial(attend_kernel, nz, relative),
        "attend",
        (sc, *kv_parts, qp, hidden, wo, gain),
        [SM] + [VM] * 6 + [ANY, VM],
        (
            shape((nz * 4 * tok, 2 * LANE), BF16),
            shape((GROUPS, HD, PER * tok), F32),
            shape((GROUPS, 1, PER * tok), F32),
            left,
            left,
            shape((tok, width), F32),
            shape((tok, width), BF16),
        ),
        [
            pltpu.VMEM((GROUPS, 1, PER * tok), F32),
            pltpu.VMEM((GROUPS, 1, PER * tok), F32),
            pltpu.VMEM((GROUPS, HD, PER * tok), F32),
            pltpu.VMEM((HEADS * HD, tok), F32),
            pltpu.VMEM(wo.shape, BF16),
            pltpu.SemaphoreType.DMA,
        ],
        after,
        60,
    )


def packed(hidden):
    return -(-(3 * hidden // FOUR) // LANE) * LANE


def feed_kernel(tile, sc, normed, grad_out, mid, gain, wo, wg, wu, wd, *rest):
    sends = rest[:FOUR]
    output, dmid, dop, gain_grad = rest[FOUR : FOUR + 4]
    vg, vu, vd, vo, dgate_s, dup_s, act_s, sems = rest[FOUR + 4 :]
    steps = wd.shape[0] // tile
    copies = []
    for t in range(steps):
        span = pl.ds(t * tile, tile)
        copies.append(
            (
                pltpu.make_async_copy(wg.at[:, span], vg.at[:, span], sems.at[0, t]),
                pltpu.make_async_copy(wu.at[:, span], vu.at[:, span], sems.at[1, t]),
                pltpu.make_async_copy(wd.at[span, :], vd.at[span, :], sems.at[2, t]),
            )
        )
    copies.append((pltpu.make_async_copy(wo, vo, sems.at[3, 0]),))
    for group in copies:
        for copy in group:
            copy.start()
    n2 = normed[...]
    dy = grad_out[...]
    for t in range(steps):
        span = slice(t * tile, (t + 1) * tile)
        for copy in copies[t]:
            copy.wait()
        gate = nn(n2, vg[:, span])
        upper = nn(n2, vu[:, span])
        d_act = nt(dy, vd[span, :])
        sigma = jax.nn.sigmoid(gate)
        swish = gate * sigma
        act_s[:, span] = (swish * upper).astype(BF16)
        dgate_s[:, span] = (d_act * upper * sigma * (1.0 + gate * (1.0 - sigma))).astype(BF16)
        dup_s[:, span] = (d_act * swish).astype(BF16)
    copies[steps][0].wait()
    middle = mid[...]
    output[...] = (middle + nn(act_s[...], vd[...])).astype(BF16)
    back = nt(dgate_s[...], vg[...]) + nt(dup_s[...], vu[...])
    inverse = lax.rsqrt(jnp.mean(middle * middle, axis=-1, keepdims=True) + eps)
    grad, gains = norm_backward(middle, gain_row(gain), inverse, back)
    grad = grad + dy.astype(F32)
    dmid[...] = grad
    gain_grad[...] = gains
    part = wg.shape[1] // FOUR
    for k in range(FOUR):
        place = sc[4] ^ k
        cols = pl.ds(pl.multiple_of((place // 2) * 2 * part, LANE), 2 * part)
        pieces = []
        for ref in (dgate_s, dup_s, act_s):
            both = ref[:, cols].astype(F32)
            pieces.append(jnp.where(place % 2 == 0, both[:, :part], both[:, part:]))
        pieces.append(jnp.zeros((both.shape[0], sends[k].shape[1] - 3 * part), F32))
        sends[k][...] = jnp.concatenate(pieces, axis=1).astype(BF16)
    turned = nt(vo[...], grad.astype(BF16)).astype(BF16)
    dop[:, 0:HD, :] = jnp.zeros((GROUPS, HD, dop.shape[2]), BF16)
    for g in range(GROUPS):
        for h in range(PER):
            row = (g * PER + h) * HD
            dop[g, HD:, h * LANE : (h + 1) * LANE] = turned[row : row + HD, :]


def feed(sc, normed, grad_out, mid, gain, wo, wg, wu, wd, after=()):
    tok, width = normed.shape
    hidden = wg.shape[1]
    tile = 2 * LANE
    wide = packed(hidden)
    return call(
        functools.partial(feed_kernel, tile),
        "feed",
        (sc, normed, grad_out, mid, gain, wo, wg, wu, wd),
        [SM] + [VM] * 4 + [ANY] * 4,
        (shape((tok, wide), BF16),) * FOUR
        + (
            shape((tok, width), BF16),
            shape((tok, width), F32),
            shape((GROUPS, 2 * HD, PER * tok), BF16),
            shape((1, width), F32),
        ),
        [
            pltpu.VMEM((width, hidden), BF16),
            pltpu.VMEM((width, hidden), BF16),
            pltpu.VMEM((hidden, width), BF16),
            pltpu.VMEM((width, width), BF16),
            pltpu.VMEM((tok, hidden), BF16),
            pltpu.VMEM((tok, hidden), BF16),
            pltpu.VMEM((tok, hidden), BF16),
            pltpu.SemaphoreType.DMA((4, hidden // tile)),
        ],
        after,
        60,
    )


def back_kernel(
    nz, sc, kvs, qp, dop, ot, logs, dq, keep_own, keep_far, send_own, send_far, acc, rows, block
):
    tok = dq.shape[0]
    x, core = sc[2], sc[3]

    @pl.loop(0, nz)
    def _(i):
        for ref in (keep_own, keep_far, send_own, send_far):
            ref[i] = jnp.zeros(ref.shape[1:], BF16)

    query, begin, low, high = doc_bounds(sc, tok)
    acc[...] = jnp.zeros(acc.shape, F32)
    for g in range(GROUPS):
        rows[g] = jnp.sum(dop[g, HD:, :].astype(F32) * ot[g], axis=0, keepdims=True)

    @pl.loop(low, high)
    def _(chunk):
        kv = kvs[pl.ds(pl.multiple_of(chunk * CHUNK, CHUNK), CHUNK), :]
        bias = chunk_bias(chunk, query, begin)
        for g in range(GROUPS):
            part = kv[:, g * LANE : (g + 1) * LANE]
            prob = jnp.exp(nn(part, qp[g]) + bias - logs[g])
            slope = (prob * (nn(part, dop[g]) - rows[g])).astype(BF16)
            block[:, g * LANE : (g + 1) * LANE] = nt(slope, qp[g]) + nt(prob.astype(BF16), dop[g])
            acc[g] += tn(part, slope)
        where_z = chunk // 2
        near = (chunk % 2) == x
        mine = block[pl.ds(pl.multiple_of(core * tok, tok), tok), :].astype(BF16)
        other = block[pl.ds(pl.multiple_of((1 - core) * tok, tok), tok), :].astype(BF16)

        @pl.when(near)
        def _():
            keep_own[where_z] = mine
            send_own[where_z] = other

        @pl.when(jnp.logical_not(near))
        def _():
            keep_far[where_z] = mine
            send_far[where_z] = other

    for g in range(GROUPS):
        for h in range(0, PER, 2):
            pair = [acc[g, 0:HD, (h + i) * LANE : (h + i + 1) * LANE] for i in range(2)]
            col = (g * PER + h) * HD
            dq[:, col : col + LANE] = (jnp.concatenate(pair, axis=0).T * scale).astype(BF16)


def attend_back(sc, kvs, qp, dop, ot, logs, nz, tok, after=()):
    part = shape((nz, tok, 2 * LANE), BF16)
    return call(
        functools.partial(back_kernel, nz),
        "attend_back",
        (sc, kvs, qp, dop, ot, logs),
        [SM] + [VM] * 5,
        (shape((tok, HEADS * HD), BF16), part, part, part, part),
        [
            pltpu.VMEM((GROUPS, 2 * HD, PER * tok), F32),
            pltpu.VMEM((GROUPS, 1, PER * tok), F32),
            pltpu.VMEM((CHUNK, 2 * LANE), F32),
        ],
        after,
        60,
        9,
    )


def stack_kernel(*refs):
    for k, ref in enumerate(refs[:-1]):
        refs[-1][k] = ref[...]


def stack(arrays, after=()):
    dims = (len(arrays),) + arrays[0].shape
    return call(
        stack_kernel, "stack", arrays, [VM] * len(arrays), (shape(dims, BF16),), after=after
    )[0]


def kv_cut_kernel(sc, *refs):
    given, rest = refs[:4], refs[4:]
    own, sends, held, sems = rest[0], rest[1:-2], rest[-2], rest[-1]
    copies = [pltpu.make_async_copy(given[i], held.at[i], sems.at[i]) for i in range(4)]
    for copy in copies:
        copy.start()
    for copy in copies:
        copy.wait()
    z = sc[1]
    for i in range(2):
        own[i] = held[i, z].astype(F32) + held[i + 2, z].astype(F32)
        for k, ref in enumerate(sends):
            at = jnp.maximum(z - k - 1, 0)
            ref[i] = (held[i, at].astype(F32) + held[i + 2, at].astype(F32)).astype(BF16)


def kv_cut(sc, terms, count, after=()):
    dims = (2,) + terms[0].shape[1:]
    return call(
        kv_cut_kernel, "kv_cut", (sc, *terms), [SM] + [HB] * 4,
        (shape(dims, F32),) + (shape(dims, BF16),) * count,
        [pltpu.VMEM((4,) + terms[0].shape, BF16), pltpu.SemaphoreType.DMA((4,))],
        after=after, room=6,
    )


def base_kernel(dq, wq, base):
    base[...] = nt(dq[...], wq[...])


def base_terms(dq, wq, after=()):
    return call(
        base_kernel, "base", (dq, wq), [VM] * 2, (shape((dq.shape[0], wq.shape[0]), F32),),
        after=after, room=6,
    )[0]


def kv_sum_kernel(*refs):
    moved, (rest, side) = refs[:-2], refs[-2:]
    total = moved[0][...].astype(F32)
    for ref in moved[1:]:
        total = total + ref[...].astype(F32)
    rest[...] = total[0]
    side[...] = total[1].astype(BF16)


def kv_sum(moved, after=()):
    dims = moved[0].shape[1:]
    return call(
        kv_sum_kernel, "kv_sum", moved, [VM] * len(moved), (shape(dims, F32), shape(dims, BF16)),
        after=after,
    )


def weight_kernel(counts, plan, extra, split, sc, *refs):
    lefts = []
    for count, unused in counts:
        lefts.append(refs[:count])
        refs = refs[count:]
    rights, refs = refs[:FOUR], refs[FOUR:]
    added, refs = refs[:extra], refs[extra:]
    outs, (wide, tall, made, sems) = refs[:-4], refs[-4:]
    tok = rights[0].shape[-2]
    copies = []
    for k in range(FOUR):
        span = pl.ds(k * tok, tok)
        count = tall.shape[1]
        pairs = [(rights[k].at[:, 0:count], tall.at[span, :])]
        for at in range(count, rights[k].shape[1], LANE):
            which, row = divmod(at - count, wide.shape[1])
            pairs.append((rights[k].at[:, at : at + LANE], wide.at[which, row : row + LANE, span]))
        for t, (source, target) in enumerate(pairs):
            copies.append(pltpu.make_async_copy(source, target, sems.at[len(counts) + t, k]))
        for i, (count, kind) in enumerate(counts):
            if count == 0:
                continue
            source = lefts[i][0].at[sc[4] ^ k]
            if kind is not None:
                source = lefts[i][0].at[sc[4] ^ k, kind]
            copies.append(pltpu.make_async_copy(source, wide.at[i, :, span], sems.at[i, k]))
    for copy in copies:
        copy.start()
    for copy in copies:
        copy.wait()
    ref = outs[0] if not split else made
    for index, begin, stop in plan:
        for at in range(begin, stop, CHUNK):
            cols = slice(at, min(at + CHUNK, stop))
            ref[:, cols] = nn(wide[index], tall[:, cols]).astype(BF16)
    for other in added:
        ref[:, plan[-1][2] :] = other[...]
    if split:
        keep, send = outs
        nz, size, unused = keep.shape

        @pl.loop(0, nz)
        def _(i):
            for out, where in ((send, 1 - sc[3]), (keep, sc[3])):
                rows = pl.ds(pl.multiple_of((2 * i + where) * size, size), size)
                out[i] = made[rows, :]


def weight_terms(sc, lefts, rights, plan, extra=(), nz=None, after=()):
    tok = rights[0].shape[-2]
    width = plan[-1][2]
    rows = lefts[0][0]
    moves = 1 + (rights[0].shape[1] - width) // LANE
    wide = width + sum(array.shape[1] for array in extra)
    counts = tuple((len(arrays), kind) for unused, arrays, kind in lefts)
    flat = [array for unused, arrays, kind in lefts for array in arrays] + rights
    if nz:
        outs = (shape((nz, rows // (2 * nz), wide), BF16),) * 2
    else:
        outs = (shape((rows, wide), BF16),)
    return call(
        functools.partial(weight_kernel, counts, plan, len(extra), bool(nz)),
        "weight_terms",
        (sc, *flat, *extra),
        [SM] + [ANY] * len(flat) + [VM] * len(extra),
        outs,
        [
            pltpu.VMEM((len(lefts), rows, FOUR * tok), BF16),
            pltpu.VMEM((FOUR * tok, width), BF16),
            pltpu.VMEM((rows, wide) if nz else (16, LANE), BF16),
            pltpu.SemaphoreType.DMA((len(lefts) + moves, FOUR)),
        ],
        after,
        60,
    )


def halve_kernel(step, sc, kept, came, keep, send):
    bit = (sc[1] >> step) & 1

    @pl.loop(0, keep.shape[0])
    def _(i):
        for ref, half in ((send, 1 - bit), (keep, bit)):
            total = kept[2 * i + half].astype(F32) + came[2 * i + half].astype(F32)
            ref[i] = total.astype(BF16)


def halve(sc, kept, came, step, after=()):
    half = shape((kept.shape[0] // 2,) + kept.shape[1:], BF16)
    return call(
        functools.partial(halve_kernel, step),
        "halve", (sc, kept, came), [SM, VM, VM], (half, half), after=after,
    )


def split_kernel(sc, *refs):
    ins, (mine, other, total) = refs[:-3], refs[-3:]
    rows = mine.shape[0]
    value = (ins[0][sc[1]] if len(ins[0].shape) == 3 else ins[0][...]).astype(F32)
    for ref in ins[1:]:
        value = value + ref[...].astype(F32)
    total[...] = value
    x = sc[2]
    for ref, at in ((mine, x), (other, 1 - x)):
        ref[...] = total[pl.ds(pl.multiple_of(at * rows, rows), rows), :].astype(BF16)


def split_rows(sc, terms, after=()):
    rows, width = terms[0].shape[-2:]
    mine, other = call(
        split_kernel, "split_rows", (sc, *terms), [SM] + [VM] * len(terms),
        (shape((rows // 2, width), BF16),) * 2,
        [pltpu.VMEM((rows, width), F32)], after=after, room=16,
    )
    return plane_swap([mine, mine, other, other])


def swap(value, axis):
    return lax.ppermute(value, axis, [(0, 1), (1, 0)])


def plane_swap(parts):
    moved = [parts[0]]
    for k in range(1, FOUR):
        moved.append(lax.ppermute(parts[k], PLANE, [(d, d ^ k) for d in range(FOUR)]))
    return moved


def place_kernel(plan, count, sc, *refs):
    results = refs[count : count + len(plan)]
    small = refs[count + len(plan) :]
    for k in range(0, FOUR, 2):
        place = sc[4] ^ k
        even = place % 2 == 0
        for (begin, stop), result in zip(plan, results):
            size = stop - begin
            near = refs[k][:, begin:stop].astype(F32)
            next_one = refs[k + 1][:, begin:stop].astype(F32)
            pair = [jnp.where(even, near, next_one), jnp.where(even, next_one, near)]
            cols = pl.ds(pl.multiple_of((place // 2) * 2 * size, LANE), 2 * size)
            result[:, cols] = jnp.concatenate(pair, axis=1)
    if small:
        expand, gains = small
        begin = plan[-1][1]
        total = [refs[k][:, begin:].astype(F32) for k in range(FOUR)]
        even = [jnp.where(sc[4] % 2 == 0, total[i], total[i + 1]) for i in (0, 2)]
        odd = [jnp.where(sc[4] % 2 == 0, total[i + 1], total[i]) for i in (0, 2)]
        value = (even[0] + odd[0]) + (even[1] + odd[1])
        size = expand.shape[0]
        for j in range(FOUR):
            expand[:, j * HD : (j + 1) * HD] = value[j * size : (j + 1) * size, :HD]
        gains[...] = value.T[HD : HD + 8, :]


def put(sc, parts, plan, widths, small=0, after=(), token=False):
    rows = parts[0].shape[0]
    outs = tuple(shape((rows, width), F32) for width in widths)
    if small:
        outs += (shape((rows // FOUR, small), F32), shape((8, rows), F32))
    return call(
        functools.partial(place_kernel, plan, len(parts)), "put", (sc, *parts),
        [SM] + [VM] * len(parts), outs, after=after, token=token,
    )


def enter_kernel(nz, hidden, gain, wl, we, dy, wq, latent, kv, left, qp, wq_s, sem):
    load = pltpu.make_async_copy(wq, wq_s, sem)
    load.start()
    value, unused = norm_forward(hidden[...].astype(F32), gain_row(gain))
    low = value.astype(BF16)
    rows = nn(low, wl[...]).astype(BF16)
    latent[...] = rows
    for g in range(GROUPS):
        span = slice(g * LANE, (g + 1) * LANE)
        kv[:, span] = nn(rows[:, g * LAT : (g + 1) * LAT], we[:, span]).astype(BF16)
    left[0] = by_core(dy[...].astype(F32).T, nz).astype(BF16)
    left[1] = by_core(value.T, nz).astype(BF16)
    load.wait()
    turned = (nn(low, wq_s[...]).astype(BF16) * scale).T
    qp[:, HD:, :] = jnp.zeros((GROUPS, HD, qp.shape[2]), BF16)
    for g in range(GROUPS):
        for h in range(PER):
            at = (g * PER + h) * HD
            qp[g, 0:HD, h * LANE : (h + 1) * LANE] = turned[at : at + HD, :]


def enter(hidden, gain, wl, we, dy, wq, nz):
    tok, width = hidden.shape
    return call(
        functools.partial(enter_kernel, nz),
        "enter",
        (hidden, gain, wl, we, dy, wq),
        [VM] * 5 + [HB],
        (
            shape((tok, wl.shape[1]), BF16),
            shape((tok, we.shape[1]), BF16),
            shape((2, width, tok), BF16),
            shape((GROUPS, 2 * HD, PER * tok), BF16),
        ),
        [pltpu.VMEM(wq.shape, BF16), pltpu.SemaphoreType.DMA],
        room=60,
    )


def leave_kernel(
    nz, count, sc, hidden, dmid, gain, dq, base, latent, gain_two, we, wl, left, *refs
):
    moved = refs[:count]
    input_grad, small = refs[count : count + 2]
    sends = refs[count + 2 : count + 2 + FOUR]
    lat, terms = refs[count + 2 + FOUR :]
    total = moved[0][...].astype(F32)
    for ref in moved[1:]:
        total = total + ref[...].astype(F32)
    kv_grad = total.astype(BF16)
    rows = latent[...]
    expand = []
    for g in range(GROUPS):
        span = slice(g * LANE, (g + 1) * LANE)
        wide = slice(g * LAT, (g + 1) * LAT)
        lat[:, wide] = nt(kv_grad[:, span], we[:, span])
        expand.append(tn(kv_grad[:, span], rows[:, wide]))
    expand = jnp.concatenate(expand, axis=0)
    grad = base[...] + nt(lat[...].astype(BF16), wl[...])
    value = hidden[...].astype(F32)
    inverse = lax.rsqrt(jnp.mean(value * value, axis=-1, keepdims=True) + eps)
    hidden_grad, gains = norm_backward(value, gain_row(gain), inverse, grad)
    input_grad[...] = (hidden_grad + dmid[...]).astype(BF16)
    width = gains.shape[1]
    blank = jnp.zeros((HD, width), F32)
    tail = jnp.zeros((LANE - HD - 2, width), F32)
    terms[...] = jnp.concatenate([blank, gains, gain_two[...], tail], axis=0).T
    count = nz * 4
    size, tall = width // count, expand.shape[0] // count
    for i in range(count):
        for j in range(FOUR):
            at = i * size + j * tall
            terms[at : at + tall, :HD] = expand[i * tall : (i + 1) * tall, j * HD : (j + 1) * HD]
    small[...] = by_core(terms[...], nz).astype(BF16)
    part, half = dq.shape[1] // FOUR, lat.shape[1] // FOUR
    for k in range(FOUR):
        place = sc[4] ^ k
        cols = pl.ds(pl.multiple_of(place * part, part), part)
        sends[k][:, :part] = dmid[:, cols].astype(BF16)
        sends[k][:, part : 2 * part] = dq[:, cols]
        cols = pl.ds(pl.multiple_of(place * half, half), half)
        end = 2 * part + half
        sends[k][:, 2 * part : end] = lat[:, cols].astype(BF16)
        for at in range(0, left.shape[0], LANE):
            sends[k][:, end + at : end + at + LANE] = left[at : at + LANE, :]


def leave(sc, hidden, dmid, gain, dq, base, latent, gain_two, we, wl, left, moved, nz, after=()):
    tok, width = hidden.shape
    lat = latent.shape[1]
    return call(
        functools.partial(leave_kernel, nz, len(moved)),
        "leave",
        (sc, hidden, dmid, gain, dq, base, latent, gain_two, we, wl, left, *moved),
        [SM] + [VM] * (10 + len(moved)),
        (shape((tok, width), BF16), shape((width, LANE), BF16))
        + (shape((tok, (2 * width + lat) // FOUR + width), BF16),) * FOUR,
        [pltpu.VMEM((tok, lat), F32), pltpu.VMEM((width, LANE), F32)],
        after,
        60,
    )


def shards(
    inputs, lengths, proj_query, proj_latent, proj_expand, proj_output,
    ffn_gate, ffn_up, ffn_down, norm_attn, norm_ffn, cotangent,
):
    tok, width = inputs.shape[1:]
    nz = lax.axis_size("z")
    z, x, core, batch = [lax.axis_index(a) for a in ("z", "x", "core", "batch")]
    place = x * 2 + batch
    hidden_size = ffn_gate.shape[1]
    first = ((z * 2 + x) * 2 + core) * tok
    sc = jnp.stack([first, z, x, core, place, place, place, place]).astype(jnp.int32)
    sc = jnp.concatenate([sc, lengths[0]])

    hidden = inputs[0]
    dy = cotangent[0]

    latent, kv, left, qp = enter(
        hidden, norm_attn, proj_latent, proj_expand, dy, proj_query, nz
    )
    early = lax.all_gather(left, PLANE, axis=0)
    relative = nz == 4
    if relative:
        moved = [kv]
        for k in range(1, nz):
            moved.append(lax.ppermute(kv, "z", [(i, i + k) for i in range(nz - k)]))
        k00 = stack(moved, after=(sc,))
    else:
        k00 = lax.all_gather(kv, "z", axis=0)
    k01 = swap(k00, "x")
    k10 = swap(k00, "core")
    k11 = swap(k01, "core")

    kvs, ot, logs, left_o, left_n2, mid, normed_two = attend(
        sc, (k00, k01, k10, k11), qp, hidden, proj_output, norm_ffn, nz, relative
    )
    n2s = lax.all_gather(left_n2, PLANE, axis=0)
    fed = feed(
        sc, normed_two, dy, mid, norm_ffn, proj_output, ffn_gate, ffn_up, ffn_down,
    )
    output, dmid, dop, gain_two = fed[FOUR:]
    parts_a = plane_swap(fed[:FOUR])

    quarter = hidden_size // FOUR
    last = []

    dq, keep_own, keep_far, send_own, send_far = attend_back(
        sc, kvs, qp, dop, ot, logs, nz, tok, after=(early,)
    )
    pieces = (keep_own, keep_far, swap(send_own, "core"), swap(send_far, "core"))
    if relative:
        moved = list(kv_cut(sc, pieces, nz - 1, after=parts_a[1:2]))
        for k in range(1, nz):
            moved[k] = lax.ppermute(moved[k], "z", [(i, i - k) for i in range(k, nz)])
        last.append(moved[0])
    else:
        both = [pieces[i].astype(F32) + pieces[i + 2].astype(F32) for i in range(2)]
        both = jnp.stack(both, axis=1)
        moved = [lax.psum_scatter(both, "z", scatter_dimension=0, tiled=False)]
    base = base_terms(dq, proj_query, after=last[-1:])
    rest, side = kv_sum(moved, after=(base,))
    last.append(rest)
    moved = [rest, swap(side, "x")]
    (main,) = weight_terms(
        sc,
        ((width, (n2s,), None), (width, (early,), 0)),
        parts_a,
        ((0, 0, 2 * quarter), (1, 2 * quarter, packed(hidden_size))),
        after=last[-1:],
    )
    last.append(main)
    main = lax.psum_scatter(main, ("z", "core"), scatter_dimension=0, tiled=True)
    left_out = leave(
        sc, hidden, dmid, norm_attn, dq, base, latent, gain_two, proj_expand, proj_latent,
        left_o, moved, nz, after=last[-1:],
    )
    input_grad, small = left_out[:2]
    last.append(input_grad)
    parts_c = plane_swap(left_out[2:])
    part, lat_part = width // FOUR, latent.shape[1] // FOUR
    end = 2 * part + lat_part
    keep, send = weight_terms(
        sc,
        ((width, (), None), (width, (early,), 1)),
        parts_c,
        ((0, 0, part), (1, part, end)),
        (small,),
        nz,
    )
    last.append(keep)
    came = swap(send, "core")
    step = 0
    while (1 << step) < nz:
        keep, send = halve(sc, keep, came, step, after=last[-1:])
        last.append(keep)
        came = lax.ppermute(send, "z", [(i, i ^ (1 << step)) for i in range(nz)])
        step += 1
    main = split_rows(sc, (main,), after=last[-1:])
    last.append(main[0])
    rest = split_rows(sc, (keep[0], came[0]), after=last[-1:])
    last.append(rest[0])
    grad_gate, grad_up, grad_down_t, token = put(
        sc,
        main,
        tuple((i * quarter, (i + 1) * quarter) for i in range(3)),
        (hidden_size,) * 3,
        after=last[-1:],
        token=True,
    )
    grad_output, grad_query, grad_latent, expand_t, gains = put(
        sc,
        rest,
        ((0, part), (part, 2 * part), (2 * part, end)),
        (width, width, latent.shape[1]),
        LAT,
        after=(token,),
    )
    grad_expand = expand_t.T
    grad_norm_attn, grad_norm_ffn = gains[0], gains[1]
    return (
        output[None],
        input_grad[None],
        grad_query,
        grad_latent,
        grad_expand,
        grad_output,
        grad_gate,
        grad_up,
        grad_down_t.T,
        grad_norm_attn,
        grad_norm_ffn,
    )


def solution(mesh):
    seq, batch = mesh.shape["seq"], mesh.shape["batch"]
    fine = Mesh(mesh.devices.reshape(seq // 4, 2, 2, batch), SEQ + ("batch",))
    return jax.shard_map(
        shards,
        mesh=fine,
        in_specs=(P("batch", SEQ, None), P("batch", None))
        + (P(),) * 9
        + (P("batch", SEQ, None),),
        out_specs=(
            P("batch", SEQ, None),
            P("batch", SEQ, None),
            P(SEQ, None),
            P(SEQ, None),
            P(None, SEQ),
            P(SEQ, None),
            P(SEQ, None),
            P(SEQ, None),
            P(None, SEQ),
            P(SEQ),
            P(SEQ),
        ),
        check_vma=False,
    )
```
